32 devices in a mesh: freq: 4 (over y, core), slab: 8 (over z, x).
Axes of the slice: x: 2, y: 2, z: 4, core: 2. Of those that a mesh axis runs over, the one named last changes fastest.
Arguments:
- inverse_permittivity: float32 [64, 24, 512], P('slab'), may hold values from 0.083 to 1
- forward_fields: float32 [4, 6, 64, 24, 512], P('freq', None, 'slab'), may hold values from -6 to 6
- adjoint_fields: float32 [4, 6, 64, 24, 512], P('freq', None, 'slab'), may hold values from -6 to 6
- source_wave: float32 [4, 3], P('freq'), may hold values from -4 to 4
- source_profile: float32 [4, 512], P('freq'), may hold values from -4 to 4
- adjoint_wave: float32 [4, 3], P('freq'), may hold values from -4 to 4
- adjoint_profile: float32 [4, 512], P('freq'), may hold values from -4 to 4
- source_plane: int32 [4], P('freq'), may hold values from 0 to 23
- monitor_plane: int32 [4], P('freq'), may hold values from 0 to 23
- radius_map: int32 [8, 8], P('slab'), may hold values from 1 to 4
- design_mask: int32 [8, 8], P('slab'), may hold values 0 or 1
- design_density: float32 [512, 64], P('slab'), may hold values from 0 to 1
Outputs:
- forward_out: float32 [4, 6, 64, 24, 512], P('freq', None, 'slab')
- adjoint_out: float32 [4, 6, 64, 24, 512], P('freq', None, 'slab')
- projected: float32 [512, 64], P('slab')
The draws below stay inside these ranges and needn't reach their ends.
Inputs may be any that keep to these rules, and one draw needn't show every extreme that they name: `radius_map`: filter radius of a tile in cells.
All inputs are finite; a program needn't handle non-finite values. No bound on the sum of `design_mask` on one device may be relied on, other than what follows from the above.
Results may differ from the reference program's by a relative error of at most 0.0003.
Values sent between devices are 32-bit elements; how exact they have to be, the bound alone decides.
No kernel may reach another device: no remote copies, remote signals or barrier semaphores. Data moves between devices by JAX's collectives and lax.ppermute only.
A program may use at most 64 MiB of HBM per device.

```python
import math
import jax
import jax.numpy as jnp
from jax import lax

NY = 512
NZ = 24
FREQS = 4
STEPS = 3
RMAX = 4
XTILES = 8
NX = 64
YTILES = 8
TILE_Y = 64
TILE_X = 8


def with_ends(drawn, key, smallest, top_value):
    dims = drawn.shape
    place = [jax.random.randint(jax.random.fold_in(key, axis), (), 0, dims[axis]) for axis in range(len(dims))]
    drawn = drawn.at[tuple(place)].set(smallest)
    longest = dims.index(max(dims))
    place[longest] = (place[longest] + 1) % dims[longest]
    return drawn.at[tuple(place)].set(top_value)


def steps_of(key, shape, shards, least, top_value):
    gain, own = 1.0, jax.random.fold_in(key, 6)
    for axis_at, shards_of in shards:
        heights = jnp.exp(jax.random.uniform(jax.random.fold_in(own, axis_at), (shards_of,), jnp.float32, least / len(shards), top_value / len(shards)))
        gain = gain * jnp.repeat(heights, shape[axis_at] // shards_of).reshape([-1 if axis == axis_at else 1 for axis in range(len(shape))])
    return gain


def bell_draw(key, shape, spread, bound, pieces=(), kind=jnp.bfloat16):
    array = jax.random.normal(key, shape, jnp.float32) * spread
    if len(pieces) > 0:
        array = steps_of(key, shape, pieces, -0.22, 0.18) * array
    return jnp.clip(array, min=-bound, max=bound).astype(kind)


def setup_inputs(seed: int = 0) -> dict:
    keys = jax.random.split(jax.random.key(seed), 13)
    inverse_permittivity = jnp.clip(jnp.exp(math.log(1.0) - 2.4889147 * jax.random.uniform(keys[0], (NX, NZ, NY), jnp.float32) ** steps_of(keys[0], (NX, NZ, NY), ((0, 8),), -0.2, 0.2)), 0.083, 1.0)
    forward_fields = bell_draw(keys[1], (FREQS, 6, NX, NZ, NY), 1.0, 6.0, ((0, 4), (2, 8)), jnp.float32)
    adjoint_fields = bell_draw(keys[2], (FREQS, 6, NX, NZ, NY), 1.0, 6.0, ((0, 4), (2, 8)), jnp.float32)
    source_wave = bell_draw(keys[3], (FREQS, STEPS), 1.0, 4.0, ((0, 4),), jnp.float32)
    source_profile = bell_draw(keys[4], (FREQS, NY), 1.0, 4.0, ((0, 4),), jnp.float32)
    adjoint_wave = bell_draw(keys[5], (FREQS, STEPS), 1.0, 4.0, ((0, 4),), jnp.float32)
    adjoint_profile = bell_draw(keys[6], (FREQS, NY), 1.0, 4.0, ((0, 4),), jnp.float32)
    source_plane = with_ends(jax.random.randint(keys[7], (FREQS,), 0, NZ), jax.random.fold_in(keys[7], 1), 0, NZ - 1).astype(jnp.int32)
    monitor_plane = with_ends(jax.random.randint(keys[8], (FREQS,), 0, NZ), jax.random.fold_in(keys[8], 1), 0, NZ - 1).astype(jnp.int32)
    radius_map = with_ends(jax.random.randint(keys[9], (YTILES, XTILES), 1, RMAX + 1), jax.random.fold_in(keys[9], 1), 1, RMAX).astype(jnp.int32)
    design_mask = with_ends((jax.random.randint(keys[10], (YTILES, XTILES), 0, 4) < 3).astype(jnp.int32), jax.random.fold_in(keys[10], 1), 0, 1)
    design_density = jnp.clip(1.0 * jax.random.uniform(keys[11], (NY, NX), jnp.float32) ** steps_of(keys[11], (NY, NX), ((0, 8),), -0.2, 0.2), 0.0, 1.0)
    return dict(inverse_permittivity=inverse_permittivity, forward_fields=forward_fields, adjoint_fields=adjoint_fields, source_wave=source_wave, source_profile=source_profile, adjoint_wave=adjoint_wave, adjoint_profile=adjoint_profile, source_plane=source_plane, monitor_plane=monitor_plane, radius_map=radius_map, design_mask=design_mask, design_density=design_density)


courant = 0.5
sharpness = 4.0
midpoint = 0.5
step_size = 0.3

def forward_cell(field, axis):
    axis = field.ndim + axis
    size = field.shape[axis]
    inner = lax.slice_in_dim(field, 1, size, axis=axis)
    edge = jnp.zeros_like(lax.slice_in_dim(field, 0, 1, axis=axis))
    return jnp.concatenate([inner, edge], axis=axis)

def backward_cell(field, axis):
    axis = field.ndim + axis
    size = field.shape[axis]
    inner = lax.slice_in_dim(field, 0, size - 1, axis=axis)
    edge = jnp.zeros_like(lax.slice_in_dim(field, 0, 1, axis=axis))
    return jnp.concatenate([edge, inner], axis=axis)

def yee_update(fields, inverse, source):
    elec_x, elec_y, elec_z, magn_x, magn_y, magn_z = fields
    magn_x = magn_x - courant * (forward_cell(elec_z, -1) - elec_z - (forward_cell(elec_y, -2) - elec_y))
    magn_y = magn_y - courant * (forward_cell(elec_x, -2) - elec_x - (forward_cell(elec_z, -3) - elec_z))
    magn_z = magn_z - courant * (forward_cell(elec_y, -3) - elec_y - (forward_cell(elec_x, -1) - elec_x))
    elec_x = elec_x + courant * inverse * (magn_z - backward_cell(magn_z, -1) - (magn_y - backward_cell(magn_y, -2))) + source
    elec_y = elec_y + courant * inverse * (magn_x - backward_cell(magn_x, -2) - (magn_z - backward_cell(magn_z, -3)))
    elec_z = elec_z + courant * inverse * (magn_y - backward_cell(magn_y, -3) - (magn_x - backward_cell(magn_x, -1)))
    return (elec_x, elec_y, elec_z, magn_x, magn_y, magn_z)

def reference(inverse_permittivity, forward_fields, adjoint_fields, source_wave, source_profile, adjoint_wave, adjoint_profile, source_plane, monitor_plane, radius_map, design_mask, design_density):
    waves = jnp.stack([source_wave, adjoint_wave], axis=1)
    profiles = jnp.stack([source_profile, adjoint_profile], axis=1)
    planes = jnp.stack([source_plane, monitor_plane], axis=1)

    def run_group(inputs):
        forward, adjoint, wave, profile, plane = inputs
        fields = tuple((jnp.stack([forward[component], adjoint[component]]) for component in range(6)))
        plane_hit = (jnp.arange(NZ, dtype=jnp.int32)[None, :] == plane[:, None]).astype(jnp.float32)
        intersection = jnp.zeros((NX, NY), jnp.float32)
        for turn in range(STEPS):
            source = wave[:, turn][:, None, None, None] * plane_hit[:, None, :, None] * profile[:, None, None, :]
            fields = yee_update(fields, inverse_permittivity, source)
            total = 0.0
            for component in range(3):
                total = total + fields[component][0] * fields[component][1]
            intersection = intersection + lax.optimization_barrier(jnp.sum(total, axis=1))
        return (jnp.stack([member[0] for member in fields]), jnp.stack([member[1] for member in fields]), intersection)
    forward_out, adjoint_out, intersections = lax.map(run_group, (forward_fields, adjoint_fields, waves, profiles, planes))
    gradient = lax.optimization_barrier(jnp.sum(intersections, axis=0))
    radius = jnp.repeat(jnp.repeat(radius_map, TILE_Y, axis=0), TILE_X, axis=1).astype(jnp.float32)
    chosen = jnp.repeat(jnp.repeat(design_mask, TILE_Y, axis=0), TILE_X, axis=1).astype(jnp.float32)
    scale = step_size / math.sqrt(3 * STEPS * NZ * FREQS)
    updated = design_density + scale * chosen * gradient.T
    padded = jnp.pad(updated, RMAX)
    inside = jnp.pad(jnp.ones((NY, NX), jnp.float32), RMAX)
    numerator = jnp.zeros((NY, NX), jnp.float32)
    weight_total = jnp.zeros((NY, NX), jnp.float32)
    for offset_y in range(2 * RMAX + 1):
        for offset_x in range(2 * RMAX + 1):
            distance = jnp.sqrt(jnp.asarray((offset_y - RMAX) ** 2 + (offset_x - RMAX) ** 2, jnp.float32))
            weight = jnp.maximum(radius - distance, 0.0)
            piece = padded[offset_y:offset_y + NY, offset_x:offset_x + NX]
            present = inside[offset_y:offset_y + NY, offset_x:offset_x + NX]
            numerator = numerator + weight * present * piece
            weight_total = weight_total + weight * present
    filtered = numerator / weight_total
    base = math.tanh(sharpness * midpoint)
    projected = (base + jnp.tanh(sharpness * (filtered - midpoint))) / (base + math.tanh(sharpness * (1.0 - midpoint)))
    return (forward_out, adjoint_out, projected)
```

```python
import math

import jax
import jax.numpy as jnp
from jax import lax
from jax.experimental import pallas as pl
from jax.experimental.pallas import tpu as pltpu
from jax.sharding import PartitionSpec as P

NY = 512
NZ = 24
FREQS = 4
STEPS = 3
RMAX = 4


courant = 0.5
sharpness = 4.0
midpoint = 0.5
step_size = 0.3

PLANE = (NZ, NY)
VMEM = pl.BlockSpec(memory_space=pltpu.VMEM)
SMEM = pl.BlockSpec(memory_space=pltpu.SMEM)
ANY = pl.BlockSpec(memory_space=pl.ANY)
GRANT = 24 * 1024 * 1024


def ahead(plane, axis):
    size = plane.shape[axis]
    at = lax.broadcasted_iota(jnp.int32, plane.shape, axis)
    return jnp.where(at == size - 1, 0.0, pltpu.roll(plane, size - 1, axis))


def behind(plane, axis):
    at = lax.broadcasted_iota(jnp.int32, plane.shape, axis)
    return jnp.where(at == 0, 0.0, pltpu.roll(plane, 1, axis))


def dy_f(plane):
    return ahead(plane, 1) - plane


def dz_f(plane):
    return ahead(plane, 0) - plane


def dy_b(plane):
    return plane - behind(plane, 1)


def dz_b(plane):
    return plane - behind(plane, 0)


def magnetic_x(magn_x, elec):
    return magn_x - courant * (dy_f(elec[2]) - dz_f(elec[1]))


def magnetic_yz(magn, elec, following):
    next_y, next_z = (0.0, 0.0) if following is None else following
    return (
        magn[0] - courant * (dz_f(elec[0]) - (next_z - elec[2])),
        magn[1] - courant * ((next_y - elec[1]) - dy_f(elec[0])),
    )


def magnetic(magn, elec, following):
    return (magnetic_x(magn[0], elec),) + magnetic_yz(magn[1:], elec, following)


def electric_x(elec_x, magn, scaled):
    return elec_x + scaled * (dy_b(magn[2]) - dz_b(magn[1]))


def electric_yz(elec, magn, prior, scaled):
    prior_y, prior_z = (0.0, 0.0) if prior is None else prior
    return (
        elec[0] + scaled * (dz_b(magn[0]) - (magn[2] - prior_z)),
        elec[1] + scaled * ((magn[1] - prior_y) - dy_b(magn[0])),
    )


def electric(elec, magn, prior, scaled, source):
    return (electric_x(elec[0], magn, scaled) + source,) + electric_yz(
        elec[1:], magn, prior, scaled
    )


def source_of(run, turn, wave, profile, plane):
    at = lax.broadcasted_iota(jnp.int32, PLANE, 0)
    return jnp.where(at == plane[run], wave[run, turn] * profile[pl.ds(run, 1), :], 0.0)


def kernel_call(body, out_shape, in_specs, out_specs, scratch, name, flops=1, **more):
    sizes = sum(math.prod(s.shape) * 4 for s in jax.tree.leaves(out_shape))
    return pl.pallas_call(
        body,
        out_shape=out_shape,
        in_specs=in_specs,
        out_specs=out_specs,
        scratch_shapes=scratch,
        compiler_params=pltpu.CompilerParams(vmem_limit_bytes=GRANT),
        cost_estimate=pl.CostEstimate(flops=flops, bytes_accessed=2 * sizes, transcendentals=0),
        name=name,
        **more,
    )


def shaped(*shape):
    return jax.ShapeDtypeStruct(shape, jnp.float32)


def first_planes(fwd, adj, inverse, to_prior, to_next, rows_in, sems):
    rows = inverse.shape[0]
    copies = [
        pltpu.make_async_copy(fwd.at[0, :, rows - 1], rows_in.at[0], sems.at[0]),
        pltpu.make_async_copy(adj.at[0, :, rows - 1], rows_in.at[1], sems.at[1]),
        pltpu.make_async_copy(fwd.at[0, pl.ds(1, 2), 0], to_prior.at[pl.ds(0, 2)], sems.at[2]),
        pltpu.make_async_copy(adj.at[0, pl.ds(1, 2), 0], to_prior.at[pl.ds(2, 2)], sems.at[3]),
        pltpu.make_async_copy(inverse.at[0], to_prior.at[4], sems.at[4]),
        pltpu.make_async_copy(inverse.at[rows - 1], to_next.at[4], sems.at[5]),
    ]
    for copy in copies:
        copy.start()
    for run in range(2):
        copies[run].wait()
        state = [rows_in[run, k] for k in range(6)]
        magn = magnetic_yz(state[4:], state[:3], None)
        to_next[2 * run] = magn[0]
        to_next[2 * run + 1] = magn[1]
    for copy in copies[2:]:
        copy.wait()


def later_planes(fwd, adj, inverse, wave, profile, plane, to_prior, to_next, head, tail, inv, sems):
    rows = inverse.shape[0]
    copies = []
    for run, fields in enumerate((fwd, adj)):
        copies.append(
            pltpu.make_async_copy(fields.at[0, :, pl.ds(0, 3)], head.at[run], sems.at[2 * run])
        )
        copies.append(
            pltpu.make_async_copy(
                fields.at[0, :, pl.ds(rows - 3, 3)], tail.at[run], sems.at[2 * run + 1]
            )
        )
    copies.append(pltpu.make_async_copy(inverse, inv, sems.at[4]))
    for copy in copies:
        copy.start()
    for copy in copies:
        copy.wait()

    def one_run(run, carry):
        def row(ref, x):
            return (
                tuple(ref[run, k, x] for k in range(3)),
                tuple(ref[run, k, x] for k in range(3, 6)),
            )

        source = source_of(run, 0, wave, profile, plane)
        (elec_0, magn_0), (elec_1, magn_1) = row(head, 0), row(head, 1)
        scaled_0, scaled_1 = courant * inv[0], courant * inv[1]
        magn_0 = magnetic(magn_0, elec_0, elec_1[1:])
        magn_1 = magnetic(magn_1, elec_1, (head[run, 1, 2], head[run, 2, 2]))
        elec_0 = electric(elec_0, magn_0, None, scaled_0, source)
        to_prior[2 * run] = elec_0[1]
        to_prior[2 * run + 1] = elec_0[2]
        after = electric_yz(elec_1[1:], magn_1, magn_0[1:], scaled_1)
        magn_0 = magnetic(magn_0, elec_0, after)
        sent = electric_yz(elec_0[1:], magn_0, None, scaled_0)
        to_prior[4 + 2 * run] = sent[0]
        to_prior[4 + 2 * run + 1] = sent[1]
        (elec_5, magn_5), (elec_6, magn_6), (elec_7, magn_7) = (row(tail, x) for x in range(3))
        scaled_6, scaled_7 = courant * inv[rows - 2], courant * inv[rows - 1]
        yz_5 = magnetic_yz(magn_5[1:], elec_5, elec_6[1:])
        magn_6 = magnetic(magn_6, elec_6, elec_7[1:])
        magn_7 = magnetic(magn_7, elec_7, None)
        elec_6 = electric(elec_6, magn_6, yz_5, scaled_6, source)
        elec_7 = electric(elec_7, magn_7, magn_6[1:], scaled_7, source)
        yz_6 = magnetic_yz(magn_6[1:], elec_6, elec_7[1:])
        magn_7 = magnetic(magn_7, elec_7, None)
        to_next[2 * run] = magn_7[1]
        to_next[2 * run + 1] = magn_7[2]
        source = source_of(run, 1, wave, profile, plane)
        elec_7 = electric(elec_7, magn_7, yz_6, scaled_7, source)
        sent = magnetic_yz(magn_7[1:], elec_7, None)
        to_next[4 + 2 * run] = sent[0]
        to_next[4 + 2 * run + 1] = sent[1]
        return carry

    lax.fori_loop(0, 2, one_run, 0)


def load_row(state, run, first, x):
    return tuple(state[run, first + k, x] for k in range(3))


def store_row(state, run, first, x, planes):
    for k, value in enumerate(planes):
        state[run, first + k, x] = value


def advance_magnetic(state, run, x, following):
    magn = magnetic(load_row(state, run, 3, x), load_row(state, run, 0, x), following)
    store_row(state, run, 3, x, magn)
    return magn


def advance_electric(state, run, x, prior, scaled, source):
    elec = electric(
        load_row(state, run, 0, x), load_row(state, run, 3, x), prior, scaled, source
    )
    store_row(state, run, 0, x, elec)
    return elec


def electric_at(state, run, x):
    return (state[run, 1, x], state[run, 2, x])


def magnetic_at(state, run, x):
    return (state[run, 4, x], state[run, 5, x])


def products(state, x):
    total = state[0, 0, x] * state[1, 0, x]
    for k in (1, 2):
        total = total + state[0, k, x] * state[1, k, x]
    return jnp.sum(total.reshape(NZ // 8, 8, NY), axis=0)


def interior(fwd, adj, inverse, wave, profile, plane, fwd_out, adj_out, share, state, inv, sems):
    rows = inverse.shape[0]
    into = [
        pltpu.make_async_copy(fwd.at[0], state.at[0], sems.at[0]),
        pltpu.make_async_copy(adj.at[0], state.at[1], sems.at[1]),
        pltpu.make_async_copy(inverse, inv, sems.at[2]),
    ]
    for copy in into:
        copy.start()
    for copy in into:
        copy.wait()
    share[...] = jnp.zeros_like(share)
    for turn in range(STEPS):

        def one_run(run, carry, turn=turn):
            source = source_of(run, turn, wave, profile, plane)

            def one_row(x, carry):
                advance_magnetic(state, run, x, electric_at(state, run, x + 1))

                @pl.when(x > turn)
                def _():
                    advance_electric(
                        state, run, x, magnetic_at(state, run, x - 1), courant * inv[x], source
                    )

                return carry

            return lax.fori_loop(turn, rows - 1 - turn, one_row, carry)

        lax.fori_loop(0, 2, one_run, 0)

        def gather(x, carry):
            share[x] = share[x] + products(state, x)
            return carry

        lax.fori_loop(turn + 1, rows - 1 - turn, gather, 0)
    out = [
        pltpu.make_async_copy(state.at[0], fwd_out.at[0], sems.at[0]),
        pltpu.make_async_copy(state.at[1], adj_out.at[0], sems.at[1]),
    ]
    for copy in out:
        copy.start()
    for copy in out:
        copy.wait()


def borders(
    fwd, adj, inverse, wave, profile, plane, has_prior, share, prior_a, prior_b, next_a, next_b,
    fwd_out, adj_out, blocks, state, inv, resp, total, sems,
):
    rows = inverse.shape[0]
    head, tail = pl.ds(0, 3), pl.ds(rows - 4, 4)
    into = [pltpu.make_async_copy(inverse, inv, sems.at[4])]
    for run, fields in enumerate((fwd, adj)):
        for part, where in enumerate((head, tail)):
            into.append(
                pltpu.make_async_copy(
                    fields.at[0, :, where], state.at[run, :, where], sems.at[2 * run + part]
                )
            )
    for copy in into:
        copy.start()
    for copy in into:
        copy.wait()
    last = rows - 1
    flagged = courant * has_prior[0]
    for turn in range(STEPS):

        def one_run(run, carry, turn=turn):
            source = source_of(run, turn, wave, profile, plane)
            scaled_prior = courant * prior_a[4]
            scaled_next = courant * next_a[4]
            own_y, own_z = electric_at(state, run, 0)
            if turn == 0:
                magn_r = (None, flagged * own_z, -flagged * own_y)
                received = (prior_a[2 * run], prior_a[2 * run + 1])
            else:
                elec_r = tuple(resp[run, k] for k in range(3))
                old = tuple(resp[run, k] for k in range(3, 6))
                magn_r = (
                    old[0] - courant * (dy_f(elec_r[2]) - dz_f(elec_r[1])),
                    old[1] - courant * (dz_f(elec_r[0]) + elec_r[2]) + flagged * own_z,
                    old[2] + courant * (elec_r[1] + dy_f(elec_r[0])) - flagged * own_y,
                )
                at = 4 * (turn - 1) + 2 * run
                received = (prior_b[at], prior_b[at + 1])
            prior = (received[0] + magn_r[1], received[1] + magn_r[2])
            if turn == 0:
                resp[run, 0] = scaled_prior * (dy_b(magn_r[2]) - dz_b(magn_r[1]))
                resp[run, 1] = -scaled_prior * magn_r[2]
                resp[run, 2] = scaled_prior * magn_r[1]
                resp[run, 3] = jnp.zeros(PLANE, jnp.float32)
            elif turn == 1:
                resp[run, 0] = elec_r[0] + scaled_prior * (dy_b(magn_r[2]) - dz_b(magn_r[1]))
                resp[run, 1] = elec_r[1] + scaled_prior * (
                    dz_b(magn_r[0]) - (magn_r[2] + courant * elec_r[1])
                )
                resp[run, 2] = elec_r[2] + scaled_prior * (
                    (magn_r[1] - courant * elec_r[2]) - dy_b(magn_r[0])
                )
                resp[run, 3] = magn_r[0]
            if turn < STEPS - 1:
                resp[run, 4] = magn_r[1]
                resp[run, 5] = magn_r[2]
            for x in range(turn):
                advance_magnetic(state, run, x, electric_at(state, run, x + 1))
            for x in range(turn + 1):
                before = prior if x == 0 else magnetic_at(state, run, x - 1)
                advance_electric(state, run, x, before, courant * inv[x], source)
            if turn == 0:
                following = (next_a[2 * run], next_a[2 * run + 1])
            else:
                at = 4 * (turn - 1) + 2 * run
                following = (next_b[at] + resp[run, 6], next_b[at + 1] + resp[run, 7])
            for x in range(last - turn, last):
                advance_magnetic(state, run, x, electric_at(state, run, x + 1))
            magn = advance_magnetic(state, run, last, following)
            for x in range(last - turn, last + 1):
                before = magnetic_at(state, run, x - 1)
                advance_electric(state, run, x, before, courant * inv[x], source)
            if turn == 0:
                resp[run, 6] = scaled_next * magn[2]
                resp[run, 7] = -scaled_next * magn[1]
            elif turn == 1:
                elec_y, elec_z = resp[run, 6], resp[run, 7]
                magn_x = -courant * (dy_f(elec_z) - dz_f(elec_y))
                resp[run, 6] = elec_y + scaled_next * (
                    dz_b(magn_x) - (courant * elec_y - magn[2])
                )
                resp[run, 7] = elec_z + scaled_next * (
                    (-courant * elec_z - magn[1]) - dy_b(magn_x)
                )
            return carry

        lax.fori_loop(0, 2, one_run, 0)
        if turn == STEPS - 1:
            out = []
            for run, fields in enumerate((fwd_out, adj_out)):
                for part, where in enumerate((pl.ds(0, 3), pl.ds(rows - 3, 3))):
                    out.append(
                        pltpu.make_async_copy(
                            state.at[run, :, where], fields.at[0, :, where], sems.at[2 * run + part]
                        )
                    )
            for copy in out:
                copy.start()
        for x in list(range(turn + 1)) + list(range(last - turn, last + 1)):
            before = share[x] if turn == min(x, last - x) else total[x]
            total[x] = before + products(state, x)
    for x in range(STEPS, rows - STEPS):
        total[x] = share[x]
    summed = jnp.sum(total[...], axis=1)
    slabs, width = blocks.shape[1], blocks.shape[3]
    for k in range(slabs):
        turned = pltpu.roll(summed, (RMAX - k * (NY // slabs)) % NY, 1)
        for f in range(blocks.shape[0]):
            blocks[f, k] = turned[:, :width]
    for copy in out:
        copy.wait()


def moved(rows, by):
    if by == 0:
        return rows
    count = rows.shape[0]
    at = lax.broadcasted_iota(jnp.int32, rows.shape, 0)
    keep = at < count - by if by > 0 else at >= -by
    return jnp.where(keep, pltpu.roll(rows, (-by) % count, 0), 0.0)


def weighted(cells, radius):
    tile = cells.shape[1] - 2 * RMAX
    columns = [cells[:, RMAX : RMAX + tile]]
    for a in range(1, RMAX + 1):
        columns.append(
            cells[:, RMAX - a : RMAX - a + tile] + cells[:, RMAX + a : RMAX + a + tile]
        )
    rings = {}
    for a in range(RMAX + 1):
        for b in range(RMAX + 1):
            part = columns[a]
            if b > 0:
                part = moved(part, b) + moved(part, -b)
            square = a * a + b * b
            rings[square] = rings[square] + part if square in rings else part
    total = None
    for square, part in rings.items():
        term = jnp.maximum(radius - math.sqrt(square), 0.0) * part
        total = term if total is None else total + term
    return total


def by_tile(values, count):
    columns = count // values.shape[1]
    at = lax.broadcasted_iota(jnp.int32, (count, 1), 0) // columns
    spread = jnp.zeros((count, 1), jnp.float32)
    for k in range(values.shape[1]):
        spread = jnp.where(at == k, values[0, k].astype(jnp.float32), spread)
    return spread


def weight_sums(radius_map, inside, weights):
    weights[...] = weighted(inside[...], by_tile(radius_map, inside.shape[0]))


def project(blocks, density, chosen, weights, radius_map, projected):
    freqs, slabs, rows, width = blocks.shape
    gradient = jnp.sum(blocks[...], axis=0).reshape(slabs * rows, width)
    updated = density[...] + chosen[...] * gradient
    numerator = weighted(updated, by_tile(radius_map, slabs * rows))
    filtered = numerator / weights[...]
    base = math.tanh(sharpness * midpoint)
    value = (base + jnp.tanh(sharpness * (filtered - midpoint))) / (
        base + math.tanh(sharpness * (1.0 - midpoint))
    )
    projected[...] = value.T


def shifted(shard, axis, by):
    length = lax.axis_size(axis)
    pairs = [(i, i + by) for i in range(length) if 0 <= i + by < length]
    return lax.ppermute(shard, axis, pairs)


def on_device(
    inverse_permittivity,
    forward_fields,
    adjoint_fields,
    source_wave,
    source_profile,
    adjoint_wave,
    adjoint_profile,
    source_plane,
    monitor_plane,
    radius_map,
    design_mask,
    design_density,
):
    rows = forward_fields.shape[2]
    freqs, slabs = lax.axis_size("freq"), lax.axis_size("slab")
    slab = lax.axis_index("slab")
    tile_rows, width = design_density.shape
    reach = tile_rows + 2 * RMAX
    wave = jnp.concatenate([source_wave, adjoint_wave])
    profile = jnp.concatenate([source_profile, adjoint_profile])
    plane = jnp.concatenate([source_plane, monitor_plane])
    fields = (forward_fields, adjoint_fields, inverse_permittivity)
    sources = (wave, profile, plane)
    source_specs = [SMEM, VMEM, SMEM]
    dma = pltpu.SemaphoreType.DMA
    work = 45 * 12 * 1024

    to_prior_a, to_next_a = kernel_call(
        first_planes,
        (shaped(5, *PLANE), shaped(5, *PLANE)),
        [ANY] * 3,
        (VMEM, VMEM),
        [pltpu.VMEM((2, 6) + PLANE, jnp.float32), dma((6,))],
        "first_planes",
    )(*fields)
    next_a = shifted(to_prior_a, "slab", -1)
    prior_a = shifted(to_next_a, "slab", 1)
    to_prior_b, to_next_b = kernel_call(
        later_planes,
        (shaped(8, *PLANE), shaped(8, *PLANE)),
        [ANY] * 3 + source_specs,
        (VMEM, VMEM),
        [
            pltpu.VMEM((2, 6, 3) + PLANE, jnp.float32),
            pltpu.VMEM((2, 6, 3) + PLANE, jnp.float32),
            pltpu.VMEM((rows,) + PLANE, jnp.float32),
            dma((5,)),
        ],
        "later_planes",
        flops=14 * work,
    )(*fields, *sources)
    next_b = shifted(to_prior_b, "slab", -1)
    prior_b = shifted(to_next_b, "slab", 1)

    chosen_row = jnp.repeat(design_mask, width // design_mask.shape[1], axis=1).astype(jnp.float32)
    top = shifted(jnp.concatenate([design_density[-RMAX:], chosen_row]), "slab", 1)
    bottom = shifted(jnp.concatenate([design_density[:RMAX], chosen_row]), "slab", -1)
    density = jnp.concatenate([top[:RMAX], design_density, bottom[:RMAX]]).T
    scale = step_size / math.sqrt(3 * STEPS * NZ * FREQS)
    chosen = scale * jnp.concatenate(
        [
            jnp.broadcast_to(top[RMAX:], (RMAX, width)),
            jnp.broadcast_to(chosen_row, (tile_rows, width)),
            jnp.broadcast_to(bottom[RMAX:], (RMAX, width)),
        ]
    ).T
    global_y = slab * tile_rows - RMAX + jnp.arange(reach, dtype=jnp.int32)
    inside_y = ((global_y >= 0) & (global_y < NY)).astype(jnp.float32)
    inside = jnp.broadcast_to(inside_y[None, :], (width, reach))
    weights = kernel_call(
        weight_sums, shaped(width, tile_rows), [SMEM, VMEM], VMEM, [], "weight_sums"
    )(radius_map, inside)

    state_shape = (2, 6, rows) + PLANE
    forward_part, adjoint_part, share = kernel_call(
        interior,
        (
            shaped(*forward_fields.shape),
            shaped(*adjoint_fields.shape),
            shaped(rows, 8, NY),
        ),
        [ANY] * 3 + source_specs,
        (ANY, ANY, VMEM),
        [
            pltpu.VMEM(state_shape, jnp.float32),
            pltpu.VMEM((rows,) + PLANE, jnp.float32),
            dma((3,)),
        ],
        "interior",
        flops=24 * work,
    )(*fields, *sources)
    has_prior = (slab > 0).astype(jnp.float32).reshape(1)
    forward_out, adjoint_out, blocks = kernel_call(
        borders,
        (
            shaped(*forward_fields.shape),
            shaped(*adjoint_fields.shape),
            shaped(freqs, slabs, rows, reach),
        ),
        [ANY] * 3 + source_specs + [SMEM] + [VMEM] * 5,
        (ANY, ANY, VMEM),
        [
            pltpu.VMEM(state_shape, jnp.float32),
            pltpu.VMEM((rows,) + PLANE, jnp.float32),
            pltpu.VMEM((2, 8) + PLANE, jnp.float32),
            pltpu.VMEM((rows, 8, NY), jnp.float32),
            dma((5,)),
        ],
        "borders",
        flops=24 * work,
        input_output_aliases={0: 0, 1: 1},
    )(
        forward_part, adjoint_part, inverse_permittivity, *sources, has_prior, share,
        prior_a, prior_b, next_a, next_b,
    )

    blocks = blocks.reshape(freqs * slabs, rows, reach)
    blocks = lax.all_to_all(blocks, ("freq", "slab"), 0, 0, tiled=True)
    blocks = blocks.reshape(freqs, slabs, rows, reach)
    projected = kernel_call(
        project,
        shaped(tile_rows, width),
        [VMEM] * 4 + [SMEM],
        VMEM,
        [],
        "project",
    )(blocks, density, chosen, weights, radius_map)
    return (forward_out, adjoint_out, projected)


def solution(mesh):
    return jax.shard_map(
        on_device,
        mesh=mesh,
        in_specs=(
            P("slab", None, None),
            P("freq", None, "slab", None, None),
            P("freq", None, "slab", None, None),
            P("freq", None),
            P("freq", None),
            P("freq", None),
            P("freq", None),
            P("freq"),
            P("freq"),
            P("slab", None),
            P("slab", None),
            P("slab", None),
        ),
        out_specs=(
            P("freq", None, "slab", None, None),
            P("freq", None, "slab", None, None),
            P("slab", None),
        ),
        check_vma=False,
    )
```

```python
import math

import jax
import jax.numpy as jnp
from jax import lax
from jax.experimental import pallas as pl
from jax.experimental.pallas import tpu as pltpu
from jax.sharding import PartitionSpec as P

NY = 512
NZ = 24
FREQS = 4
STEPS = 3
RMAX = 4


courant = 0.5
sharpness = 4.0
midpoint = 0.5
step_size = 0.3

PLANE = (NZ, NY)
VMEM = pl.BlockSpec(memory_space=pltpu.VMEM)
SMEM = pl.BlockSpec(memory_space=pltpu.SMEM)
HBM = pl.BlockSpec(memory_space=pltpu.HBM)
ANY = pl.BlockSpec(memory_space=pl.ANY)
GRANT = 16 * 1024 * 1024
EXTRA = 8
SENT = 5 * NZ + EXTRA


def ahead(plane, axis):
    size = plane.shape[axis]
    at = lax.broadcasted_iota(jnp.int32, plane.shape, axis)
    return jnp.where(at == size - 1, 0.0, pltpu.roll(plane, size - 1, axis))


def behind(plane, axis):
    at = lax.broadcasted_iota(jnp.int32, plane.shape, axis)
    return jnp.where(at == 0, 0.0, pltpu.roll(plane, 1, axis))


def dy_f(plane):
    return ahead(plane, 1) - plane


def dz_f(plane):
    return ahead(plane, 0) - plane


def dy_b(plane):
    return plane - behind(plane, 1)


def dz_b(plane):
    return plane - behind(plane, 0)


def magnetic_x(magn_x, elec):
    return magn_x - courant * (dy_f(elec[2]) - dz_f(elec[1]))


def magnetic_yz(magn, elec, following):
    next_y, next_z = (0.0, 0.0) if following is None else following
    return (
        magn[0] - courant * (dz_f(elec[0]) - (next_z - elec[2])),
        magn[1] - courant * ((next_y - elec[1]) - dy_f(elec[0])),
    )


def magnetic(magn, elec, following):
    return (magnetic_x(magn[0], elec),) + magnetic_yz(magn[1:], elec, following)


def electric_x(elec_x, magn, scaled):
    return elec_x + scaled * (dy_b(magn[2]) - dz_b(magn[1]))


def electric_yz(elec, magn, prior, scaled):
    prior_y, prior_z = (0.0, 0.0) if prior is None else prior
    return (
        elec[0] + scaled * (dz_b(magn[0]) - (magn[2] - prior_z)),
        elec[1] + scaled * ((magn[1] - prior_y) - dy_b(magn[0])),
    )


def electric(elec, magn, prior, scaled, source):
    return (electric_x(elec[0], magn, scaled) + source,) + electric_yz(
        elec[1:], magn, prior, scaled
    )


SOURCE_SCRATCH = [
    pltpu.VMEM((2, 1, STEPS), jnp.float32),
    pltpu.VMEM((2, 1, NY), jnp.float32),
    pltpu.SemaphoreType.DMA((4,)),
]
SOURCE_SPECS = [HBM] * 4 + [SMEM] * 2
SOURCE_VALUES = [VMEM] * 4 + [SMEM] * 2


def source_copies(given, scratch):
    wave, profile, sems = scratch
    return [
        pltpu.make_async_copy(given[2 * k + run], ref.at[run], sems.at[2 * k + run])
        for k, ref in enumerate((wave, profile))
        for run in range(2)
    ]


def source_of(run, turn, given, scratch):
    if scratch:
        wave, profile = scratch[0][run], scratch[1][run]
    else:
        wave, profile = (jnp.where(run == 0, given[k][...], given[k + 1][...]) for k in (0, 2))
    row = wave[:, turn : turn + 1] * profile
    plane = jnp.where(run == 0, given[4][0], given[5][0])
    at = lax.broadcasted_iota(jnp.int32, PLANE, 0)
    return jnp.where(at == plane, row, 0.0)


def kernel_call(body, out_shape, in_specs, out_specs, scratch, name, micros=1, **more):
    sizes = sum(math.prod(s.shape) * 4 for s in jax.tree.leaves(out_shape))
    return pl.pallas_call(
        body,
        out_shape=out_shape,
        in_specs=in_specs,
        out_specs=out_specs,
        scratch_shapes=scratch,
        compiler_params=pltpu.CompilerParams(vmem_limit_bytes=GRANT),
        cost_estimate=pl.CostEstimate(
            flops=micros * 10**9, bytes_accessed=2 * sizes, transcendentals=0
        ),
        name=name,
        **more,
    )


def shaped(*shape):
    return jax.ShapeDtypeStruct(shape, jnp.float32)


def start_all(copies):
    for copy in copies:
        copy.start()


def wait_all(copies):
    for copy in copies:
        copy.wait()


def plane_at(index):
    return pl.ds(pl.multiple_of(index * NZ, 8), NZ)


def first_planes(
    fwd, adj, inverse, density, mask, to_prior, to_next, rows_in, cells, chosen, sems
):
    rows = inverse.shape[0]
    width = density.shape[1]
    copies = [
        pltpu.make_async_copy(fwd.at[0, :, rows - 1], rows_in.at[0], sems.at[0]),
        pltpu.make_async_copy(adj.at[0, :, rows - 1], rows_in.at[1], sems.at[1]),
        pltpu.make_async_copy(density, cells, sems.at[2]),
        pltpu.make_async_copy(mask, chosen, sems.at[3]),
        pltpu.make_async_copy(inverse.at[0], to_prior.at[plane_at(4)], sems.at[4]),
        pltpu.make_async_copy(inverse.at[rows - 1], to_next.at[plane_at(4)], sems.at[5]),
    ]
    for run, fields in enumerate((fwd, adj)):
        for k in range(2):
            at = 2 * run + k
            copies.append(
                pltpu.make_async_copy(
                    fields.at[0, 1 + k, 0], to_prior.at[plane_at(at)], sems.at[6 + at]
                )
            )
    start_all(copies)
    wait_all(copies[2:4])
    at = lax.broadcasted_iota(jnp.int32, (1, width), 1) // (width // mask.shape[1])
    spread = jnp.zeros((1, width), jnp.float32)
    for k in range(mask.shape[1]):
        spread = jnp.where(at == k, chosen[:, k : k + 1].astype(jnp.float32), spread)
    for sent, first in ((to_prior, 0), (to_next, density.shape[0] - RMAX)):
        sent[pl.ds(5 * NZ, EXTRA), :] = jnp.zeros((EXTRA, NY), jnp.float32)
        sent[pl.ds(5 * NZ, RMAX), pl.ds(0, width)] = cells[pl.ds(first, RMAX), :]
        sent[pl.ds(5 * NZ + RMAX, 1), pl.ds(0, width)] = spread
    for run in range(2):
        copies[run].wait()
        planes = [rows_in[run, k] for k in range(6)]
        magn = magnetic_yz(planes[4:], planes[:3], None)
        for k in range(2):
            to_next[plane_at(2 * run + k), :] = magn[k]
    wait_all(copies[4:])


class State:
    def __init__(self, given, home, written):
        self.given, self.home = given, home
        self.written = None if given is None else set(written)

    def load(self, run, first, x, count=3):
        parts = []
        for k in range(first, first + count):
            at_home = self.written is None or (k, x) in self.written
            ref, at = (self.home if at_home else self.given)(k, x)
            parts.append(ref[run, k, at])
        return tuple(parts)

    def store(self, run, first, x, planes):
        for k, value in enumerate(planes):
            ref, at = self.home(first + k, x)
            ref[run, first + k, at] = value
            if self.written is not None:
                self.written.add((first + k, x))

    def magnetic(self, run, x, following):
        magn = magnetic(self.load(run, 3, x), self.load(run, 0, x), following)
        self.store(run, 3, x, magn)
        return magn

    def electric(self, run, x, prior, scaled, source):
        elec = electric(self.load(run, 0, x), self.load(run, 3, x), prior, scaled, source)
        self.store(run, 0, x, elec)

    def electric_yz(self, run, x):
        return self.load(run, 1, x, 2)

    def magnetic_yz(self, run, x):
        return self.load(run, 4, x, 2)


def in_place(ref):
    return State(None, lambda k, x: (ref, x), ())


def products(ref, x):
    total = ref[0, 0, x] * ref[1, 0, x]
    for k in (1, 2):
        total = total + ref[0, k, x] * ref[1, k, x]
    return jnp.sum(total.reshape(NZ // 8, 8, NY), axis=0)


def interior(fwd, adj, inverse, *rest):
    given, (to_prior, to_next, own, fwd_out, adj_out, state, share), (inv, sems, *scratch) = (
        rest[:6], rest[6:13], rest[13:]
    )
    rows = inverse.shape[0]
    last = rows - 1
    into = source_copies(given, scratch) + [pltpu.make_async_copy(inverse, inv, sems.at[4])]

    def load(fields, run):
        return pltpu.make_async_copy(fields.at[0], state.at[run], sems.at[run])

    start_all([load(fwd, 0)] + into + [load(adj, 1)])
    wait_all(into)
    rows_of = in_place(state)

    def edges(run, source):
        elec = electric(
            rows_of.load(run, 0, 0), rows_of.load(run, 3, 0), None, courant * inv[0], source
        )
        for k in range(2):
            to_prior[plane_at(2 * run + k), :] = elec[1 + k]
        for k in range(3):
            own[run, k] = elec[k]
        elec, magn = rows_of.load(run, 0, last), rows_of.load(run, 3, last)
        magn = magnetic(magn, elec, None)
        elec = electric(
            elec, magn, rows_of.magnetic_yz(run, last - 1), courant * inv[last], source
        )
        magn = magnetic(magn, elec, None)
        for k in range(2):
            to_next[plane_at(2 * run + k), :] = magn[1 + k]
        for k in range(3):
            own[run, 3 + k] = elec[k]
            own[run, 6 + k] = magn[k]

    for turn in range(STEPS):

        def one_run(run, carry, turn=turn):
            if turn == 0:
                load(fwd, run).wait()
            source = source_of(run, turn, given, scratch)
            for x in range(turn, last - turn):
                rows_of.magnetic(run, x, rows_of.electric_yz(run, x + 1))
                if x > turn:
                    rows_of.electric(
                        run, x, rows_of.magnetic_yz(run, x - 1), courant * inv[x], source
                    )
            if turn == 0:
                edges(run, source)
            return carry

        lax.fori_loop(0, 2, one_run, 0)
        for x in range(turn + 1, last - turn):
            share[x] = products(state, x) + (share[x] if turn > 0 else 0.0)
    for x in (0, last):
        share[x] = jnp.zeros(share.shape[1:], jnp.float32)
    out = []
    for run, fields in enumerate((fwd_out, adj_out)):
        for kind, first in enumerate((STEPS, STEPS - 1)):
            done = (pl.ds(3 * kind, 3), pl.ds(first, rows - STEPS - first))
            out.append(
                pltpu.make_async_copy(
                    state.at[run, *done], fields.at[0, *done], sems.at[2 * run + kind]
                )
            )
    start_all(out)
    wait_all(out)


def flags():
    slab = lax.axis_index("slab")
    has_prior = (slab > 0).astype(jnp.float32)
    has_next = (slab < lax.axis_size("slab") - 1).astype(jnp.float32)
    return has_prior, has_next


def border_rows(run, turn, state, source, inv, resp_in, resp_out, prior_a, next_a, here):
    has_prior, has_next = flags()
    flagged = courant * has_prior
    last = inv.shape[0] - 1
    whole = here is not None
    scaled_prior = flagged * prior_a[plane_at(4), :]
    scaled_next = (courant * has_next) * next_a[plane_at(4), :]

    def received(ref):
        return tuple(ref[plane_at(2 * run + k), :] for k in range(2))

    own_y, own_z = state.electric_yz(run, 0)
    if turn == 0:
        magn_r = (None, flagged * own_z, -flagged * own_y)
    else:
        elec_r = tuple(resp_in[run, k] for k in range(3))
        old = tuple(resp_in[run, k] for k in range(3, 6))
        magn_r = (
            old[0] - courant * (dy_f(elec_r[2]) - dz_f(elec_r[1])),
            old[1] - courant * (dz_f(elec_r[0]) + elec_r[2]) + flagged * own_z,
            old[2] + courant * (elec_r[1] + dy_f(elec_r[0])) - flagged * own_y,
        )
    if turn == 0:
        resp_out[run, 0] = scaled_prior * (dy_b(magn_r[2]) - dz_b(magn_r[1]))
        resp_out[run, 1] = -scaled_prior * magn_r[2]
        resp_out[run, 2] = scaled_prior * magn_r[1]
        resp_out[run, 3] = jnp.zeros(PLANE, jnp.float32)
    elif whole:
        resp_out[run, 0] = elec_r[0] + scaled_prior * (dy_b(magn_r[2]) - dz_b(magn_r[1]))
        resp_out[run, 1] = elec_r[1] + scaled_prior * (
            dz_b(magn_r[0]) - (magn_r[2] + courant * elec_r[1])
        )
        resp_out[run, 2] = elec_r[2] + scaled_prior * (
            (magn_r[1] - courant * elec_r[2]) - dy_b(magn_r[0])
        )
        resp_out[run, 3] = magn_r[0]
    resp_out[run, 4] = magn_r[1]
    resp_out[run, 5] = magn_r[2]
    for x in range(turn):
        state.magnetic(run, x, state.electric_yz(run, x + 1))
    if whole:
        arrived = received(here[0])
        prior = tuple(has_prior * arrived[k] + magn_r[1 + k] for k in range(2))
        state.electric(run, 0, prior, courant * inv[0], source)
    else:
        elec_x = electric_x(state.load(run, 0, 0, 1)[0], state.load(run, 3, 0), courant * inv[0])
        state.store(run, 0, 0, (elec_x + source,))
    for x in range(1, turn + 1):
        state.electric(run, x, state.magnetic_yz(run, x - 1), courant * inv[x], source)
    for x in range(last - turn, last):
        state.magnetic(run, x, state.electric_yz(run, x + 1))
    if whole:
        arrived = received(here[1])
        following = tuple(has_next * plane for plane in arrived)
        if turn > 0:
            following = tuple(following[k] + resp_in[run, 6 + k] for k in range(2))
        magn = state.magnetic(run, last, following)
    else:
        magn_x = magnetic_x(state.load(run, 3, last, 1)[0], state.load(run, 0, last))
        state.store(run, 3, last, (magn_x,))
    for x in range(last - turn, last + (1 if whole else 0)):
        state.electric(run, x, state.magnetic_yz(run, x - 1), courant * inv[x], source)
    if turn == 0:
        resp_out[run, 6] = scaled_next * magn[2]
        resp_out[run, 7] = -scaled_next * magn[1]
    elif whole:
        elec_y, elec_z = resp_in[run, 6], resp_in[run, 7]
        magn_x = -courant * (dy_f(elec_z) - dz_f(elec_y))
        resp_out[run, 6] = elec_y + scaled_next * (dz_b(magn_x) - (courant * elec_y - magn[2]))
        resp_out[run, 7] = elec_z + scaled_next * (
            (-courant * elec_z - magn[1]) - dy_b(magn_x)
        )
    else:
        resp_out[run, 6] = resp_in[run, 6]
        resp_out[run, 7] = resp_in[run, 7]


def step_one(inv, *rest):
    given, (before, own, prior_a, next_a), (to_prior, to_next, early, resp, share) = (
        rest[:6], rest[6:10], rest[10:]
    )
    last = inv.shape[0] - 1

    def one_run(run, carry):
        state = State(lambda k, x: (before, x), lambda k, x: (early, min(x, 1)), ())
        source = source_of(run, 0, given, ())
        scaled = courant * inv[0]
        elec = tuple(own[run, k] for k in range(3))
        magn = magnetic(state.load(run, 3, 0), elec, state.electric_yz(run, 1))
        sent = electric_yz(elec[1:], magn, None, scaled)
        for k in range(2):
            to_prior[plane_at(2 * run + k), :] = sent[k]
        elec = tuple(own[run, 3 + k] for k in range(3))
        magn = tuple(own[run, 6 + k] for k in range(3))
        yz = magnetic_yz(
            state.magnetic_yz(run, last - 1), state.load(run, 0, last - 1), elec[1:]
        )
        elec = electric(elec, magn, yz, courant * inv[last], source_of(run, 1, given, ()))
        sent = magnetic_yz(magn[1:], elec, None)
        for k in range(2):
            to_next[plane_at(2 * run + k), :] = sent[k]
        border_rows(
            run, 0, state, source, inv, None, resp, prior_a, next_a, (prior_a, next_a)
        )
        return carry

    lax.fori_loop(0, 2, one_run, 0)
    for side in range(2):
        share[side] = products(early, side)


def borders(fwd, adj, inv, *rest):
    given, (before, early, resp_in, share, ends, prior_a, next_a, prior_b, next_b) = (
        rest[:6], rest[6:15]
    )
    fwd_out, adj_out, kept, summed, waiting, inner, resp, total, sems = rest[15:]
    rows = inv.shape[0]
    last = rows - 1
    homes = {0: (kept, 0), last - 1: (kept, 1), last: (kept, 2)}
    homes |= {1: (inner, 0), 2: (inner, 1), last - 2: (inner, 2)}

    def handed_in(k, x):
        if x == last or (x == 0 and k < 3):
            return (early, min(x, 1))
        return (before, x)

    written = set()
    for turn in range(1, STEPS):
        whole = turn < STEPS - 1
        seen = []

        def one_run(run, carry, turn=turn, whole=whole, seen=seen):
            state = State(handed_in, lambda k, x: homes[x], written)
            border_rows(
                run, turn, state, source_of(run, turn, given, ()), inv,
                resp_in if turn == 1 else resp, resp if whole else waiting, prior_a, next_a,
                (prior_b, next_b) if whole else None,
            )
            seen[:] = [state.written]
            return carry

        lax.fori_loop(0, 2, one_run, 0)
        written = seen[0]
        if not whole:
            out = []
            for run, fields in enumerate((fwd_out, adj_out)):
                for part, (ref, at, x, count, first, parts) in enumerate(
                    (
                        (inner, 0, 1, 1, 0, 6),
                        (inner, 1, 2, 1, 0, 3),
                        (inner, 2, last - 2, 1, 0, 6),
                        (kept, 1, last - 1, 1, 0, 6),
                        (kept, 0, 0, 1, 0, 1),
                        (kept, 0, 0, 1, 3, 3),
                        (kept, 2, last, 1, 3, 1),
                    )
                ):
                    out.append(
                        pltpu.make_async_copy(
                            ref.at[run, pl.ds(first, parts), pl.ds(at, count)],
                            fields.at[0, pl.ds(first, parts), pl.ds(x, count)],
                            sems.at[7 * run + part],
                        )
                    )
            start_all(out)
        reached = list(range(turn + 1)) + list(range(last - turn, last + 1))
        for x in reached if whole else reached[1:-1]:
            if turn > 1 and min(x, last - x) < turn:
                so_far = total[x]
            else:
                so_far = ends[min(x, 1)] if x in (0, last) else share[x]
            total[x] = so_far + products(*homes[x])
    for x in range(STEPS, rows - STEPS):
        total[x] = share[x]
    summed[...] = jnp.sum(total[...], axis=1)
    wait_all(out)


def last_planes(fwd, adj, inv, *rest):
    given, (kept, summed, waiting, prior_c, next_c) = rest[:6], rest[6:11]
    fwd_out, adj_out, blocks, front, back, back_h, sems = rest[11:]
    last = inv.shape[0] - 1
    has_prior, has_next = flags()

    def one_run(run, carry):
        def row(first, slot, count):
            return tuple(kept[run, first + k, slot] for k in range(count))

        def arrived(ref, flag, first):
            return tuple(
                flag * ref[plane_at(2 * run + k), :] + waiting[run, first + k] for k in range(2)
            )

        elec = electric_yz(
            row(1, 0, 2), row(3, 0, 3), arrived(prior_c, has_prior, 4), courant * inv[0]
        )
        for k in range(2):
            front[run, k] = elec[k]
        elec = row(0, 2, 3)
        yz = magnetic_yz(row(4, 2, 2), elec, arrived(next_c, has_next, 6))
        source = source_of(run, STEPS - 1, given, ())
        elec = electric(elec, row(3, 2, 1) + yz, row(4, 1, 2), courant * inv[last], source)
        for k in range(3):
            back[run, k] = elec[k]
        for k in range(2):
            back_h[run, k] = yz[k]
        return carry

    lax.fori_loop(0, 2, one_run, 0)
    out = []
    for run, fields in enumerate((fwd_out, adj_out)):
        for part, (source, first, count, x) in enumerate(
            ((front, 1, 2, 0), (back, 0, 3, last), (back_h, 4, 2, last))
        ):
            out.append(
                pltpu.make_async_copy(
                    source.at[run],
                    fields.at[0, pl.ds(first, count), x],
                    sems.at[3 * run + part],
                )
            )
    start_all(out)

    def row_sum(pairs):
        total = pairs[0][0] * pairs[0][1]
        for first, second in pairs[1:]:
            total = total + first * second
        return jnp.sum(total, axis=0, keepdims=True)

    head = row_sum([(kept[0, 0, 0], kept[1, 0, 0])] + [(front[0, k], front[1, k]) for k in range(2)])
    tail = row_sum([(back[0, k], back[1, k]) for k in range(3)])
    at = lax.broadcasted_iota(jnp.int32, summed.shape, 0)
    full = summed[...] + jnp.where(at == 0, head, 0.0) + jnp.where(at == last, tail, 0.0)
    slabs, width = blocks.shape[1], blocks.shape[3]
    for k in range(slabs):
        turned = pltpu.roll(full, (RMAX - k * (NY // slabs)) % NY, 1)
        for f in range(blocks.shape[0]):
            blocks[f, k] = turned[:, :width]
    wait_all(out)


def moved(rows, by):
    if by == 0:
        return rows
    count = rows.shape[0]
    at = lax.broadcasted_iota(jnp.int32, rows.shape, 0)
    keep = at < count - by if by > 0 else at >= -by
    return jnp.where(keep, pltpu.roll(rows, (-by) % count, 0), 0.0)


def weighted(cells, radius):
    tile = cells.shape[1] - 2 * RMAX
    columns = [cells[:, RMAX : RMAX + tile]]
    for a in range(1, RMAX + 1):
        columns.append(
            cells[:, RMAX - a : RMAX - a + tile] + cells[:, RMAX + a : RMAX + a + tile]
        )
    rings = {}
    for a in range(RMAX + 1):
        for b in range(RMAX + 1):
            part = columns[a]
            if b > 0:
                part = moved(part, b) + moved(part, -b)
            square = a * a + b * b
            rings[square] = rings[square] + part if square in rings else part
    total = None
    for square, part in rings.items():
        term = jnp.maximum(radius - math.sqrt(square), 0.0) * part
        total = term if total is None else total + term
    return total


def by_tile(values, count):
    columns = count // values.shape[1]
    at = lax.broadcasted_iota(jnp.int32, (count, 1), 0) // columns
    spread = jnp.zeros((count, 1), jnp.float32)
    for k in range(values.shape[1]):
        spread = jnp.where(at == k, values[:, k : k + 1].astype(jnp.float32), spread)
    return spread


def filter_operands(
    prior_a, next_a, density, mask, radius_map, padded, chosen, weights, rows_of, marks_of
):
    tile_rows, width = density.shape
    reach = padded.shape[1]
    above, below = (ref[pl.ds(5 * NZ, EXTRA), :] for ref in (prior_a, next_a))
    rows_of[pl.ds(0, RMAX), :] = above[:RMAX, :width]
    rows_of[pl.ds(RMAX, tile_rows), :] = density[...]
    rows_of[pl.ds(RMAX + tile_rows, RMAX), :] = below[:RMAX, :width]
    marks_of[...] = jnp.zeros_like(marks_of)
    marks_of[pl.ds(0, 1), :] = above[RMAX : RMAX + 1, :width]
    marks_of[pl.ds(1, 1), :] = below[RMAX : RMAX + 1, :width]
    sides = marks_of[...].T
    first = lax.axis_index("slab") * tile_rows - RMAX
    at = lax.broadcasted_iota(jnp.int32, (width, reach), 1)
    inside = (at + first >= 0) & (at + first < NY)
    padded[...] = jnp.where(inside, rows_of[...].T, 0.0)
    mark = jnp.where(
        at < RMAX,
        sides[:, 0:1],
        jnp.where(at < RMAX + tile_rows, by_tile(mask, width), sides[:, 1:2]),
    )
    scale = step_size / math.sqrt(3 * STEPS * NZ * FREQS)
    chosen[...] = jnp.where(inside, scale * mark, 0.0)
    weights[...] = weighted(inside.astype(jnp.float32), by_tile(radius_map, width))


def project(blocks, padded, chosen, weights, radius_map, projected):
    freqs, slabs, rows, width = blocks.shape
    gradient = jnp.sum(blocks[...], axis=0).reshape(slabs * rows, width)
    updated = padded[...] + chosen[...] * gradient
    numerator = weighted(updated, by_tile(radius_map, slabs * rows))
    filtered = numerator / weights[...]
    base = math.tanh(sharpness * midpoint)
    value = (base + jnp.tanh(sharpness * (filtered - midpoint))) / (
        base + math.tanh(sharpness * (1.0 - midpoint))
    )
    projected[...] = value.T


def around(shard, axis, by):
    count = lax.axis_size(axis)
    return lax.ppermute(shard, axis, [(i, (i + by) % count) for i in range(count)])


def on_device(
    inverse_permittivity,
    forward_fields,
    adjoint_fields,
    source_wave,
    source_profile,
    adjoint_wave,
    adjoint_profile,
    source_plane,
    monitor_plane,
    radius_map,
    design_mask,
    design_density,
):
    rows = forward_fields.shape[2]
    freqs, slabs = lax.axis_size("freq"), lax.axis_size("slab")
    tile_rows, width = design_density.shape
    reach = tile_rows + 2 * RMAX
    waves = (source_wave, adjoint_wave, source_profile, adjoint_profile)
    planes = (source_plane, monitor_plane)

    def pinned(arrays):
        return tuple(pltpu.with_memory_space_constraint(array, pltpu.HBM) for array in arrays)

    fields = pinned((forward_fields, adjoint_fields, inverse_permittivity))
    sources = pinned(waves) + planes
    dma = pltpu.SemaphoreType.DMA
    field_shape = shaped(*forward_fields.shape)
    state_shape = shaped(2, 6, rows, *PLANE)
    four = shaped(4 * NZ, NY)

    def vmem(*shape, kind=jnp.float32):
        return pltpu.VMEM(shape, kind)

    to_prior, to_next = kernel_call(
        first_planes,
        (shaped(SENT, NY), shaped(SENT, NY)),
        [HBM] * 5,
        (VMEM, VMEM),
        [
            vmem(2, 6, *PLANE),
            vmem(tile_rows, width),
            vmem(*design_mask.shape, kind=jnp.int32),
            dma((10,)),
        ],
        "first_planes",
    )(*fields, *pinned((design_density, design_mask)))
    prior_a = around(to_next, "slab", 1)
    next_a = around(to_prior, "slab", -1)
    to_prior, to_next, own, forward_part, adjoint_part, state, share = kernel_call(
        interior,
        (
            four,
            four,
            shaped(2, 9, *PLANE),
            field_shape,
            field_shape,
            state_shape,
            shaped(rows, 8, NY),
        ),
        [HBM] * 3 + SOURCE_SPECS,
        (VMEM, VMEM, VMEM, HBM, HBM, VMEM, VMEM),
        [vmem(rows, *PLANE), dma((5,)), *SOURCE_SCRATCH],
        "interior",
        micros=8,
    )(*fields, *sources)
    prior_b = around(to_next, "slab", 1)
    next_b = around(to_prior, "slab", -1)
    to_prior, to_next, early, resp, ends = kernel_call(
        step_one,
        (four, four, shaped(2, 6, 2, *PLANE), shaped(2, 8, *PLANE), shaped(2, 8, NY)),
        [VMEM] + SOURCE_VALUES + [VMEM] * 4,
        (VMEM,) * 5,
        [],
        "step_one",
        micros=3,
    )(inverse_permittivity, *waves, *planes, state, own, prior_a, next_a)
    prior_c = around(to_next, "slab", 1)
    next_c = around(to_prior, "slab", -1)
    padded, chosen, weights = kernel_call(
        filter_operands,
        (shaped(width, reach), shaped(width, reach), shaped(width, tile_rows)),
        [VMEM] * 5,
        (VMEM,) * 3,
        [vmem(reach, width), vmem(8, width)],
        "filter_operands",
    )(prior_a, next_a, design_density, design_mask, radius_map)
    forward_part, adjoint_part, kept, summed, waiting = kernel_call(
        borders,
        (
            field_shape,
            field_shape,
            shaped(2, 6, 3, *PLANE),
            shaped(rows, NY),
            shaped(2, 8, *PLANE),
        ),
        [HBM] * 2 + [VMEM] + SOURCE_VALUES + [VMEM] * 9,
        (HBM, HBM, VMEM, VMEM, VMEM),
        [
            vmem(2, 6, 3, *PLANE),
            vmem(2, 8, *PLANE),
            vmem(rows, 8, NY),
            dma((14,)),
        ],
        "borders",
        micros=3,
        input_output_aliases={0: 0, 1: 1},
    )(
        forward_part, adjoint_part, inverse_permittivity, *waves, *planes, state, early, resp,
        share, ends, prior_a, next_a, prior_b, next_b,
    )
    forward_out, adjoint_out, blocks = kernel_call(
        last_planes,
        (field_shape, field_shape, shaped(freqs, slabs, rows, reach)),
        [HBM] * 2 + [VMEM] + SOURCE_VALUES + [VMEM] * 5,
        (HBM, HBM, VMEM),
        [
            vmem(2, 2, *PLANE),
            vmem(2, 3, *PLANE),
            vmem(2, 2, *PLANE),
            dma((6,)),
        ],
        "last_planes",
        micros=2,
        input_output_aliases={0: 0, 1: 1},
    )(
        forward_part, adjoint_part, inverse_permittivity, *waves, *planes,
        kept, summed, waiting, prior_c, next_c,
    )

    blocks = blocks.reshape(freqs * slabs, rows, reach)
    blocks = lax.all_to_all(blocks, ("freq", "slab"), 0, 0, tiled=True)
    blocks = blocks.reshape(freqs, slabs, rows, reach)
    projected = kernel_call(
        project,
        shaped(tile_rows, width),
        [VMEM] * 5,
        VMEM,
        [],
        "project",
    )(blocks, padded, chosen, weights, radius_map)
    return (forward_out, adjoint_out, projected)


def solution(mesh):
    return jax.shard_map(
        on_device,
        mesh=mesh,
        in_specs=(
            P("slab", None, None),
            P("freq", None, "slab", None, None),
            P("freq", None, "slab", None, None),
            P("freq", None),
            P("freq", None),
            P("freq", None),
            P("freq", None),
            P("freq"),
            P("freq"),
            P("slab", None),
            P("slab", None),
            P("slab", None),
        ),
        out_specs=(
            P("freq", None, "slab", None, None),
            P("freq", None, "slab", None, None),
            P("slab", None),
        ),
        check_vma=False,
    )
```

```python
import math

import jax
import jax.numpy as jnp
from jax import lax
from jax.experimental import pallas as pl
from jax.experimental.pallas import tpu as pltpu
from jax.sharding import PartitionSpec as P

NY = 512
NZ = 24
FREQS = 4
STEPS = 3
RMAX = 4


courant = 0.5
sharpness = 4.0
midpoint = 0.5
step_size = 0.3

PLANE = (NZ, NY)
VMEM = pl.BlockSpec(memory_space=pltpu.VMEM)
HBM = pl.BlockSpec(memory_space=pltpu.HBM)
ANY = pl.BlockSpec(memory_space=pl.ANY)
GRANT = 8 * 1024 * 1024
HALF = NZ // 2
HALO = 4 * NZ + HALF


def mark_at(width):
    return (HALO, width) if 2 * width <= NY else (HALO + RMAX, 0)


def sent_rows(width):
    return -(-(max(HALO + RMAX, mark_at(width)[0] + 1)) // 8) * 8


def second_core():
    return lax.rem(lax.axis_index("freq"), 2) == 1


def neighbour(plane, axis, by):
    size = (8, 128)[axis]
    count = plane.shape[axis] // size
    tiles = [lax.slice_in_dim(plane, k * size, (k + 1) * size, axis=axis) for k in range(count)]
    turned = [pltpu.roll(tile, (-by) % size, axis) for tile in tiles]
    at = lax.broadcasted_iota(jnp.int32, tiles[0].shape, axis)
    edge = at == (size - 1 if by > 0 else 0)
    out = []
    for k in range(count):
        other = turned[k + by] if 0 <= k + by < count else 0.0
        out.append(jnp.where(edge, other, turned[k]))
    return jnp.concatenate(out, axis=axis)


def ahead(plane, axis):
    return neighbour(plane, axis, 1)


def behind(plane, axis):
    return neighbour(plane, axis, -1)


def dy_f(plane):
    return ahead(plane, 1) - plane


def dz_f(plane):
    return ahead(plane, 0) - plane


def dy_b(plane):
    return plane - behind(plane, 1)


def dz_b(plane):
    return plane - behind(plane, 0)


def magnetic_x(magn_x, elec):
    return magn_x - courant * (dy_f(elec[2]) - dz_f(elec[1]))


def magnetic_yz(magn, elec, following):
    next_y, next_z = (0.0, 0.0) if following is None else following
    return (
        magn[0] - courant * (dz_f(elec[0]) - (next_z - elec[2])),
        magn[1] - courant * ((next_y - elec[1]) - dy_f(elec[0])),
    )


def magnetic(magn, elec, following):
    return (magnetic_x(magn[0], elec),) + magnetic_yz(magn[1:], elec, following)


def electric_x(elec_x, magn, scaled):
    return elec_x + scaled * (dy_b(magn[2]) - dz_b(magn[1]))


def electric_yz(elec, magn, prior, scaled):
    prior_y, prior_z = (0.0, 0.0) if prior is None else prior
    return (
        elec[0] + scaled * (dz_b(magn[0]) - (magn[2] - prior_z)),
        elec[1] + scaled * ((magn[1] - prior_y) - dy_b(magn[0])),
    )


def electric(elec, magn, prior, scaled, source):
    return (electric_x(elec[0], magn, scaled) + source,) + electric_yz(
        elec[1:], magn, prior, scaled
    )


SOURCE_SCRATCH = [
    pltpu.VMEM((2, 1, STEPS), jnp.float32),
    pltpu.VMEM((2, 1, NY), jnp.float32),
    pltpu.SemaphoreType.DMA((4,)),
]
SOURCE_SPECS = [HBM] * 4 + [VMEM] * 2
SOURCE_VALUES = [VMEM] * 6


def source_copies(given, scratch):
    wave, profile, sems = scratch
    return [
        pltpu.make_async_copy(given[2 * k + run], ref.at[run], sems.at[2 * k + run])
        for k, ref in enumerate((wave, profile))
        for run in range(2)
    ]


def source_of(run, turn, given, scratch):
    if scratch:
        wave, profile = scratch[0][run], scratch[1][run]
    else:
        wave, profile = (jnp.where(run == 0, given[k][...], given[k + 1][...]) for k in (0, 2))
    row = wave[:, turn : turn + 1] * profile
    plane = jnp.where(run == 0, *(given[k][...].reshape(1, 1) for k in (4, 5)))
    at = lax.broadcasted_iota(jnp.int32, PLANE, 0)
    return jnp.where(at == plane, row, 0.0)


def kernel_call(body, out_shape, in_specs, out_specs, scratch, name, micros=1, grant=GRANT, **more):
    return pl.pallas_call(
        body,
        out_shape=out_shape,
        in_specs=in_specs,
        out_specs=out_specs,
        scratch_shapes=scratch,
        compiler_params=pltpu.CompilerParams(vmem_limit_bytes=grant),
        cost_estimate=pl.CostEstimate(
            flops=micros * 10**9, bytes_accessed=0, transcendentals=0
        ),
        name=name,
        **more,
    )


def shaped(*shape):
    return jax.ShapeDtypeStruct(shape, jnp.float32)


def start_all(copies):
    for copy in copies:
        copy.start()


def wait_all(copies):
    for copy in copies:
        copy.wait()


def plane_at(index):
    return pl.ds(pl.multiple_of(index * NZ, 8), NZ)


def first_planes(
    fwd, adj, inverse, density, mask, to_prior, to_next, rows_in, inv, cells, chosen, sems
):
    rows = inverse.shape[0]
    width = density.shape[1]
    copies = [
        pltpu.make_async_copy(fwd.at[0, :, rows - 1], rows_in.at[0], sems.at[0]),
        pltpu.make_async_copy(adj.at[0, :, rows - 1], rows_in.at[1], sems.at[1]),
        pltpu.make_async_copy(density, cells, sems.at[2]),
        pltpu.make_async_copy(mask, chosen, sems.at[3]),
        pltpu.make_async_copy(inverse.at[0], inv.at[0], sems.at[4]),
        pltpu.make_async_copy(inverse.at[rows - 1], inv.at[1], sems.at[5]),
    ]
    for run, fields in enumerate((fwd, adj)):
        for k in range(2):
            at = 2 * run + k
            copies.append(
                pltpu.make_async_copy(
                    fields.at[0, 1 + k, 0], to_prior.at[plane_at(at)], sems.at[6 + at]
                )
            )
    start_all(copies)
    wait_all(copies[2:6])
    at = lax.broadcasted_iota(jnp.int32, (1, width), 1) // (width // mask.shape[1])
    spread = jnp.zeros((1, width), jnp.float32)
    for k in range(mask.shape[1]):
        spread = jnp.where(at == k, chosen[:, k : k + 1].astype(jnp.float32), spread)
    mark_row, mark_lane = mark_at(width)
    tail = to_next.shape[0] - HALO
    for side, (sent, first) in enumerate(((to_prior, 0), (to_next, density.shape[0] - RMAX))):
        half = jnp.where(second_core(), inv[side, HALF:, :], inv[side, :HALF, :])
        sent[pl.ds(4 * NZ, HALF), :] = half
        sent[pl.ds(HALO, tail), :] = jnp.zeros((tail, NY), jnp.float32)
        sent[pl.ds(HALO, RMAX), pl.ds(0, width)] = cells[pl.ds(first, RMAX), :]
        sent[pl.ds(mark_row, 1), pl.ds(mark_lane, width)] = spread
    for run in range(2):
        copies[run].wait()
        planes = [rows_in[run, k] for k in range(6)]
        magn = magnetic_yz(planes[4:], planes[:3], None)
        for k in range(2):
            to_next[plane_at(2 * run + k), :] = magn[k]
    wait_all(copies[6:])


def second_planes(fwd, adj, inverse, *rest):
    given, (_, to_prior, to_next, own, head, tail, inv, sems, *scratch) = rest[:6], rest[6:]
    rows = inverse.shape[0]
    small = source_copies(given, scratch) + [
        pltpu.make_async_copy(inverse.at[0], inv.at[0], sems.at[4]),
        pltpu.make_async_copy(inverse.at[rows - 1], inv.at[1], sems.at[5]),
    ]

    def ends(fields, run):
        return [
            pltpu.make_async_copy(fields.at[0, :, pl.ds(0, 2)], head.at[run], sems.at[2 * run]),
            pltpu.make_async_copy(
                fields.at[0, :, pl.ds(rows - 2, 2)], tail.at[run], sems.at[2 * run + 1]
            ),
        ]

    start_all(ends(fwd, 0) + small + ends(adj, 1))
    wait_all(small)

    def one_run(run, carry):
        wait_all(ends(fwd, run))

        def row(ref, x):
            return tuple(
                tuple(ref[run, k, x] for k in range(first, first + 3)) for first in (0, 3)
            )

        source = source_of(run, 0, given, scratch)
        elec, magn = row(head, 0)
        magn = magnetic(magn, elec, (head[run, 1, 1], head[run, 2, 1]))
        elec = electric(elec, magn, None, courant * inv[0], source)
        for k in range(2):
            to_prior[plane_at(2 * run + k), :] = elec[1 + k]
        for k in range(3):
            own[run, k] = elec[k]
        (elec_6, magn_6), (elec, magn) = row(tail, 0), row(tail, 1)
        yz_6 = magnetic_yz(magn_6[1:], elec_6, elec[1:])
        magn = magnetic(magn, elec, None)
        elec = electric(elec, magn, yz_6, courant * inv[1], source)
        magn = magnetic(magn, elec, None)
        for k in range(2):
            to_next[plane_at(2 * run + k), :] = magn[1 + k]
        for k in range(3):
            own[run, 3 + k] = elec[k]
            own[run, 6 + k] = magn[k]
        return carry

    lax.fori_loop(0, 2, one_run, 0)


class State:
    def __init__(self, given, home, written):
        self.given, self.home = given, home
        self.written = None if given is None else set(written)

    def load(self, run, first, x, count=3):
        parts = []
        for k in range(first, first + count):
            at_home = self.written is None or (k, x) in self.written
            ref, at = (self.home if at_home else self.given)(k, x)
            parts.append(ref[run, k, at])
        return tuple(parts)

    def store(self, run, first, x, planes):
        for k, value in enumerate(planes):
            ref, at = self.home(first + k, x)
            ref[run, first + k, at] = value
            if self.written is not None:
                self.written.add((first + k, x))

    def magnetic(self, run, x, following):
        magn = magnetic(self.load(run, 3, x), self.load(run, 0, x), following)
        self.store(run, 3, x, magn)
        return magn

    def electric(self, run, x, prior, scaled, source):
        elec = electric(self.load(run, 0, x), self.load(run, 3, x), prior, scaled, source)
        self.store(run, 0, x, elec)

    def electric_yz(self, run, x):
        return self.load(run, 1, x, 2)

    def magnetic_yz(self, run, x):
        return self.load(run, 4, x, 2)


def in_place(ref):
    return State(None, lambda k, x: (ref, x), ())


def products(ref, x):
    total = ref[0, 0, x] * ref[1, 0, x]
    for k in (1, 2):
        total = total + ref[0, k, x] * ref[1, k, x]
    return jnp.sum(total.reshape(NZ // 8, 8, NY), axis=0)


def interior(fwd, adj, inverse, *rest):
    given, (_, state, share, inv, sems, *scratch) = rest[:6], rest[6:]
    rows = inverse.shape[0]
    last = rows - 1
    into = source_copies(given, scratch) + [pltpu.make_async_copy(inverse, inv, sems.at[4])]

    def load(fields, run):
        return pltpu.make_async_copy(fields.at[0], state.at[run], sems.at[run])

    start_all([load(fwd, 0)] + into + [load(adj, 1)])
    wait_all(into)
    rows_of = in_place(state)

    for turn in range(STEPS):

        def one_run(run, carry, turn=turn):
            if turn == 0:
                load(fwd, run).wait()
            source = source_of(run, turn, given, scratch)
            for x in range(turn, last - turn):
                rows_of.magnetic(run, x, rows_of.electric_yz(run, x + 1))
                if x > turn:
                    rows_of.electric(
                        run, x, rows_of.magnetic_yz(run, x - 1), courant * inv[x], source
                    )
            return carry

        lax.fori_loop(0, 2, one_run, 0)
        for x in range(turn + 1, last - turn):
            share[x] = products(state, x) + (share[x] if turn > 0 else 0.0)
    for x in (0, last):
        share[x] = jnp.zeros(share.shape[1:], jnp.float32)


def flags():
    slab = lax.axis_index("slab")
    has_prior = (slab > 0).astype(jnp.float32)
    has_next = (slab < lax.axis_size("slab") - 1).astype(jnp.float32)
    return has_prior, has_next


def write_copies(parts, fields, sems):
    return [
        pltpu.make_async_copy(
            ref.at[run, *(pl.ds(at, n) for at, n in zip(source, count))],
            fields[run].at[0, *(pl.ds(at, n) for at, n in zip(target, count))],
            sems.at[len(parts) * run + part],
        )
        for run in range(2)
        for part, (ref, source, count, target) in enumerate(parts)
    ]


def respond(before, early, own, other, resp, scaled):
    second = second_core()
    for side, flag in enumerate(flags()):
        mine, theirs = (ref[pl.ds(side * HALF, HALF), :] for ref in (own, other))
        scaled[side, pl.ds(0, HALF), :] = courant * flag * jnp.where(second, theirs, mine)
        scaled[side, pl.ds(HALF, HALF), :] = courant * flag * jnp.where(second, mine, theirs)
    flagged = courant * flags()[0]

    def one_run(run, carry):
        magn_y, magn_z = flagged * before[run, 2, 0], -flagged * before[run, 1, 0]
        resp[run, 0] = scaled[0] * (dy_b(magn_z) - dz_b(magn_y))
        resp[run, 1] = -scaled[0] * magn_z
        resp[run, 2] = scaled[0] * magn_y
        resp[run, 3] = jnp.zeros(PLANE, jnp.float32)
        resp[run, 4] = magn_y
        resp[run, 5] = magn_z
        resp[run, 6] = scaled[1] * early[run, 5, 1]
        resp[run, 7] = -scaled[1] * early[run, 4, 1]
        return carry

    lax.fori_loop(0, 2, one_run, 0)


def border_rows(run, turn, state, source, inv, here, resp_in=None, resp_out=None, scaled=None):
    has_prior, has_next = flags()
    flagged = courant * has_prior
    last = inv.shape[0] - 1
    whole = here is not None

    def received(ref):
        return tuple(ref[plane_at(2 * run + k), :] for k in range(2))

    own_y, own_z = state.electric_yz(run, 0)
    if turn == 0:
        magn_r = (None, flagged * own_z, -flagged * own_y)
    else:
        elec_r = tuple(resp_in[run, k] for k in range(3))
        old = tuple(resp_in[run, k] for k in range(3, 6))
        magn_r = (
            old[0] - courant * (dy_f(elec_r[2]) - dz_f(elec_r[1])),
            old[1] - courant * (dz_f(elec_r[0]) + elec_r[2]) + flagged * own_z,
            old[2] + courant * (elec_r[1] + dy_f(elec_r[0])) - flagged * own_y,
        )
        if whole:
            resp_out[run, 0] = elec_r[0] + scaled[0] * (dy_b(magn_r[2]) - dz_b(magn_r[1]))
            resp_out[run, 1] = elec_r[1] + scaled[0] * (
                dz_b(magn_r[0]) - (magn_r[2] + courant * elec_r[1])
            )
            resp_out[run, 2] = elec_r[2] + scaled[0] * (
                (magn_r[1] - courant * elec_r[2]) - dy_b(magn_r[0])
            )
            resp_out[run, 3] = magn_r[0]
        resp_out[run, 4] = magn_r[1]
        resp_out[run, 5] = magn_r[2]
    for x in range(turn):
        state.magnetic(run, x, state.electric_yz(run, x + 1))
    if whole:
        arrived = received(here[0])
        prior = tuple(has_prior * arrived[k] + magn_r[1 + k] for k in range(2))
        state.electric(run, 0, prior, courant * inv[0], source)
    else:
        elec_x = electric_x(state.load(run, 0, 0, 1)[0], state.load(run, 3, 0), courant * inv[0])
        state.store(run, 0, 0, (elec_x + source,))
    for x in range(1, turn + 1):
        state.electric(run, x, state.magnetic_yz(run, x - 1), courant * inv[x], source)
    for x in range(last - turn, last):
        state.magnetic(run, x, state.electric_yz(run, x + 1))
    if whole:
        arrived = received(here[1])
        following = tuple(has_next * plane for plane in arrived)
        if turn > 0:
            following = tuple(following[k] + resp_in[run, 6 + k] for k in range(2))
        magn = state.magnetic(run, last, following)
    else:
        magn_x = magnetic_x(state.load(run, 3, last, 1)[0], state.load(run, 0, last))
        state.store(run, 3, last, (magn_x,))
    for x in range(last - turn, last + (1 if whole else 0)):
        state.electric(run, x, state.magnetic_yz(run, x - 1), courant * inv[x], source)
    if turn > 0 and whole:
        elec_y, elec_z = resp_in[run, 6], resp_in[run, 7]
        magn_x = -courant * (dy_f(elec_z) - dz_f(elec_y))
        resp_out[run, 6] = elec_y + scaled[1] * (dz_b(magn_x) - (courant * elec_y - magn[2]))
        resp_out[run, 7] = elec_z + scaled[1] * ((-courant * elec_z - magn[1]) - dy_b(magn_x))
    elif turn > 0:
        resp_out[run, 6] = resp_in[run, 6]
        resp_out[run, 7] = resp_in[run, 7]


def third_planes(inv, *rest):
    given, (before, own, to_prior, to_next) = rest[:6], rest[6:]
    last = inv.shape[0] - 1

    def one_run(run, carry):
        state = State(lambda k, x: (before, x), None, ())
        elec = tuple(own[run, k] for k in range(3))
        magn = magnetic(state.load(run, 3, 0), elec, state.electric_yz(run, 1))
        sent = electric_yz(elec[1:], magn, None, courant * inv[0])
        for k in range(2):
            to_prior[plane_at(2 * run + k), :] = sent[k]
        elec = tuple(own[run, 3 + k] for k in range(3))
        magn = tuple(own[run, 6 + k] for k in range(3))
        yz = magnetic_yz(
            state.magnetic_yz(run, last - 1), state.load(run, 0, last - 1), elec[1:]
        )
        elec = electric(elec, magn, yz, courant * inv[last], source_of(run, 1, given, ()))
        sent = magnetic_yz(magn[1:], elec, None)
        for k in range(2):
            to_next[plane_at(2 * run + k), :] = sent[k]
        return carry

    lax.fori_loop(0, 2, one_run, 0)


def step_one(inv, *rest):
    given, (before, prior_a, next_a, early, halves, share) = rest[:6], rest[6:]
    for side, ref in enumerate((prior_a, next_a)):
        halves[pl.ds(side * HALF, HALF), :] = ref[pl.ds(4 * NZ, HALF), :]

    def one_run(run, carry):
        state = State(lambda k, x: (before, x), lambda k, x: (early, min(x, 1)), ())
        border_rows(run, 0, state, source_of(run, 0, given, ()), inv, (prior_a, next_a))
        return carry

    lax.fori_loop(0, 2, one_run, 0)
    for side in range(2):
        share[side] = products(early, side)


def borders(inv, *rest):
    given, (before, early, resp_in, scaled, share, ends, prior_b, next_b) = rest[:6], rest[6:14]
    kept, inner, summed, waiting, fwd_out, adj_out, resp, total, sems = rest[14:]
    rows = inv.shape[0]
    last = rows - 1
    inside = rows - 2 * STEPS
    out = write_copies(
        (
            (before, (0, STEPS), (3, inside), (0, STEPS)),
            (before, (3, STEPS - 1), (3, inside + 1), (3, STEPS - 1)),
        ),
        (fwd_out, adj_out),
        sems,
    )
    start_all(out)
    homes = {0: (kept, 0), last - 1: (kept, 1), last: (kept, 2)}
    homes |= {1: (inner, 0), 2: (inner, 1), last - 2: (inner, 2)}

    def handed_in(k, x):
        if x == last or (x == 0 and k < 3):
            return (early, min(x, 1))
        return (before, x)

    written = set()
    for turn in range(1, STEPS):
        whole = turn < STEPS - 1
        seen = []

        def one_run(run, carry, turn=turn, whole=whole, seen=seen):
            state = State(handed_in, lambda k, x: homes[x], written)
            border_rows(
                run, turn, state, source_of(run, turn, given, ()), inv,
                (prior_b, next_b) if whole else None,
                resp_in if turn == 1 else resp, resp if whole else waiting, scaled,
            )
            seen[:] = [state.written]
            return carry

        lax.fori_loop(0, 2, one_run, 0)
        written = seen[0]
        reached = list(range(turn + 1)) + list(range(last - turn, last + 1))
        for x in reached if whole else reached[1:-1]:
            if turn > 1 and min(x, last - x) < turn:
                so_far = total[x]
            else:
                so_far = ends[min(x, 1)] if x in (0, last) else share[x]
            total[x] = so_far + products(*homes[x])
    for x in range(STEPS, rows - STEPS):
        total[x] = share[x]
    summed[...] = jnp.sum(total[...], axis=1)
    wait_all(out)


def last_planes(inv, *rest):
    given, (kept, summed, waiting, prior_c, next_c, _, blocks, ends) = rest[:6], rest[6:]
    last = inv.shape[0] - 1
    has_prior, has_next = flags()

    def one_run(run, carry):
        def row(first, slot, count):
            return tuple(kept[run, first + k, slot] for k in range(count))

        def arrived(ref, flag, first):
            return tuple(
                flag * ref[plane_at(2 * run + k), :] + waiting[run, first + k] for k in range(2)
            )

        elec = electric_yz(
            row(1, 0, 2), row(3, 0, 3), arrived(prior_c, has_prior, 4), courant * inv[0]
        )
        for k in range(2):
            ends[run, k, 0] = elec[k]
        elec = row(0, 2, 3)
        yz = magnetic_yz(row(4, 2, 2), elec, arrived(next_c, has_next, 6))
        source = source_of(run, STEPS - 1, given, ())
        elec = electric(elec, row(3, 2, 1) + yz, row(4, 1, 2), courant * inv[last], source)
        for k in range(3):
            ends[run, 2 + k, 0] = elec[k]
        for k in range(2):
            ends[run, 5 + k, 0] = yz[k]
        return carry

    lax.fori_loop(0, 2, one_run, 0)

    def row_sum(pairs):
        total = pairs[0][0] * pairs[0][1]
        for first, second in pairs[1:]:
            total = total + first * second
        return jnp.sum(total, axis=0, keepdims=True)

    head = row_sum(
        [(kept[0, 0, 0], kept[1, 0, 0])] + [(ends[0, k, 0], ends[1, k, 0]) for k in range(2)]
    )
    tail = row_sum([(ends[0, 2 + k, 0], ends[1, 2 + k, 0]) for k in range(3)])
    at = lax.broadcasted_iota(jnp.int32, summed.shape, 0)
    full = summed[...] + jnp.where(at == 0, head, 0.0) + jnp.where(at == last, tail, 0.0)
    slabs, width = blocks.shape[1], blocks.shape[3]
    for k in range(slabs):
        turned = pltpu.roll(full, (RMAX - k * (NY // slabs)) % NY, 1)
        for f in range(blocks.shape[0]):
            blocks[f, k] = turned[:, :width]


def write_borders(fwd, adj, kept, inner, fwd_out, adj_out, done, sems):
    last = fwd.shape[2] - 1
    done[...] = jnp.zeros_like(done)
    out = write_copies(
        (
            (inner, (0, 0), (6, 1), (0, 1)),
            (inner, (0, 1), (3, 1), (0, 2)),
            (inner, (0, 2), (6, 1), (0, last - 2)),
            (kept, (0, 1), (6, 1), (0, last - 1)),
            (kept, (0, 0), (1, 1), (0, 0)),
            (kept, (3, 0), (3, 1), (3, 0)),
            (kept, (3, 2), (1, 1), (3, last)),
        ),
        (fwd_out, adj_out),
        sems,
    )
    start_all(out)
    wait_all(out)


def write_ends(fwd, adj, ends, fwd_out, adj_out, sems):
    last = fwd.shape[2] - 1
    out = write_copies(
        (
            (ends, (0, 0), (2, 1), (1, 0)),
            (ends, (2, 0), (3, 1), (0, last)),
            (ends, (5, 0), (2, 1), (4, last)),
        ),
        (fwd_out, adj_out),
        sems,
    )
    start_all(out)
    wait_all(out)


def moved(rows, by):
    if by == 0:
        return rows
    count = rows.shape[0]
    at = lax.broadcasted_iota(jnp.int32, rows.shape, 0)
    keep = at < count - by if by > 0 else at >= -by
    return jnp.where(keep, pltpu.roll(rows, (-by) % count, 0), 0.0)


def weighted(cells, radius):
    tile = cells.shape[1] - 2 * RMAX
    columns = [cells[:, RMAX : RMAX + tile]]
    for a in range(1, RMAX + 1):
        columns.append(
            cells[:, RMAX - a : RMAX - a + tile] + cells[:, RMAX + a : RMAX + a + tile]
        )
    rings = {}
    for a in range(RMAX + 1):
        for b in range(RMAX + 1):
            part = columns[a]
            if b > 0:
                part = moved(part, b) + moved(part, -b)
            square = a * a + b * b
            rings[square] = rings[square] + part if square in rings else part
    total = None
    for square, part in rings.items():
        term = jnp.maximum(radius - math.sqrt(square), 0.0) * part
        total = term if total is None else total + term
    return total


def by_tile(values, count):
    columns = count // values.shape[1]
    at = lax.broadcasted_iota(jnp.int32, (count, 1), 0) // columns
    spread = jnp.zeros((count, 1), jnp.float32)
    for k in range(values.shape[1]):
        spread = jnp.where(at == k, values[:, k : k + 1].astype(jnp.float32), spread)
    return spread


def filter_operands(
    prior_a, next_a, density, mask, radius_map, padded, chosen, weights, rows_of, marks_of
):
    tile_rows, width = density.shape
    reach = padded.shape[1]
    above, below = (ref[pl.ds(HALO, RMAX), :] for ref in (prior_a, next_a))
    mark_row, mark_lane = mark_at(width)
    rows_of[pl.ds(0, RMAX), :] = above[:, :width]
    rows_of[pl.ds(RMAX, tile_rows), :] = density[...]
    rows_of[pl.ds(RMAX + tile_rows, RMAX), :] = below[:, :width]
    marks_of[...] = jnp.zeros_like(marks_of)
    for side, ref in enumerate((prior_a, next_a)):
        marks_of[pl.ds(side, 1), :] = ref[pl.ds(mark_row, 1), pl.ds(mark_lane, width)]
    sides = marks_of[...].T
    first = lax.axis_index("slab") * tile_rows - RMAX
    at = lax.broadcasted_iota(jnp.int32, (width, reach), 1)
    inside = (at + first >= 0) & (at + first < NY)
    padded[...] = jnp.where(inside, rows_of[...].T, 0.0)
    mark = jnp.where(
        at < RMAX,
        sides[:, 0:1],
        jnp.where(at < RMAX + tile_rows, by_tile(mask, width), sides[:, 1:2]),
    )
    scale = step_size / math.sqrt(3 * STEPS * NZ * FREQS)
    chosen[...] = jnp.where(inside, scale * mark, 0.0)
    weights[...] = weighted(inside.astype(jnp.float32), by_tile(radius_map, width))


def project(blocks, padded, chosen, weights, radius_map, projected):
    freqs, slabs, rows, width = blocks.shape
    gradient = jnp.sum(blocks[...], axis=0).reshape(slabs * rows, width)
    updated = padded[...] + chosen[...] * gradient
    numerator = weighted(updated, by_tile(radius_map, slabs * rows))
    filtered = numerator / weights[...]
    base = math.tanh(sharpness * midpoint)
    value = (base + jnp.tanh(sharpness * (filtered - midpoint))) / (
        base + math.tanh(sharpness * (1.0 - midpoint))
    )
    projected[...] = value.T


def around(shard, axis, by):
    count = lax.axis_size(axis)
    return lax.ppermute(shard, axis, [(i, (i + by) % count) for i in range(count)])


def on_device(
    inverse_permittivity,
    forward_fields,
    adjoint_fields,
    source_wave,
    source_profile,
    adjoint_wave,
    adjoint_profile,
    source_plane,
    monitor_plane,
    radius_map,
    design_mask,
    design_density,
):
    rows = forward_fields.shape[2]
    freqs, slabs = lax.axis_size("freq"), lax.axis_size("slab")
    tile_rows, width = design_density.shape
    reach = tile_rows + 2 * RMAX
    waves = (source_wave, adjoint_wave, source_profile, adjoint_profile)
    planes = (source_plane, monitor_plane)

    def pinned(arrays):
        return tuple(pltpu.with_memory_space_constraint(array, pltpu.HBM) for array in arrays)

    fields = pinned((forward_fields, adjoint_fields, inverse_permittivity))
    sources = pinned(waves) + planes
    dma = pltpu.SemaphoreType.DMA
    field_shape = shaped(*forward_fields.shape)
    state_shape = shaped(2, 6, rows, *PLANE)
    four = shaped(4 * NZ, NY)

    def vmem(*shape, kind=jnp.float32):
        return pltpu.VMEM(shape, kind)

    to_prior, to_next = kernel_call(
        first_planes,
        (shaped(sent_rows(width), NY),) * 2,
        [HBM] * 5,
        (VMEM, VMEM),
        [
            vmem(2, 6, *PLANE),
            vmem(2, *PLANE),
            vmem(tile_rows, width),
            vmem(*design_mask.shape, kind=jnp.int32),
            dma((10,)),
        ],
        "first_planes",
    )(*fields, *pinned((design_density, design_mask)))
    prior_a = around(to_next, "slab", 1)
    next_a = around(to_prior, "slab", -1)
    to_prior, to_next, own = kernel_call(
        second_planes,
        (four, four, shaped(2, 9, *PLANE)),
        [HBM] * 3 + SOURCE_SPECS + [ANY],
        (VMEM,) * 3,
        [
            vmem(2, 6, 2, *PLANE),
            vmem(2, 6, 2, *PLANE),
            vmem(2, *PLANE),
            dma((6,)),
            *SOURCE_SCRATCH,
        ],
        "second_planes",
        micros=2,
    )(*fields, *sources, to_prior)
    prior_b = around(to_next, "slab", 1)
    next_b = around(to_prior, "slab", -1)
    state, share = kernel_call(
        interior,
        (state_shape, shaped(rows, 8, NY)),
        [HBM] * 3 + SOURCE_SPECS + [ANY],
        (VMEM, VMEM),
        [vmem(rows, *PLANE), dma((5,)), *SOURCE_SCRATCH],
        "interior",
        micros=8,
    )(*fields, *sources, own)
    to_prior, to_next = kernel_call(
        third_planes,
        (four, four),
        [VMEM] + SOURCE_VALUES + [VMEM] * 2,
        (VMEM,) * 2,
        [],
        "third_planes",
    )(inverse_permittivity, *waves, *planes, state, own)
    prior_c = around(to_next, "slab", 1)
    next_c = around(to_prior, "slab", -1)
    early, halves, ends = kernel_call(
        step_one,
        (shaped(2, 6, 2, *PLANE), shaped(*PLANE), shaped(2, 8, NY)),
        [VMEM] + SOURCE_VALUES + [VMEM] * 3,
        (VMEM,) * 3,
        [],
        "step_one",
        micros=0,
    )(inverse_permittivity, *waves, *planes, state, prior_a, next_a)
    other = lax.ppermute(halves, "freq", [(i, i ^ 1) for i in range(freqs)])
    resp, scaled = kernel_call(
        respond,
        (shaped(2, 8, *PLANE), shaped(2, *PLANE)),
        [VMEM] * 4,
        (VMEM,) * 2,
        [],
        "respond",
        micros=0,
    )(state, early, halves, other)
    padded, chosen, weights = kernel_call(
        filter_operands,
        (shaped(width, reach), shaped(width, reach), shaped(width, tile_rows)),
        [VMEM] * 5,
        (VMEM,) * 3,
        [vmem(reach, width), vmem(8, width)],
        "filter_operands",
        micros=0,
    )(prior_a, next_a, design_density, design_mask, radius_map)
    three = shaped(2, 6, 3, *PLANE)
    kept, inner, summed, waiting, forward_part, adjoint_part = kernel_call(
        borders,
        (three, three, shaped(rows, NY), shaped(2, 8, *PLANE), field_shape, field_shape),
        [VMEM] + SOURCE_VALUES + [VMEM] * 8,
        (VMEM,) * 4 + (HBM,) * 2,
        [vmem(2, 8, *PLANE), vmem(rows, 8, NY), dma((4,))],
        "borders",
        micros=0,
        grant=2 * GRANT,
    )(
        inverse_permittivity, *waves, *planes, state, early, resp, scaled, share, ends,
        prior_b, next_b,
    )
    forward_part, adjoint_part, done = kernel_call(
        write_borders,
        (field_shape, field_shape, shaped(8, 128)),
        [HBM] * 2 + [VMEM] * 2,
        (HBM, HBM, VMEM),
        [dma((14,))],
        "write_borders",
        input_output_aliases={0: 0, 1: 1},
    )(forward_part, adjoint_part, kept, inner)
    blocks, ends = kernel_call(
        last_planes,
        (shaped(freqs, slabs, rows, reach), shaped(2, 7, 1, *PLANE)),
        [VMEM] + SOURCE_VALUES + [VMEM] * 6,
        (VMEM, VMEM),
        [],
        "last_planes",
    )(inverse_permittivity, *waves, *planes, kept, summed, waiting, prior_c, next_c, done)
    forward_out, adjoint_out = kernel_call(
        write_ends,
        (field_shape, field_shape),
        [HBM] * 2 + [VMEM],
        (HBM, HBM),
        [dma((6,))],
        "write_ends",
        input_output_aliases={0: 0, 1: 1},
    )(forward_part, adjoint_part, ends)

    blocks = blocks.reshape(freqs * slabs, rows, reach)
    blocks = lax.all_to_all(blocks, ("freq", "slab"), 0, 0, tiled=True)
    blocks = blocks.reshape(freqs, slabs, rows, reach)
    projected = kernel_call(
        project,
        shaped(tile_rows, width),
        [VMEM] * 5,
        VMEM,
        [],
        "project",
    )(blocks, padded, chosen, weights, radius_map)
    return (forward_out, adjoint_out, projected)


def solution(mesh):
    return jax.shard_map(
        on_device,
        mesh=mesh,
        in_specs=(
            P("slab", None, None),
            P("freq", None, "slab", None, None),
            P("freq", None, "slab", None, None),
            P("freq", None),
            P("freq", None),
            P("freq", None),
            P("freq", None),
            P("freq"),
            P("freq"),
            P("slab", None),
            P("slab", None),
            P("slab", None),
        ),
        out_specs=(
            P("freq", None, "slab", None, None),
            P("freq", None, "slab", None, None),
            P("slab", None),
        ),
        check_vma=False,
    )
```

```python
import math

import jax
import jax.numpy as jnp
from jax import lax
from jax.experimental import pallas as pl
from jax.experimental.pallas import tpu as pltpu
from jax.sharding import PartitionSpec as P

NY = 512
NZ = 24
FREQS = 4
STEPS = 3
RMAX = 4


courant = 0.5
sharpness = 4.0
midpoint = 0.5
step_size = 0.3

PLANE = (NZ, NY)
VMEM = pl.BlockSpec(memory_space=pltpu.VMEM)
HBM = pl.BlockSpec(memory_space=pltpu.HBM)
ANY = pl.BlockSpec(memory_space=pl.ANY)
GRANT = 8 * 1024 * 1024
HALF = NZ // 2
HALO = 4 * NZ + HALF


def mark_at(width):
    return (HALO, width) if 2 * width <= NY else (HALO + RMAX, 0)


def sent_rows(width):
    return -(-(max(HALO + RMAX, mark_at(width)[0] + 1)) // 8) * 8


def second_core():
    return lax.rem(lax.axis_index("freq"), 2) == 1


def neighbour(plane, axis, by):
    size = (8, 128)[axis]
    count = plane.shape[axis] // size
    tiles = [lax.slice_in_dim(plane, k * size, (k + 1) * size, axis=axis) for k in range(count)]
    turned = [pltpu.roll(tile, (-by) % size, axis) for tile in tiles]
    at = lax.broadcasted_iota(jnp.int32, tiles[0].shape, axis)
    edge = at == (size - 1 if by > 0 else 0)
    out = []
    for k in range(count):
        other = turned[k + by] if 0 <= k + by < count else 0.0
        out.append(jnp.where(edge, other, turned[k]))
    return jnp.concatenate(out, axis=axis)


def ahead(plane, axis):
    return neighbour(plane, axis, 1)


def behind(plane, axis):
    return neighbour(plane, axis, -1)


def dy_f(plane):
    return ahead(plane, 1) - plane


def dz_f(plane):
    return ahead(plane, 0) - plane


def dy_b(plane):
    return plane - behind(plane, 1)


def dz_b(plane):
    return plane - behind(plane, 0)


def magnetic_x(magn_x, elec):
    return magn_x - courant * (dy_f(elec[2]) - dz_f(elec[1]))


def magnetic_yz(magn, elec, following):
    next_y, next_z = (0.0, 0.0) if following is None else following
    return (
        magn[0] - courant * (dz_f(elec[0]) - (next_z - elec[2])),
        magn[1] - courant * ((next_y - elec[1]) - dy_f(elec[0])),
    )


def magnetic(magn, elec, following):
    return (magnetic_x(magn[0], elec),) + magnetic_yz(magn[1:], elec, following)


def electric_x(elec_x, magn, scaled):
    return elec_x + scaled * (dy_b(magn[2]) - dz_b(magn[1]))


def electric_yz(elec, magn, prior, scaled):
    prior_y, prior_z = (0.0, 0.0) if prior is None else prior
    return (
        elec[0] + scaled * (dz_b(magn[0]) - (magn[2] - prior_z)),
        elec[1] + scaled * ((magn[1] - prior_y) - dy_b(magn[0])),
    )


def electric(elec, magn, prior, scaled, source):
    return (electric_x(elec[0], magn, scaled) + source,) + electric_yz(
        elec[1:], magn, prior, scaled
    )


SOURCE_SCRATCH = [
    pltpu.VMEM((2, 1, STEPS), jnp.float32),
    pltpu.VMEM((2, 1, NY), jnp.float32),
    pltpu.SemaphoreType.DMA((4,)),
]
SOURCE_SPECS = [HBM] * 4 + [VMEM] * 2
SOURCE_VALUES = [VMEM] * 6


def source_copies(given, scratch):
    wave, profile, sems = scratch
    return [
        pltpu.make_async_copy(given[2 * k + run], ref.at[run], sems.at[2 * k + run])
        for k, ref in enumerate((wave, profile))
        for run in range(2)
    ]


def source_of(run, turn, given, scratch):
    if scratch:
        wave, profile = scratch[0][run], scratch[1][run]
    else:
        wave, profile = (jnp.where(run == 0, given[k][...], given[k + 1][...]) for k in (0, 2))
    row = wave[:, turn : turn + 1] * profile
    plane = jnp.where(run == 0, *(given[k][...].reshape(1, 1) for k in (4, 5)))
    at = lax.broadcasted_iota(jnp.int32, PLANE, 0)
    return jnp.where(at == plane, row, 0.0)


def kernel_call(body, out_shape, in_specs, out_specs, scratch, name, micros=1, grant=GRANT, **more):
    return pl.pallas_call(
        body,
        out_shape=out_shape,
        in_specs=in_specs,
        out_specs=out_specs,
        scratch_shapes=scratch,
        compiler_params=pltpu.CompilerParams(vmem_limit_bytes=grant),
        cost_estimate=pl.CostEstimate(
            flops=micros * 10**9, bytes_accessed=0, transcendentals=0
        ),
        name=name,
        **more,
    )


def shaped(*shape):
    return jax.ShapeDtypeStruct(shape, jnp.float32)


def start_all(copies):
    for copy in copies:
        copy.start()


def wait_all(copies):
    for copy in copies:
        copy.wait()


def plane_at(index):
    return pl.ds(pl.multiple_of(index * NZ, 8), NZ)


def first_planes(
    fwd, adj, inverse, density, mask, to_prior, to_next, rows_in, inv, cells, chosen, sems
):
    rows = inverse.shape[0]
    width = density.shape[1]
    copies = [
        pltpu.make_async_copy(fwd.at[0, :, rows - 1], rows_in.at[0], sems.at[0]),
        pltpu.make_async_copy(adj.at[0, :, rows - 1], rows_in.at[1], sems.at[1]),
        pltpu.make_async_copy(density, cells, sems.at[2]),
        pltpu.make_async_copy(mask, chosen, sems.at[3]),
        pltpu.make_async_copy(inverse.at[0], inv.at[0], sems.at[4]),
        pltpu.make_async_copy(inverse.at[rows - 1], inv.at[1], sems.at[5]),
    ]
    for run, fields in enumerate((fwd, adj)):
        for k in range(2):
            at = 2 * run + k
            copies.append(
                pltpu.make_async_copy(
                    fields.at[0, 1 + k, 0], to_prior.at[plane_at(at)], sems.at[6 + at]
                )
            )
    start_all(copies)
    wait_all(copies[2:6])
    at = lax.broadcasted_iota(jnp.int32, (1, width), 1) // (width // mask.shape[1])
    spread = jnp.zeros((1, width), jnp.float32)
    for k in range(mask.shape[1]):
        spread = jnp.where(at == k, chosen[:, k : k + 1].astype(jnp.float32), spread)
    mark_row, mark_lane = mark_at(width)
    tail = to_next.shape[0] - HALO
    for side, (sent, first) in enumerate(((to_prior, 0), (to_next, density.shape[0] - RMAX))):
        half = jnp.where(second_core(), inv[side, HALF:, :], inv[side, :HALF, :])
        sent[pl.ds(4 * NZ, HALF), :] = half
        sent[pl.ds(HALO, tail), :] = jnp.zeros((tail, NY), jnp.float32)
        sent[pl.ds(HALO, RMAX), pl.ds(0, width)] = cells[pl.ds(first, RMAX), :]
        sent[pl.ds(mark_row, 1), pl.ds(mark_lane, width)] = spread
    for run in range(2):
        copies[run].wait()
        planes = [rows_in[run, k] for k in range(6)]
        magn = magnetic_yz(planes[4:], planes[:3], None)
        for k in range(2):
            to_next[plane_at(2 * run + k), :] = magn[k]
    wait_all(copies[6:])


def second_planes(fwd, adj, inverse, *rest):
    given, (_, to_prior, to_next, own, head, tail, inv, sems, *scratch) = rest[:6], rest[6:]
    rows = inverse.shape[0]
    small = source_copies(given, scratch) + [
        pltpu.make_async_copy(inverse.at[0], inv.at[0], sems.at[4]),
        pltpu.make_async_copy(inverse.at[rows - 1], inv.at[1], sems.at[5]),
    ]

    def ends(fields, run):
        return [
            pltpu.make_async_copy(fields.at[0, :, pl.ds(0, 2)], head.at[run], sems.at[2 * run]),
            pltpu.make_async_copy(
                fields.at[0, :, pl.ds(rows - 2, 2)], tail.at[run], sems.at[2 * run + 1]
            ),
        ]

    start_all(ends(fwd, 0) + small + ends(adj, 1))
    wait_all(small)

    def one_run(run, carry):
        wait_all(ends(fwd, run))

        def row(ref, x):
            return tuple(
                tuple(ref[run, k, x] for k in range(first, first + 3)) for first in (0, 3)
            )

        source = source_of(run, 0, given, scratch)
        elec, magn = row(head, 0)
        magn = magnetic(magn, elec, (head[run, 1, 1], head[run, 2, 1]))
        elec = electric(elec, magn, None, courant * inv[0], source)
        for k in range(2):
            to_prior[plane_at(2 * run + k), :] = elec[1 + k]
        for k in range(3):
            own[run, k] = elec[k]
        (elec_6, magn_6), (elec, magn) = row(tail, 0), row(tail, 1)
        yz_6 = magnetic_yz(magn_6[1:], elec_6, elec[1:])
        magn = magnetic(magn, elec, None)
        elec = electric(elec, magn, yz_6, courant * inv[1], source)
        magn = magnetic(magn, elec, None)
        for k in range(2):
            to_next[plane_at(2 * run + k), :] = magn[1 + k]
        for k in range(3):
            own[run, 3 + k] = elec[k]
            own[run, 6 + k] = magn[k]
        return carry

    lax.fori_loop(0, 2, one_run, 0)


class State:
    def __init__(self, given, home, written):
        self.given, self.home = given, home
        self.written = None if given is None else set(written)

    def load(self, run, first, x, count=3):
        parts = []
        for k in range(first, first + count):
            at_home = self.written is None or (k, x) in self.written
            ref, at = (self.home if at_home else self.given)(k, x)
            parts.append(ref[run, k, at])
        return tuple(parts)

    def store(self, run, first, x, planes):
        for k, value in enumerate(planes):
            ref, at = self.home(first + k, x)
            ref[run, first + k, at] = value
            if self.written is not None:
                self.written.add((first + k, x))

    def magnetic(self, run, x, following):
        magn = magnetic(self.load(run, 3, x), self.load(run, 0, x), following)
        self.store(run, 3, x, magn)
        return magn

    def electric(self, run, x, prior, scaled, source):
        elec = electric(self.load(run, 0, x), self.load(run, 3, x), prior, scaled, source)
        self.store(run, 0, x, elec)

    def electric_yz(self, run, x):
        return self.load(run, 1, x, 2)

    def magnetic_yz(self, run, x):
        return self.load(run, 4, x, 2)


def in_place(ref):
    return State(None, lambda k, x: (ref, x), ())


def products(ref, x):
    total = ref[0, 0, x] * ref[1, 0, x]
    for k in (1, 2):
        total = total + ref[0, k, x] * ref[1, k, x]
    return jnp.sum(total.reshape(NZ // 8, 8, NY), axis=0)


def interior(fwd, adj, inverse, *rest):
    given, (_, state, share, inv, sems, *scratch) = rest[:6], rest[6:]
    rows = inverse.shape[0]
    last = rows - 1
    into = source_copies(given, scratch) + [pltpu.make_async_copy(inverse, inv, sems.at[4])]

    def load(fields, run):
        return pltpu.make_async_copy(fields.at[0], state.at[run], sems.at[run])

    start_all([load(fwd, 0)] + into + [load(adj, 1)])
    wait_all(into)
    rows_of = in_place(state)

    for turn in range(STEPS):

        def one_run(run, carry, turn=turn):
            if turn == 0:
                load(fwd, run).wait()
            source = source_of(run, turn, given, scratch)
            for x in range(turn, last - turn):
                rows_of.magnetic(run, x, rows_of.electric_yz(run, x + 1))
                if x > turn:
                    rows_of.electric(
                        run, x, rows_of.magnetic_yz(run, x - 1), courant * inv[x], source
                    )
            return carry

        lax.fori_loop(0, 2, one_run, 0)
        for x in range(turn + 1, last - turn):
            share[x] = products(state, x) + (share[x] if turn > 0 else 0.0)
    for x in (0, last):
        share[x] = jnp.zeros(share.shape[1:], jnp.float32)


def flags():
    slab = lax.axis_index("slab")
    has_prior = (slab > 0).astype(jnp.float32)
    has_next = (slab < lax.axis_size("slab") - 1).astype(jnp.float32)
    return has_prior, has_next


def write_copies(parts, fields, sems):
    return [
        pltpu.make_async_copy(
            ref.at[run, *(pl.ds(at, n) for at, n in zip(source, count))],
            fields[run].at[0, *(pl.ds(at, n) for at, n in zip(target, count))],
            sems.at[len(parts) * run + part],
        )
        for run in range(2)
        for part, (ref, source, count, target) in enumerate(parts)
    ]


def respond(before, early, own, other, resp, scaled):
    second = second_core()
    for side, flag in enumerate(flags()):
        mine, theirs = (ref[pl.ds(side * HALF, HALF), :] for ref in (own, other))
        scaled[side, pl.ds(0, HALF), :] = courant * flag * jnp.where(second, theirs, mine)
        scaled[side, pl.ds(HALF, HALF), :] = courant * flag * jnp.where(second, mine, theirs)
    flagged = courant * flags()[0]

    def one_run(run, carry):
        magn_y, magn_z = flagged * before[run, 2, 0], -flagged * before[run, 1, 0]
        resp[run, 0] = scaled[0] * (dy_b(magn_z) - dz_b(magn_y))
        resp[run, 1] = -scaled[0] * magn_z
        resp[run, 2] = scaled[0] * magn_y
        resp[run, 3] = jnp.zeros(PLANE, jnp.float32)
        resp[run, 4] = magn_y
        resp[run, 5] = magn_z
        resp[run, 6] = scaled[1] * early[run, 5, 1]
        resp[run, 7] = -scaled[1] * early[run, 4, 1]
        return carry

    lax.fori_loop(0, 2, one_run, 0)


def border_rows(run, turn, state, source, inv, here, resp_in=None, resp_out=None, scaled=None):
    has_prior, has_next = flags()
    flagged = courant * has_prior
    last = inv.shape[0] - 1
    whole = here is not None

    def received(ref):
        return tuple(ref[plane_at(2 * run + k), :] for k in range(2))

    own_y, own_z = state.electric_yz(run, 0)
    if turn == 0:
        magn_r = (None, flagged * own_z, -flagged * own_y)
    else:
        elec_r = tuple(resp_in[run, k] for k in range(3))
        old = tuple(resp_in[run, k] for k in range(3, 6))
        magn_r = (
            old[0] - courant * (dy_f(elec_r[2]) - dz_f(elec_r[1])),
            old[1] - courant * (dz_f(elec_r[0]) + elec_r[2]) + flagged * own_z,
            old[2] + courant * (elec_r[1] + dy_f(elec_r[0])) - flagged * own_y,
        )
        if whole:
            resp_out[run, 0] = elec_r[0] + scaled[0] * (dy_b(magn_r[2]) - dz_b(magn_r[1]))
            resp_out[run, 1] = elec_r[1] + scaled[0] * (
                dz_b(magn_r[0]) - (magn_r[2] + courant * elec_r[1])
            )
            resp_out[run, 2] = elec_r[2] + scaled[0] * (
                (magn_r[1] - courant * elec_r[2]) - dy_b(magn_r[0])
            )
            resp_out[run, 3] = magn_r[0]
        resp_out[run, 4] = magn_r[1]
        resp_out[run, 5] = magn_r[2]
    for x in range(turn):
        state.magnetic(run, x, state.electric_yz(run, x + 1))
    if whole:
        arrived = received(here[0])
        prior = tuple(has_prior * arrived[k] + magn_r[1 + k] for k in range(2))
        state.electric(run, 0, prior, courant * inv[0], source)
    else:
        elec_x = electric_x(state.load(run, 0, 0, 1)[0], state.load(run, 3, 0), courant * inv[0])
        state.store(run, 0, 0, (elec_x + source,))
    for x in range(1, turn + 1):
        state.electric(run, x, state.magnetic_yz(run, x - 1), courant * inv[x], source)
    for x in range(last - turn, last):
        state.magnetic(run, x, state.electric_yz(run, x + 1))
    if whole:
        arrived = received(here[1])
        following = tuple(has_next * plane for plane in arrived)
        if turn > 0:
            following = tuple(following[k] + resp_in[run, 6 + k] for k in range(2))
        magn = state.magnetic(run, last, following)
    else:
        magn_x = magnetic_x(state.load(run, 3, last, 1)[0], state.load(run, 0, last))
        state.store(run, 3, last, (magn_x,))
    for x in range(last - turn, last + (1 if whole else 0)):
        state.electric(run, x, state.magnetic_yz(run, x - 1), courant * inv[x], source)
    if turn > 0 and whole:
        elec_y, elec_z = resp_in[run, 6], resp_in[run, 7]
        magn_x = -courant * (dy_f(elec_z) - dz_f(elec_y))
        resp_out[run, 6] = elec_y + scaled[1] * (dz_b(magn_x) - (courant * elec_y - magn[2]))
        resp_out[run, 7] = elec_z + scaled[1] * ((-courant * elec_z - magn[1]) - dy_b(magn_x))
    elif turn > 0:
        resp_out[run, 6] = resp_in[run, 6]
        resp_out[run, 7] = resp_in[run, 7]


def third_planes(inv, *rest):
    given, (before, own, to_prior, to_next) = rest[:6], rest[6:]
    last = inv.shape[0] - 1

    def one_run(run, carry):
        state = State(lambda k, x: (before, x), None, ())
        elec = tuple(own[run, k] for k in range(3))
        magn = magnetic(state.load(run, 3, 0), elec, state.electric_yz(run, 1))
        sent = electric_yz(elec[1:], magn, None, courant * inv[0])
        for k in range(2):
            to_prior[plane_at(2 * run + k), :] = sent[k]
        elec = tuple(own[run, 3 + k] for k in range(3))
        magn = tuple(own[run, 6 + k] for k in range(3))
        yz = magnetic_yz(
            state.magnetic_yz(run, last - 1), state.load(run, 0, last - 1), elec[1:]
        )
        elec = electric(elec, magn, yz, courant * inv[last], source_of(run, 1, given, ()))
        sent = magnetic_yz(magn[1:], elec, None)
        for k in range(2):
            to_next[plane_at(2 * run + k), :] = sent[k]
        return carry

    lax.fori_loop(0, 2, one_run, 0)


def step_one(inv, *rest):
    given, (before, prior_a, next_a, early, halves, share) = rest[:6], rest[6:]
    for side, ref in enumerate((prior_a, next_a)):
        halves[pl.ds(side * HALF, HALF), :] = ref[pl.ds(4 * NZ, HALF), :]

    def one_run(run, carry):
        state = State(lambda k, x: (before, x), lambda k, x: (early, min(x, 1)), ())
        border_rows(run, 0, state, source_of(run, 0, given, ()), inv, (prior_a, next_a))
        return carry

    lax.fori_loop(0, 2, one_run, 0)
    for side in range(2):
        share[side] = products(early, side)


def borders(inv, *rest):
    given, (before, early, resp_in, scaled, share, ends, prior_b, next_b) = rest[:6], rest[6:14]
    kept, inner, summed, waiting, fwd_out, adj_out, resp, total, sems = rest[14:]
    rows = inv.shape[0]
    last = rows - 1
    inside = rows - 2 * STEPS
    out = write_copies(
        (
            (before, (0, STEPS), (3, inside), (0, STEPS)),
            (before, (3, STEPS - 1), (3, inside + 1), (3, STEPS - 1)),
        ),
        (fwd_out, adj_out),
        sems,
    )
    start_all(out)
    homes = {0: (kept, 0), last - 1: (kept, 1), last: (kept, 2)}
    homes |= {1: (inner, 0), 2: (inner, 1), last - 2: (inner, 2)}

    def handed_in(k, x):
        if x == last or (x == 0 and k < 3):
            return (early, min(x, 1))
        return (before, x)

    written = set()
    for turn in range(1, STEPS):
        whole = turn < STEPS - 1
        seen = []

        def one_run(run, carry, turn=turn, whole=whole, seen=seen):
            state = State(handed_in, lambda k, x: homes[x], written)
            border_rows(
                run, turn, state, source_of(run, turn, given, ()), inv,
                (prior_b, next_b) if whole else None,
                resp_in if turn == 1 else resp, resp if whole else waiting, scaled,
            )
            seen[:] = [state.written]
            return carry

        lax.fori_loop(0, 2, one_run, 0)
        written = seen[0]
        reached = list(range(turn + 1)) + list(range(last - turn, last + 1))
        for x in reached if whole else reached[1:-1]:
            if turn > 1 and min(x, last - x) < turn:
                so_far = total[x]
            else:
                so_far = ends[min(x, 1)] if x in (0, last) else share[x]
            total[x] = so_far + products(*homes[x])
    for x in range(STEPS, rows - STEPS):
        total[x] = share[x]
    summed[...] = jnp.sum(total[...], axis=1)
    wait_all(out)


def last_planes(inv, *rest):
    given, (kept, summed, waiting, prior_c, next_c, _, blocks, ends) = rest[:6], rest[6:]
    last = inv.shape[0] - 1
    has_prior, has_next = flags()

    def one_run(run, carry):
        def row(first, slot, count):
            return tuple(kept[run, first + k, slot] for k in range(count))

        def arrived(ref, flag, first):
            return tuple(
                flag * ref[plane_at(2 * run + k), :] + waiting[run, first + k] for k in range(2)
            )

        elec = electric_yz(
            row(1, 0, 2), row(3, 0, 3), arrived(prior_c, has_prior, 4), courant * inv[0]
        )
        for k in range(2):
            ends[run, k, 0] = elec[k]
        elec = row(0, 2, 3)
        yz = magnetic_yz(row(4, 2, 2), elec, arrived(next_c, has_next, 6))
        source = source_of(run, STEPS - 1, given, ())
        elec = electric(elec, row(3, 2, 1) + yz, row(4, 1, 2), courant * inv[last], source)
        for k in range(3):
            ends[run, 2 + k, 0] = elec[k]
        for k in range(2):
            ends[run, 5 + k, 0] = yz[k]
        return carry

    lax.fori_loop(0, 2, one_run, 0)

    def row_sum(pairs):
        total = pairs[0][0] * pairs[0][1]
        for first, second in pairs[1:]:
            total = total + first * second
        return jnp.sum(total, axis=0, keepdims=True)

    head = row_sum(
        [(kept[0, 0, 0], kept[1, 0, 0])] + [(ends[0, k, 0], ends[1, k, 0]) for k in range(2)]
    )
    tail = row_sum([(ends[0, 2 + k, 0], ends[1, 2 + k, 0]) for k in range(3)])
    at = lax.broadcasted_iota(jnp.int32, summed.shape, 0)
    full = summed[...] + jnp.where(at == 0, head, 0.0) + jnp.where(at == last, tail, 0.0)
    slabs, width = blocks.shape[1], blocks.shape[3]
    for k in range(slabs):
        turned = pltpu.roll(full, (RMAX - k * (NY // slabs)) % NY, 1)
        for f in range(blocks.shape[0]):
            blocks[f, k] = turned[:, :width]


def write_borders(fwd, adj, kept, inner, fwd_out, adj_out, done, sems):
    last = fwd.shape[2] - 1
    done[...] = jnp.zeros_like(done)
    out = write_copies(
        (
            (inner, (0, 0), (6, 1), (0, 1)),
            (inner, (0, 1), (3, 1), (0, 2)),
            (inner, (0, 2), (6, 1), (0, last - 2)),
            (kept, (0, 1), (6, 1), (0, last - 1)),
            (kept, (0, 0), (1, 1), (0, 0)),
            (kept, (3, 0), (3, 1), (3, 0)),
            (kept, (3, 2), (1, 1), (3, last)),
        ),
        (fwd_out, adj_out),
        sems,
    )
    start_all(out)
    wait_all(out)


def write_ends(fwd, adj, ends, fwd_out, adj_out, sems):
    last = fwd.shape[2] - 1
    out = write_copies(
        (
            (ends, (0, 0), (2, 1), (1, 0)),
            (ends, (2, 0), (3, 1), (0, last)),
            (ends, (5, 0), (2, 1), (4, last)),
        ),
        (fwd_out, adj_out),
        sems,
    )
    start_all(out)
    wait_all(out)


def moved(rows, by):
    if by == 0:
        return rows
    count = rows.shape[0]
    at = lax.broadcasted_iota(jnp.int32, rows.shape, 0)
    keep = at < count - by if by > 0 else at >= -by
    return jnp.where(keep, pltpu.roll(rows, (-by) % count, 0), 0.0)


def rings(cells):
    tile = cells.shape[1] - 2 * RMAX
    columns = [cells[:, RMAX : RMAX + tile]]
    for a in range(1, RMAX + 1):
        columns.append(
            cells[:, RMAX - a : RMAX - a + tile] + cells[:, RMAX + a : RMAX + a + tile]
        )
    sums = {}
    for a in range(RMAX + 1):
        for b in range(RMAX + 1):
            part = columns[a]
            if b > 0:
                part = moved(part, b) + moved(part, -b)
            square = a * a + b * b
            sums[square] = sums[square] + part if square in sums else part
    return sums.items()


RINGS = len({a * a + b * b for a in range(RMAX + 1) for b in range(RMAX + 1)})


def by_tile(values, count):
    columns = count // values.shape[1]
    at = lax.broadcasted_iota(jnp.int32, (count, 1), 0) // columns
    spread = jnp.zeros((count, 1), jnp.float32)
    for k in range(values.shape[1]):
        spread = jnp.where(at == k, values[:, k : k + 1].astype(jnp.float32), spread)
    return spread


def filter_operands(
    prior_a, next_a, density, mask, radius_map, padded, chosen, weights, rows_of, marks_of
):
    tile_rows, width = density.shape
    reach = padded.shape[1]
    above, below = (ref[pl.ds(HALO, RMAX), :] for ref in (prior_a, next_a))
    mark_row, mark_lane = mark_at(width)
    rows_of[pl.ds(0, RMAX), :] = above[:, :width]
    rows_of[pl.ds(RMAX, tile_rows), :] = density[...]
    rows_of[pl.ds(RMAX + tile_rows, RMAX), :] = below[:, :width]
    marks_of[...] = jnp.zeros_like(marks_of)
    for side, ref in enumerate((prior_a, next_a)):
        marks_of[pl.ds(side, 1), :] = ref[pl.ds(mark_row, 1), pl.ds(mark_lane, width)]
    sides = marks_of[...].T
    first = lax.axis_index("slab") * tile_rows - RMAX
    at = lax.broadcasted_iota(jnp.int32, (width, reach), 1)
    inside = (at + first >= 0) & (at + first < NY)
    padded[...] = jnp.where(inside, rows_of[...].T, 0.0)
    mark = jnp.where(
        at < RMAX,
        sides[:, 0:1],
        jnp.where(at < RMAX + tile_rows, by_tile(mask, width), sides[:, 1:2]),
    )
    scale = step_size / math.sqrt(3 * STEPS * NZ * FREQS)
    chosen[...] = jnp.where(inside, scale * mark, 0.0)
    radius = by_tile(radius_map, width)
    total = jnp.zeros((width, tile_rows), jnp.float32)
    for k, (square, part) in enumerate(rings(inside.astype(jnp.float32))):
        weight = jnp.maximum(radius - math.sqrt(square), 0.0)
        weights[k] = jnp.broadcast_to(weight, total.shape)
        total = total + weight * part
    total = 1.0 / total
    for k in range(RINGS):
        weights[k] = weights[k] * total


def project(blocks, padded, chosen, weights, projected):
    freqs, slabs, rows, width = blocks.shape
    gradient = jnp.sum(blocks[...], axis=0).reshape(slabs * rows, width)
    updated = padded[...] + chosen[...] * gradient
    filtered = jnp.zeros(weights.shape[1:], jnp.float32)
    for k, (_, part) in enumerate(rings(updated)):
        filtered = filtered + weights[k] * part
    base = math.tanh(sharpness * midpoint)
    value = (base + jnp.tanh(sharpness * (filtered - midpoint))) / (
        base + math.tanh(sharpness * (1.0 - midpoint))
    )
    projected[...] = value.T


def around(shard, axis, by):
    count = lax.axis_size(axis)
    return lax.ppermute(shard, axis, [(i, (i + by) % count) for i in range(count)])


def on_device(
    inverse_permittivity,
    forward_fields,
    adjoint_fields,
    source_wave,
    source_profile,
    adjoint_wave,
    adjoint_profile,
    source_plane,
    monitor_plane,
    radius_map,
    design_mask,
    design_density,
):
    rows = forward_fields.shape[2]
    freqs, slabs = lax.axis_size("freq"), lax.axis_size("slab")
    tile_rows, width = design_density.shape
    reach = tile_rows + 2 * RMAX
    waves = (source_wave, adjoint_wave, source_profile, adjoint_profile)
    planes = (source_plane, monitor_plane)

    def pinned(arrays):
        return tuple(pltpu.with_memory_space_constraint(array, pltpu.HBM) for array in arrays)

    fields = pinned((forward_fields, adjoint_fields, inverse_permittivity))
    sources = pinned(waves) + planes
    dma = pltpu.SemaphoreType.DMA
    field_shape = shaped(*forward_fields.shape)
    state_shape = shaped(2, 6, rows, *PLANE)
    four = shaped(4 * NZ, NY)

    def vmem(*shape, kind=jnp.float32):
        return pltpu.VMEM(shape, kind)

    to_prior, to_next = kernel_call(
        first_planes,
        (shaped(sent_rows(width), NY),) * 2,
        [HBM] * 5,
        (VMEM, VMEM),
        [
            vmem(2, 6, *PLANE),
            vmem(2, *PLANE),
            vmem(tile_rows, width),
            vmem(*design_mask.shape, kind=jnp.int32),
            dma((10,)),
        ],
        "first_planes",
    )(*fields, *pinned((design_density, design_mask)))
    prior_a = around(to_next, "slab", 1)
    next_a = around(to_prior, "slab", -1)
    to_prior, to_next, own = kernel_call(
        second_planes,
        (four, four, shaped(2, 9, *PLANE)),
        [HBM] * 3 + SOURCE_SPECS + [ANY],
        (VMEM,) * 3,
        [
            vmem(2, 6, 2, *PLANE),
            vmem(2, 6, 2, *PLANE),
            vmem(2, *PLANE),
            dma((6,)),
            *SOURCE_SCRATCH,
        ],
        "second_planes",
        micros=2,
    )(*fields, *sources, to_prior)
    prior_b = around(to_next, "slab", 1)
    next_b = around(to_prior, "slab", -1)
    state, share = kernel_call(
        interior,
        (state_shape, shaped(rows, 8, NY)),
        [HBM] * 3 + SOURCE_SPECS + [ANY],
        (VMEM, VMEM),
        [vmem(rows, *PLANE), dma((5,)), *SOURCE_SCRATCH],
        "interior",
        micros=8,
    )(*fields, *sources, own)
    to_prior, to_next = kernel_call(
        third_planes,
        (four, four),
        [VMEM] + SOURCE_VALUES + [VMEM] * 2,
        (VMEM,) * 2,
        [],
        "third_planes",
    )(inverse_permittivity, *waves, *planes, state, own)
    prior_c = around(to_next, "slab", 1)
    next_c = around(to_prior, "slab", -1)
    early, halves, ends = kernel_call(
        step_one,
        (shaped(2, 6, 2, *PLANE), shaped(*PLANE), shaped(2, 8, NY)),
        [VMEM] + SOURCE_VALUES + [VMEM] * 3,
        (VMEM,) * 3,
        [],
        "step_one",
        micros=0,
    )(inverse_permittivity, *waves, *planes, state, prior_a, next_a)
    other = lax.ppermute(halves, "freq", [(i, i ^ 1) for i in range(freqs)])
    resp, scaled = kernel_call(
        respond,
        (shaped(2, 8, *PLANE), shaped(2, *PLANE)),
        [VMEM] * 4,
        (VMEM,) * 2,
        [],
        "respond",
        micros=0,
    )(state, early, halves, other)
    padded, chosen, weights = kernel_call(
        filter_operands,
        (shaped(width, reach), shaped(width, reach), shaped(RINGS, width, tile_rows)),
        [VMEM] * 5,
        (VMEM,) * 3,
        [vmem(reach, width), vmem(8, width)],
        "filter_operands",
        micros=0,
    )(prior_a, next_a, design_density, design_mask, radius_map)
    three = shaped(2, 6, 3, *PLANE)
    kept, inner, summed, waiting, forward_part, adjoint_part = kernel_call(
        borders,
        (three, three, shaped(rows, NY), shaped(2, 8, *PLANE), field_shape, field_shape),
        [VMEM] + SOURCE_VALUES + [VMEM] * 8,
        (VMEM,) * 4 + (HBM,) * 2,
        [vmem(2, 8, *PLANE), vmem(rows, 8, NY), dma((4,))],
        "borders",
        micros=0,
        grant=2 * GRANT,
    )(
        inverse_permittivity, *waves, *planes, state, early, resp, scaled, share, ends,
        prior_b, next_b,
    )
    forward_part, adjoint_part, done = kernel_call(
        write_borders,
        (field_shape, field_shape, shaped(8, 128)),
        [HBM] * 2 + [VMEM] * 2,
        (HBM, HBM, VMEM),
        [dma((14,))],
        "write_borders",
        input_output_aliases={0: 0, 1: 1},
    )(forward_part, adjoint_part, kept, inner)
    blocks, ends = kernel_call(
        last_planes,
        (shaped(freqs, slabs, rows, reach), shaped(2, 7, 1, *PLANE)),
        [VMEM] + SOURCE_VALUES + [VMEM] * 6,
        (VMEM, VMEM),
        [],
        "last_planes",
    )(inverse_permittivity, *waves, *planes, kept, summed, waiting, prior_c, next_c, done)
    forward_out, adjoint_out = kernel_call(
        write_ends,
        (field_shape, field_shape),
        [HBM] * 2 + [VMEM],
        (HBM, HBM),
        [dma((6,))],
        "write_ends",
        input_output_aliases={0: 0, 1: 1},
    )(forward_part, adjoint_part, ends)

    blocks = blocks.reshape(freqs * slabs, rows, reach)
    blocks = lax.all_to_all(blocks, ("freq", "slab"), 0, 0, tiled=True)
    blocks = blocks.reshape(freqs, slabs, rows, reach)
    projected = kernel_call(
        project,
        shaped(tile_rows, width),
        [VMEM] * 4,
        VMEM,
        [],
        "project",
    )(blocks, padded, chosen, weights)
    return (forward_out, adjoint_out, projected)


def solution(mesh):
    return jax.shard_map(
        on_device,
        mesh=mesh,
        in_specs=(
            P("slab", None, None),
            P("freq", None, "slab", None, None),
            P("freq", None, "slab", None, None),
            P("freq", None),
            P("freq", None),
            P("freq", None),
            P("freq", None),
            P("freq"),
            P("freq"),
            P("slab", None),
            P("slab", None),
            P("slab", None),
        ),
        out_specs=(
            P("freq", None, "slab", None, None),
            P("freq", None, "slab", None, None),
            P("slab", None),
        ),
        check_vma=False,
    )
```

```python
import math

import jax
import jax.numpy as jnp
from jax import lax
from jax.experimental import pallas as pl
from jax.experimental.pallas import tpu as pltpu
from jax.sharding import PartitionSpec as P

NY = 512
NZ = 24
FREQS = 4
STEPS = 3
RMAX = 4


courant = 0.5
sharpness = 4.0
midpoint = 0.5
step_size = 0.3

PLANE = (NZ, NY)
VMEM = pl.BlockSpec(memory_space=pltpu.VMEM)
HBM = pl.BlockSpec(memory_space=pltpu.HBM)
ANY = pl.BlockSpec(memory_space=pl.ANY)
GRANT = 8 * 1024 * 1024
PART = NZ // FREQS
HALO = 4 * NZ + PART


def slot_at(index, width):
    beside = NY // width
    return (pl.ds(HALO + index // beside, 1), pl.ds(index % beside * width, width))


def sent_rows(width):
    return -(-(HALO + RMAX // (NY // width) + 1) // 8) * 8


def neighbour(plane, axis, by):
    size = (8, 128)[axis]
    count = plane.shape[axis] // size
    tiles = [lax.slice_in_dim(plane, k * size, (k + 1) * size, axis=axis) for k in range(count)]
    turned = [pltpu.roll(tile, (-by) % size, axis) for tile in tiles]
    at = lax.broadcasted_iota(jnp.int32, tiles[0].shape, axis)
    edge = at == (size - 1 if by > 0 else 0)
    out = []
    for k in range(count):
        other = turned[k + by] if 0 <= k + by < count else 0.0
        out.append(jnp.where(edge, other, turned[k]))
    return jnp.concatenate(out, axis=axis)


def ahead(plane, axis):
    return neighbour(plane, axis, 1)


def behind(plane, axis):
    return neighbour(plane, axis, -1)


def dy_f(plane):
    return ahead(plane, 1) - plane


def dz_f(plane):
    return ahead(plane, 0) - plane


def dy_b(plane):
    return plane - behind(plane, 1)


def dz_b(plane):
    return plane - behind(plane, 0)


def magnetic_x(magn_x, elec):
    return magn_x - courant * (dy_f(elec[2]) - dz_f(elec[1]))


def magnetic_yz(magn, elec, following):
    next_y, next_z = (0.0, 0.0) if following is None else following
    return (
        magn[0] - courant * (dz_f(elec[0]) - (next_z - elec[2])),
        magn[1] - courant * ((next_y - elec[1]) - dy_f(elec[0])),
    )


def magnetic(magn, elec, following):
    return (magnetic_x(magn[0], elec),) + magnetic_yz(magn[1:], elec, following)


def electric_x(elec_x, magn, scaled):
    return elec_x + scaled * (dy_b(magn[2]) - dz_b(magn[1]))


def electric_yz(elec, magn, prior, scaled):
    prior_y, prior_z = (0.0, 0.0) if prior is None else prior
    return (
        elec[0] + scaled * (dz_b(magn[0]) - (magn[2] - prior_z)),
        elec[1] + scaled * ((magn[1] - prior_y) - dy_b(magn[0])),
    )


def electric(elec, magn, prior, scaled, source):
    return (electric_x(elec[0], magn, scaled) + source,) + electric_yz(
        elec[1:], magn, prior, scaled
    )


SOURCE_SCRATCH = [
    pltpu.VMEM((2, 1, STEPS), jnp.float32),
    pltpu.VMEM((2, 1, NY), jnp.float32),
    pltpu.SemaphoreType.DMA((4,)),
]
SOURCE_SPECS = [HBM] * 4 + [VMEM] * 2
SOURCE_VALUES = [VMEM] * 6


def source_copies(given, scratch):
    wave, profile, sems = scratch
    return [
        pltpu.make_async_copy(given[2 * k + run], ref.at[run], sems.at[2 * k + run])
        for k, ref in enumerate((wave, profile))
        for run in range(2)
    ]


def source_of(run, turn, given, scratch):
    if scratch:
        wave, profile = scratch[0][run], scratch[1][run]
    else:
        wave, profile = (jnp.where(run == 0, given[k][...], given[k + 1][...]) for k in (0, 2))
    row = wave[:, turn : turn + 1] * profile
    plane = jnp.where(run == 0, *(given[k][...].reshape(1, 1) for k in (4, 5)))
    at = lax.broadcasted_iota(jnp.int32, PLANE, 0)
    return jnp.where(at == plane, row, 0.0)


def kernel_call(body, out_shape, in_specs, out_specs, scratch, name, micros=1, grant=GRANT, **more):
    return pl.pallas_call(
        body,
        out_shape=out_shape,
        in_specs=in_specs,
        out_specs=out_specs,
        scratch_shapes=scratch,
        compiler_params=pltpu.CompilerParams(vmem_limit_bytes=grant),
        cost_estimate=pl.CostEstimate(
            flops=micros * 10**9, bytes_accessed=0, transcendentals=0
        ),
        name=name,
        **more,
    )


def shaped(*shape):
    return jax.ShapeDtypeStruct(shape, jnp.float32)


def start_all(copies):
    for copy in copies:
        copy.start()


def wait_all(copies):
    for copy in copies:
        copy.wait()


def plane_at(index):
    return pl.ds(pl.multiple_of(index * NZ, 8), NZ)


def first_planes(
    fwd, adj, inverse, density, mask, to_prior, to_next, rows_in, inv, cells, chosen, sems
):
    rows = inverse.shape[0]
    width = density.shape[1]
    copies = [
        pltpu.make_async_copy(fwd.at[0, :, rows - 1], rows_in.at[0], sems.at[0]),
        pltpu.make_async_copy(adj.at[0, :, rows - 1], rows_in.at[1], sems.at[1]),
        pltpu.make_async_copy(density, cells, sems.at[2]),
        pltpu.make_async_copy(mask, chosen, sems.at[3]),
        pltpu.make_async_copy(inverse.at[0], inv.at[0], sems.at[4]),
        pltpu.make_async_copy(inverse.at[rows - 1], inv.at[1], sems.at[5]),
    ]
    for run, fields in enumerate((fwd, adj)):
        for k in range(2):
            at = 2 * run + k
            copies.append(
                pltpu.make_async_copy(
                    fields.at[0, 1 + k, 0], to_prior.at[plane_at(at)], sems.at[6 + at]
                )
            )
    start_all(copies)
    wait_all(copies[2:6])
    at = lax.broadcasted_iota(jnp.int32, (1, width), 1) // (width // mask.shape[1])
    spread = jnp.zeros((1, width), jnp.float32)
    for k in range(mask.shape[1]):
        spread = jnp.where(at == k, chosen[:, k : k + 1].astype(jnp.float32), spread)
    rest = pl.ds(4 * NZ, to_next.shape[0] - 4 * NZ)
    group = lax.axis_index("freq")
    for side, (sent, first) in enumerate(((to_prior, 0), (to_next, density.shape[0] - RMAX))):
        part = inv[side, :PART, :]
        for k in range(1, FREQS):
            part = jnp.where(group == k, inv[side, k * PART : (k + 1) * PART, :], part)
        sent[rest, :] = jnp.zeros((to_next.shape[0] - 4 * NZ, NY), jnp.float32)
        sent[pl.ds(4 * NZ, PART), :] = part
        for k in range(RMAX):
            sent[slot_at(k, width)] = cells[pl.ds(first + k, 1), :]
        sent[slot_at(RMAX, width)] = spread
    for run in range(2):
        copies[run].wait()
        planes = [rows_in[run, k] for k in range(6)]
        magn = magnetic_yz(planes[4:], planes[:3], None)
        for k in range(2):
            to_next[plane_at(2 * run + k), :] = magn[k]
    wait_all(copies[6:])


def second_planes(fwd, adj, inverse, *rest):
    given, (_, to_prior, to_next, own, head, tail, inv, sems, *scratch) = rest[:6], rest[6:]
    rows = inverse.shape[0]
    small = source_copies(given, scratch) + [
        pltpu.make_async_copy(inverse.at[0], inv.at[0], sems.at[4]),
        pltpu.make_async_copy(inverse.at[rows - 1], inv.at[1], sems.at[5]),
    ]

    def ends(fields, run):
        return [
            pltpu.make_async_copy(fields.at[0, :, pl.ds(0, 2)], head.at[run], sems.at[2 * run]),
            pltpu.make_async_copy(
                fields.at[0, :, pl.ds(rows - 2, 2)], tail.at[run], sems.at[2 * run + 1]
            ),
        ]

    start_all(ends(fwd, 0) + small + ends(adj, 1))
    wait_all(small)

    def one_run(run, carry):
        wait_all(ends(fwd, run))

        def row(ref, x):
            return tuple(
                tuple(ref[run, k, x] for k in range(first, first + 3)) for first in (0, 3)
            )

        source = source_of(run, 0, given, scratch)
        elec, magn = row(head, 0)
        magn = magnetic(magn, elec, (head[run, 1, 1], head[run, 2, 1]))
        elec = electric(elec, magn, None, courant * inv[0], source)
        for k in range(2):
            to_prior[plane_at(2 * run + k), :] = elec[1 + k]
        for k in range(3):
            own[run, k] = elec[k]
        (elec_6, magn_6), (elec, magn) = row(tail, 0), row(tail, 1)
        yz_6 = magnetic_yz(magn_6[1:], elec_6, elec[1:])
        magn = magnetic(magn, elec, None)
        elec = electric(elec, magn, yz_6, courant * inv[1], source)
        magn = magnetic(magn, elec, None)
        for k in range(2):
            to_next[plane_at(2 * run + k), :] = magn[1 + k]
        for k in range(3):
            own[run, 3 + k] = elec[k]
            own[run, 6 + k] = magn[k]
        return carry

    lax.fori_loop(0, 2, one_run, 0)


class State:
    def __init__(self, given, home, written):
        self.given, self.home = given, home
        self.written = None if given is None else set(written)

    def load(self, run, first, x, count=3):
        parts = []
        for k in range(first, first + count):
            at_home = self.written is None or (k, x) in self.written
            ref, at = (self.home if at_home else self.given)(k, x)
            parts.append(ref[run, k, at])
        return tuple(parts)

    def store(self, run, first, x, planes):
        for k, value in enumerate(planes):
            ref, at = self.home(first + k, x)
            ref[run, first + k, at] = value
            if self.written is not None:
                self.written.add((first + k, x))

    def magnetic(self, run, x, following):
        magn = magnetic(self.load(run, 3, x), self.load(run, 0, x), following)
        self.store(run, 3, x, magn)
        return magn

    def electric(self, run, x, prior, scaled, source):
        elec = electric(self.load(run, 0, x), self.load(run, 3, x), prior, scaled, source)
        self.store(run, 0, x, elec)

    def electric_yz(self, run, x):
        return self.load(run, 1, x, 2)

    def magnetic_yz(self, run, x):
        return self.load(run, 4, x, 2)


def in_place(ref):
    return State(None, lambda k, x: (ref, x), ())


def products(ref, x):
    total = ref[0, 0, x] * ref[1, 0, x]
    for k in (1, 2):
        total = total + ref[0, k, x] * ref[1, k, x]
    return jnp.sum(total.reshape(NZ // 8, 8, NY), axis=0)


def interior(fwd, adj, inverse, *rest):
    given, (_, state, share, inv, sems, *scratch) = rest[:6], rest[6:]
    rows = inverse.shape[0]
    last = rows - 1
    into = source_copies(given, scratch) + [pltpu.make_async_copy(inverse, inv, sems.at[4])]

    def load(fields, run):
        return pltpu.make_async_copy(fields.at[0], state.at[run], sems.at[run])

    start_all([load(fwd, 0)] + into + [load(adj, 1)])
    wait_all(into)
    rows_of = in_place(state)

    for turn in range(STEPS):

        def one_run(run, carry, turn=turn):
            if turn == 0:
                load(fwd, run).wait()
            source = source_of(run, turn, given, scratch)
            for x in range(turn, last - turn):
                rows_of.magnetic(run, x, rows_of.electric_yz(run, x + 1))
                if x > turn:
                    rows_of.electric(
                        run, x, rows_of.magnetic_yz(run, x - 1), courant * inv[x], source
                    )
            return carry

        lax.fori_loop(0, 2, one_run, 0)
        for x in range(turn + 1, last - turn):
            share[x] = products(state, x) + (share[x] if turn > 0 else 0.0)
    for x in (0, last):
        share[x] = jnp.zeros(share.shape[1:], jnp.float32)


def flags():
    slab = lax.axis_index("slab")
    has_prior = (slab > 0).astype(jnp.float32)
    has_next = (slab < lax.axis_size("slab") - 1).astype(jnp.float32)
    return has_prior, has_next


def write_copies(parts, fields, sems):
    return [
        pltpu.make_async_copy(
            ref.at[run, *(pl.ds(at, n) for at, n in zip(source, count))],
            fields[run].at[0, *(pl.ds(at, n) for at, n in zip(target, count))],
            sems.at[len(parts) * run + part],
        )
        for run in range(2)
        for part, (ref, source, count, target) in enumerate(parts)
    ]


def respond(before, early, parts, resp, scaled):
    for side, flag in enumerate(flags()):
        for k in range(FREQS):
            part = parts[k, pl.ds(side * PART, PART), :]
            scaled[side, pl.ds(k * PART, PART), :] = courant * flag * part
    flagged = courant * flags()[0]

    def one_run(run, carry):
        magn_y, magn_z = flagged * before[run, 2, 0], -flagged * before[run, 1, 0]
        resp[run, 0] = scaled[0] * (dy_b(magn_z) - dz_b(magn_y))
        resp[run, 1] = -scaled[0] * magn_z
        resp[run, 2] = scaled[0] * magn_y
        resp[run, 3] = jnp.zeros(PLANE, jnp.float32)
        resp[run, 4] = magn_y
        resp[run, 5] = magn_z
        resp[run, 6] = scaled[1] * early[run, 5, 1]
        resp[run, 7] = -scaled[1] * early[run, 4, 1]
        return carry

    lax.fori_loop(0, 2, one_run, 0)


def border_rows(run, turn, state, source, inv, here, resp_in=None, resp_out=None, scaled=None):
    has_prior, has_next = flags()
    flagged = courant * has_prior
    last = inv.shape[0] - 1
    whole = here is not None

    def received(ref):
        return tuple(ref[plane_at(2 * run + k), :] for k in range(2))

    own_y, own_z = state.electric_yz(run, 0)
    if turn == 0:
        magn_r = (None, flagged * own_z, -flagged * own_y)
    else:
        elec_r = tuple(resp_in[run, k] for k in range(3))
        old = tuple(resp_in[run, k] for k in range(3, 6))
        magn_r = (
            old[0] - courant * (dy_f(elec_r[2]) - dz_f(elec_r[1])),
            old[1] - courant * (dz_f(elec_r[0]) + elec_r[2]) + flagged * own_z,
            old[2] + courant * (elec_r[1] + dy_f(elec_r[0])) - flagged * own_y,
        )
        if whole:
            resp_out[run, 0] = elec_r[0] + scaled[0] * (dy_b(magn_r[2]) - dz_b(magn_r[1]))
            resp_out[run, 1] = elec_r[1] + scaled[0] * (
                dz_b(magn_r[0]) - (magn_r[2] + courant * elec_r[1])
            )
            resp_out[run, 2] = elec_r[2] + scaled[0] * (
                (magn_r[1] - courant * elec_r[2]) - dy_b(magn_r[0])
            )
            resp_out[run, 3] = magn_r[0]
        resp_out[run, 4] = magn_r[1]
        resp_out[run, 5] = magn_r[2]
    for x in range(turn):
        state.magnetic(run, x, state.electric_yz(run, x + 1))
    if whole:
        arrived = received(here[0])
        prior = tuple(has_prior * arrived[k] + magn_r[1 + k] for k in range(2))
        state.electric(run, 0, prior, courant * inv[0], source)
    else:
        elec_x = electric_x(state.load(run, 0, 0, 1)[0], state.load(run, 3, 0), courant * inv[0])
        state.store(run, 0, 0, (elec_x + source,))
    for x in range(1, turn + 1):
        state.electric(run, x, state.magnetic_yz(run, x - 1), courant * inv[x], source)
    for x in range(last - turn, last):
        state.magnetic(run, x, state.electric_yz(run, x + 1))
    if whole:
        arrived = received(here[1])
        following = tuple(has_next * plane for plane in arrived)
        if turn > 0:
            following = tuple(following[k] + resp_in[run, 6 + k] for k in range(2))
        magn = state.magnetic(run, last, following)
    else:
        magn_x = magnetic_x(state.load(run, 3, last, 1)[0], state.load(run, 0, last))
        state.store(run, 3, last, (magn_x,))
    for x in range(last - turn, last + (1 if whole else 0)):
        state.electric(run, x, state.magnetic_yz(run, x - 1), courant * inv[x], source)
    if turn > 0 and whole:
        elec_y, elec_z = resp_in[run, 6], resp_in[run, 7]
        magn_x = -courant * (dy_f(elec_z) - dz_f(elec_y))
        resp_out[run, 6] = elec_y + scaled[1] * (dz_b(magn_x) - (courant * elec_y - magn[2]))
        resp_out[run, 7] = elec_z + scaled[1] * ((-courant * elec_z - magn[1]) - dy_b(magn_x))
    elif turn > 0:
        resp_out[run, 6] = resp_in[run, 6]
        resp_out[run, 7] = resp_in[run, 7]


def third_planes(inv, *rest):
    given, (before, own, to_prior, to_next) = rest[:6], rest[6:]
    last = inv.shape[0] - 1

    def one_run(run, carry):
        state = State(lambda k, x: (before, x), None, ())
        elec = tuple(own[run, k] for k in range(3))
        magn = magnetic(state.load(run, 3, 0), elec, state.electric_yz(run, 1))
        sent = electric_yz(elec[1:], magn, None, courant * inv[0])
        for k in range(2):
            to_prior[plane_at(2 * run + k), :] = sent[k]
        elec = tuple(own[run, 3 + k] for k in range(3))
        magn = tuple(own[run, 6 + k] for k in range(3))
        yz = magnetic_yz(
            state.magnetic_yz(run, last - 1), state.load(run, 0, last - 1), elec[1:]
        )
        elec = electric(elec, magn, yz, courant * inv[last], source_of(run, 1, given, ()))
        sent = magnetic_yz(magn[1:], elec, None)
        for k in range(2):
            to_next[plane_at(2 * run + k), :] = sent[k]
        return carry

    lax.fori_loop(0, 2, one_run, 0)


def step_one(inv, *rest):
    given, (before, prior_a, next_a, early, parts, share) = rest[:6], rest[6:]
    parts[...] = jnp.zeros_like(parts)
    for side, ref in enumerate((prior_a, next_a)):
        parts[pl.ds(side * PART, PART), :] = ref[pl.ds(4 * NZ, PART), :]

    def one_run(run, carry):
        state = State(lambda k, x: (before, x), lambda k, x: (early, min(x, 1)), ())
        border_rows(run, 0, state, source_of(run, 0, given, ()), inv, (prior_a, next_a))
        return carry

    lax.fori_loop(0, 2, one_run, 0)
    for side in range(2):
        share[side] = products(early, side)


def borders(inv, *rest):
    given, (before, early, resp_in, scaled, share, ends, next_b, prior_b) = rest[:6], rest[6:14]
    kept, inner, summed, waiting, fwd_out, adj_out, resp, total, sems = rest[14:]
    rows = inv.shape[0]
    last = rows - 1
    inside = rows - 2 * STEPS
    out = write_copies(
        (
            (before, (0, STEPS), (3, inside), (0, STEPS)),
            (before, (3, STEPS - 1), (3, inside + 1), (3, STEPS - 1)),
        ),
        (fwd_out, adj_out),
        sems,
    )
    start_all(out)
    homes = {0: (kept, 0), last - 1: (kept, 1), last: (kept, 2)}
    homes |= {1: (inner, 0), 2: (inner, 1), last - 2: (inner, 2)}

    def handed_in(k, x):
        if x == last or (x == 0 and k < 3):
            return (early, min(x, 1))
        return (before, x)

    written = set()
    for turn in range(1, STEPS):
        whole = turn < STEPS - 1
        seen = []

        def one_run(run, carry, turn=turn, whole=whole, seen=seen):
            state = State(handed_in, lambda k, x: homes[x], written)
            border_rows(
                run, turn, state, source_of(run, turn, given, ()), inv,
                (prior_b, next_b) if whole else None,
                resp_in if turn == 1 else resp, resp if whole else waiting, scaled,
            )
            seen[:] = [state.written]
            return carry

        lax.fori_loop(0, 2, one_run, 0)
        written = seen[0]
        reached = list(range(turn + 1)) + list(range(last - turn, last + 1))
        for x in reached if whole else reached[1:-1]:
            if turn > 1 and min(x, last - x) < turn:
                so_far = total[x]
            else:
                so_far = ends[min(x, 1)] if x in (0, last) else share[x]
            total[x] = so_far + products(*homes[x])
    for x in range(STEPS, rows - STEPS):
        total[x] = share[x]
    summed[...] = jnp.sum(total[...], axis=1)
    wait_all(out)


def last_planes(inv, *rest):
    given, (kept, summed, waiting, prior_c, next_c, _, blocks, ends) = rest[:6], rest[6:]
    last = inv.shape[0] - 1
    has_prior, has_next = flags()

    def one_run(run, carry):
        def row(first, slot, count):
            return tuple(kept[run, first + k, slot] for k in range(count))

        def arrived(ref, flag, first):
            return tuple(
                flag * ref[plane_at(2 * run + k), :] + waiting[run, first + k] for k in range(2)
            )

        elec = electric_yz(
            row(1, 0, 2), row(3, 0, 3), arrived(prior_c, has_prior, 4), courant * inv[0]
        )
        for k in range(2):
            ends[run, k, 0] = elec[k]
        elec = row(0, 2, 3)
        yz = magnetic_yz(row(4, 2, 2), elec, arrived(next_c, has_next, 6))
        source = source_of(run, STEPS - 1, given, ())
        elec = electric(elec, row(3, 2, 1) + yz, row(4, 1, 2), courant * inv[last], source)
        for k in range(3):
            ends[run, 2 + k, 0] = elec[k]
        for k in range(2):
            ends[run, 5 + k, 0] = yz[k]
        return carry

    lax.fori_loop(0, 2, one_run, 0)

    def row_sum(pairs):
        total = pairs[0][0] * pairs[0][1]
        for first, second in pairs[1:]:
            total = total + first * second
        return jnp.sum(total, axis=0, keepdims=True)

    head = row_sum(
        [(kept[0, 0, 0], kept[1, 0, 0])] + [(ends[0, k, 0], ends[1, k, 0]) for k in range(2)]
    )
    tail = row_sum([(ends[0, 2 + k, 0], ends[1, 2 + k, 0]) for k in range(3)])
    at = lax.broadcasted_iota(jnp.int32, summed.shape, 0)
    full = summed[...] + jnp.where(at == 0, head, 0.0) + jnp.where(at == last, tail, 0.0)
    slabs, width = blocks.shape[1], blocks.shape[3]
    for k in range(slabs):
        turned = pltpu.roll(full, (RMAX - k * (NY // slabs)) % NY, 1)
        for f in range(blocks.shape[0]):
            blocks[f, k] = turned[:, :width]


def write_borders(fwd, adj, kept, inner, fwd_out, adj_out, done, sems):
    last = fwd.shape[2] - 1
    done[...] = jnp.zeros_like(done)
    out = write_copies(
        (
            (inner, (0, 0), (6, 1), (0, 1)),
            (inner, (0, 1), (3, 1), (0, 2)),
            (inner, (0, 2), (6, 1), (0, last - 2)),
            (kept, (0, 1), (6, 1), (0, last - 1)),
            (kept, (0, 0), (1, 1), (0, 0)),
            (kept, (3, 0), (3, 1), (3, 0)),
            (kept, (3, 2), (1, 1), (3, last)),
        ),
        (fwd_out, adj_out),
        sems,
    )
    start_all(out)
    wait_all(out)


def write_ends(fwd, adj, ends, fwd_out, adj_out, sems):
    last = fwd.shape[2] - 1
    out = write_copies(
        (
            (ends, (0, 0), (2, 1), (1, 0)),
            (ends, (2, 0), (3, 1), (0, last)),
            (ends, (5, 0), (2, 1), (4, last)),
        ),
        (fwd_out, adj_out),
        sems,
    )
    start_all(out)
    wait_all(out)


def moved(rows, by):
    if by == 0:
        return rows
    count = rows.shape[0]
    at = lax.broadcasted_iota(jnp.int32, rows.shape, 0)
    keep = at < count - by if by > 0 else at >= -by
    return jnp.where(keep, pltpu.roll(rows, (-by) % count, 0), 0.0)


def rings(cells):
    tile = cells.shape[1] - 2 * RMAX
    columns = [cells[:, RMAX : RMAX + tile]]
    for a in range(1, RMAX + 1):
        columns.append(
            cells[:, RMAX - a : RMAX - a + tile] + cells[:, RMAX + a : RMAX + a + tile]
        )
    sums = {}
    for a in range(RMAX + 1):
        for b in range(RMAX + 1):
            part = columns[a]
            if b > 0:
                part = moved(part, b) + moved(part, -b)
            square = a * a + b * b
            sums[square] = sums[square] + part if square in sums else part
    return sums.items()


RINGS = len({a * a + b * b for a in range(RMAX + 1) for b in range(RMAX + 1)})


def by_tile(values, count):
    columns = count // values.shape[1]
    at = lax.broadcasted_iota(jnp.int32, (count, 1), 0) // columns
    spread = jnp.zeros((count, 1), jnp.float32)
    for k in range(values.shape[1]):
        spread = jnp.where(at == k, values[:, k : k + 1].astype(jnp.float32), spread)
    return spread


def filter_operands(
    prior_a, next_a, density, mask, radius_map, padded, chosen, weights, rows_of, marks_of
):
    tile_rows, width = density.shape
    reach = padded.shape[1]
    for side, (ref, first) in enumerate(((prior_a, 0), (next_a, RMAX + tile_rows))):
        for k in range(RMAX):
            rows_of[pl.ds(first + k, 1), :] = ref[slot_at(k, width)]
    rows_of[pl.ds(RMAX, tile_rows), :] = density[...]
    marks_of[...] = jnp.zeros_like(marks_of)
    for side, ref in enumerate((prior_a, next_a)):
        marks_of[pl.ds(side, 1), :] = ref[slot_at(RMAX, width)]
    sides = marks_of[...].T
    first = lax.axis_index("slab") * tile_rows - RMAX
    at = lax.broadcasted_iota(jnp.int32, (width, reach), 1)
    inside = (at + first >= 0) & (at + first < NY)
    padded[...] = jnp.where(inside, rows_of[...].T, 0.0)
    mark = jnp.where(
        at < RMAX,
        sides[:, 0:1],
        jnp.where(at < RMAX + tile_rows, by_tile(mask, width), sides[:, 1:2]),
    )
    scale = step_size / math.sqrt(3 * STEPS * NZ * FREQS)
    chosen[...] = jnp.where(inside, scale * mark, 0.0)
    radius = by_tile(radius_map, width)
    total = jnp.zeros((width, tile_rows), jnp.float32)
    for k, (square, part) in enumerate(rings(inside.astype(jnp.float32))):
        weight = jnp.maximum(radius - math.sqrt(square), 0.0)
        weights[k] = jnp.broadcast_to(weight, total.shape)
        total = total + weight * part
    total = 1.0 / total
    for k in range(RINGS):
        weights[k] = weights[k] * total


def project(blocks, padded, chosen, weights, projected):
    freqs, slabs, rows, width = blocks.shape
    gradient = jnp.sum(blocks[...], axis=0).reshape(slabs * rows, width)
    updated = padded[...] + chosen[...] * gradient
    filtered = jnp.zeros(weights.shape[1:], jnp.float32)
    for k, (_, part) in enumerate(rings(updated)):
        filtered = filtered + weights[k] * part
    base = math.tanh(sharpness * midpoint)
    value = (base + jnp.tanh(sharpness * (filtered - midpoint))) / (
        base + math.tanh(sharpness * (1.0 - midpoint))
    )
    projected[...] = value.T


def around(shard, axis, by):
    count = lax.axis_size(axis)
    return lax.ppermute(shard, axis, [(i, (i + by) % count) for i in range(count)])


def on_device(
    inverse_permittivity,
    forward_fields,
    adjoint_fields,
    source_wave,
    source_profile,
    adjoint_wave,
    adjoint_profile,
    source_plane,
    monitor_plane,
    radius_map,
    design_mask,
    design_density,
):
    rows = forward_fields.shape[2]
    freqs, slabs = lax.axis_size("freq"), lax.axis_size("slab")
    tile_rows, width = design_density.shape
    reach = tile_rows + 2 * RMAX
    waves = (source_wave, adjoint_wave, source_profile, adjoint_profile)
    planes = (source_plane, monitor_plane)

    def pinned(arrays):
        return tuple(pltpu.with_memory_space_constraint(array, pltpu.HBM) for array in arrays)

    fields = pinned((forward_fields, adjoint_fields, inverse_permittivity))
    sources = pinned(waves) + planes
    dma = pltpu.SemaphoreType.DMA
    field_shape = shaped(*forward_fields.shape)
    state_shape = shaped(2, 6, rows, *PLANE)
    four = shaped(4 * NZ, NY)

    def vmem(*shape, kind=jnp.float32):
        return pltpu.VMEM(shape, kind)

    to_prior, to_next = kernel_call(
        first_planes,
        (shaped(sent_rows(width), NY),) * 2,
        [HBM] * 5,
        (VMEM, VMEM),
        [
            vmem(2, 6, *PLANE),
            vmem(2, *PLANE),
            vmem(tile_rows, width),
            vmem(*design_mask.shape, kind=jnp.int32),
            dma((10,)),
        ],
        "first_planes",
    )(*fields, *pinned((design_density, design_mask)))
    prior_a = around(to_next, "slab", 1)
    next_a = around(to_prior, "slab", -1)
    to_prior, to_next, own = kernel_call(
        second_planes,
        (four, four, shaped(2, 9, *PLANE)),
        [HBM] * 3 + SOURCE_SPECS + [ANY],
        (VMEM,) * 3,
        [
            vmem(2, 6, 2, *PLANE),
            vmem(2, 6, 2, *PLANE),
            vmem(2, *PLANE),
            dma((6,)),
            *SOURCE_SCRATCH,
        ],
        "second_planes",
        micros=2,
    )(*fields, *sources, to_prior)
    prior_b = around(to_next, "slab", 1)
    next_b = around(to_prior, "slab", -1)
    state, share = kernel_call(
        interior,
        (state_shape, shaped(rows, 8, NY)),
        [HBM] * 3 + SOURCE_SPECS + [ANY],
        (VMEM, VMEM),
        [vmem(rows, *PLANE), dma((5,)), *SOURCE_SCRATCH],
        "interior",
        micros=8,
    )(*fields, *sources, own)
    to_prior, to_next = kernel_call(
        third_planes,
        (four, four),
        [VMEM] + SOURCE_VALUES + [VMEM] * 2,
        (VMEM,) * 2,
        [],
        "third_planes",
    )(inverse_permittivity, *waves, *planes, state, own)
    prior_c = around(to_next, "slab", 1)
    next_c = around(to_prior, "slab", -1)
    early, parts, ends = kernel_call(
        step_one,
        (shaped(2, 6, 2, *PLANE), shaped(-(-2 * PART // 8) * 8, NY), shaped(2, 8, NY)),
        [VMEM] + SOURCE_VALUES + [VMEM] * 3,
        (VMEM,) * 3,
        [],
        "step_one",
        micros=0,
    )(inverse_permittivity, *waves, *planes, state, prior_a, next_a)
    parts = lax.all_gather(parts, "freq")
    resp, scaled = kernel_call(
        respond,
        (shaped(2, 8, *PLANE), shaped(2, *PLANE)),
        [VMEM] * 3,
        (VMEM,) * 2,
        [],
        "respond",
        micros=0,
    )(state, early, parts)
    padded, chosen, weights = kernel_call(
        filter_operands,
        (shaped(width, reach), shaped(width, reach), shaped(RINGS, width, tile_rows)),
        [VMEM] * 5,
        (VMEM,) * 3,
        [vmem(reach, width), vmem(8, width)],
        "filter_operands",
        micros=0,
    )(prior_a, next_a, design_density, design_mask, radius_map)
    three = shaped(2, 6, 3, *PLANE)
    kept, inner, summed, waiting, forward_part, adjoint_part = kernel_call(
        borders,
        (three, three, shaped(rows, NY), shaped(2, 8, *PLANE), field_shape, field_shape),
        [VMEM] + SOURCE_VALUES + [VMEM] * 8,
        (VMEM,) * 4 + (HBM,) * 2,
        [vmem(2, 8, *PLANE), vmem(rows, 8, NY), dma((4,))],
        "borders",
        micros=0,
        grant=2 * GRANT,
    )(
        inverse_permittivity, *waves, *planes, state, early, resp, scaled, share, ends,
        next_b, prior_b,
    )
    forward_part, adjoint_part, done = kernel_call(
        write_borders,
        (field_shape, field_shape, shaped(8, 128)),
        [HBM] * 2 + [VMEM] * 2,
        (HBM, HBM, VMEM),
        [dma((14,))],
        "write_borders",
        input_output_aliases={0: 0, 1: 1},
    )(forward_part, adjoint_part, kept, inner)
    blocks, ends = kernel_call(
        last_planes,
        (shaped(freqs, slabs, rows, reach), shaped(2, 7, 1, *PLANE)),
        [VMEM] + SOURCE_VALUES + [VMEM] * 6,
        (VMEM, VMEM),
        [],
        "last_planes",
    )(inverse_permittivity, *waves, *planes, kept, summed, waiting, prior_c, next_c, done)
    forward_out, adjoint_out = kernel_call(
        write_ends,
        (field_shape, field_shape),
        [HBM] * 2 + [VMEM],
        (HBM, HBM),
        [dma((6,))],
        "write_ends",
        input_output_aliases={0: 0, 1: 1},
    )(forward_part, adjoint_part, ends)

    blocks = blocks.reshape(freqs * slabs, rows, reach)
    blocks = lax.all_to_all(blocks, ("freq", "slab"), 0, 0, tiled=True)
    blocks = blocks.reshape(freqs, slabs, rows, reach)
    projected = kernel_call(
        project,
        shaped(tile_rows, width),
        [VMEM] * 4,
        VMEM,
        [],
        "project",
    )(blocks, padded, chosen, weights)
    return (forward_out, adjoint_out, projected)


def solution(mesh):
    return jax.shard_map(
        on_device,
        mesh=mesh,
        in_specs=(
            P("slab", None, None),
            P("freq", None, "slab", None, None),
            P("freq", None, "slab", None, None),
            P("freq", None),
            P("freq", None),
            P("freq", None),
            P("freq", None),
            P("freq"),
            P("freq"),
            P("slab", None),
            P("slab", None),
            P("slab", None),
        ),
        out_specs=(
            P("freq", None, "slab", None, None),
            P("freq", None, "slab", None, None),
            P("slab", None),
        ),
        check_vma=False,
    )
```

```python
import math

import jax
import jax.numpy as jnp
from jax import lax
from jax.experimental import pallas as pl
from jax.experimental.pallas import tpu as pltpu
from jax.sharding import PartitionSpec as P

NY = 512
NZ = 24
FREQS = 4
STEPS = 3
RMAX = 4


courant = 0.5
sharpness = 4.0
midpoint = 0.5
step_size = 0.3

PLANE = (NZ, NY)
VMEM = pl.BlockSpec(memory_space=pltpu.VMEM)
HBM = pl.BlockSpec(memory_space=pltpu.HBM)
ANY = pl.BlockSpec(memory_space=pl.ANY)
GRANT = 8 * 1024 * 1024
PART = NZ // FREQS
HALO = 4 * NZ + PART


def slot_at(index, width):
    beside = NY // width
    return (pl.ds(HALO + index // beside, 1), pl.ds(index % beside * width, width))


def sent_rows(width):
    return -(-(HALO + RMAX // (NY // width) + 1) // 8) * 8


def neighbour(plane, axis, by):
    size = (8, 128)[axis]
    count = plane.shape[axis] // size
    tiles = [lax.slice_in_dim(plane, k * size, (k + 1) * size, axis=axis) for k in range(count)]
    turned = [pltpu.roll(tile, (-by) % size, axis) for tile in tiles]
    at = lax.broadcasted_iota(jnp.int32, tiles[0].shape, axis)
    edge = at == (size - 1 if by > 0 else 0)
    out = []
    for k in range(count):
        other = turned[k + by] if 0 <= k + by < count else 0.0
        out.append(jnp.where(edge, other, turned[k]))
    return jnp.concatenate(out, axis=axis)


def ahead(plane, axis):
    return neighbour(plane, axis, 1)


def behind(plane, axis):
    return neighbour(plane, axis, -1)


def dy_f(plane):
    return ahead(plane, 1) - plane


def dz_f(plane):
    return ahead(plane, 0) - plane


def dy_b(plane):
    return plane - behind(plane, 1)


def dz_b(plane):
    return plane - behind(plane, 0)


def magnetic_x(magn_x, elec):
    return magn_x - courant * (dy_f(elec[2]) - dz_f(elec[1]))


def magnetic_yz(magn, elec, following):
    next_y, next_z = (0.0, 0.0) if following is None else following
    return (
        magn[0] - courant * (dz_f(elec[0]) - (next_z - elec[2])),
        magn[1] - courant * ((next_y - elec[1]) - dy_f(elec[0])),
    )


def magnetic(magn, elec, following):
    return (magnetic_x(magn[0], elec),) + magnetic_yz(magn[1:], elec, following)


def electric_x(elec_x, magn, scaled):
    return elec_x + scaled * (dy_b(magn[2]) - dz_b(magn[1]))


def electric_yz(elec, magn, prior, scaled):
    prior_y, prior_z = (0.0, 0.0) if prior is None else prior
    return (
        elec[0] + scaled * (dz_b(magn[0]) - (magn[2] - prior_z)),
        elec[1] + scaled * ((magn[1] - prior_y) - dy_b(magn[0])),
    )


def electric(elec, magn, prior, scaled, source):
    return (electric_x(elec[0], magn, scaled) + source,) + electric_yz(
        elec[1:], magn, prior, scaled
    )


SOURCE_SCRATCH = [
    pltpu.VMEM((2, 1, STEPS), jnp.float32),
    pltpu.VMEM((2, 1, NY), jnp.float32),
    pltpu.SemaphoreType.DMA((4,)),
]
SOURCE_SPECS = [HBM] * 4 + [VMEM] * 2
SOURCE_VALUES = [VMEM] * 6


def source_copies(given, scratch):
    wave, profile, sems = scratch
    return [
        pltpu.make_async_copy(given[2 * k + run], ref.at[run], sems.at[2 * k + run])
        for k, ref in enumerate((wave, profile))
        for run in range(2)
    ]


def source_of(run, turn, given, scratch):
    if scratch:
        wave, profile = scratch[0][run], scratch[1][run]
    else:
        wave, profile = (jnp.where(run == 0, given[k][...], given[k + 1][...]) for k in (0, 2))
    row = wave[:, turn : turn + 1] * profile
    plane = jnp.where(run == 0, *(given[k][...].reshape(1, 1) for k in (4, 5)))
    at = lax.broadcasted_iota(jnp.int32, PLANE, 0)
    return jnp.where(at == plane, row, 0.0)


def kernel_call(body, out_shape, in_specs, out_specs, scratch, name, micros=1, grant=GRANT, **more):
    return pl.pallas_call(
        body,
        out_shape=out_shape,
        in_specs=in_specs,
        out_specs=out_specs,
        scratch_shapes=scratch,
        compiler_params=pltpu.CompilerParams(vmem_limit_bytes=grant),
        cost_estimate=pl.CostEstimate(
            flops=micros * 10**9, bytes_accessed=0, transcendentals=0
        ),
        name=name,
        **more,
    )


def shaped(*shape):
    return jax.ShapeDtypeStruct(shape, jnp.float32)


def start_all(copies):
    for copy in copies:
        copy.start()


def wait_all(copies):
    for copy in copies:
        copy.wait()


def plane_at(index):
    return pl.ds(pl.multiple_of(index * NZ, 8), NZ)


def first_planes(
    fwd, adj, inverse, density, mask, to_prior, to_next, rows_in, inv, cells, chosen, sems
):
    rows = inverse.shape[0]
    width = density.shape[1]
    copies = [
        pltpu.make_async_copy(fwd.at[0, :, rows - 1], rows_in.at[0], sems.at[0]),
        pltpu.make_async_copy(adj.at[0, :, rows - 1], rows_in.at[1], sems.at[1]),
        pltpu.make_async_copy(density, cells, sems.at[2]),
        pltpu.make_async_copy(mask, chosen, sems.at[3]),
        pltpu.make_async_copy(inverse.at[0], inv.at[0], sems.at[4]),
        pltpu.make_async_copy(inverse.at[rows - 1], inv.at[1], sems.at[5]),
    ]
    for run, fields in enumerate((fwd, adj)):
        for k in range(2):
            at = 2 * run + k
            copies.append(
                pltpu.make_async_copy(
                    fields.at[0, 1 + k, 0], to_prior.at[plane_at(at)], sems.at[6 + at]
                )
            )
    start_all(copies)
    wait_all(copies[2:6])
    at = lax.broadcasted_iota(jnp.int32, (1, width), 1) // (width // mask.shape[1])
    spread = jnp.zeros((1, width), jnp.float32)
    for k in range(mask.shape[1]):
        spread = jnp.where(at == k, chosen[:, k : k + 1].astype(jnp.float32), spread)
    rest = pl.ds(4 * NZ, to_next.shape[0] - 4 * NZ)
    group = lax.axis_index("freq")
    for side, (sent, first) in enumerate(((to_prior, 0), (to_next, density.shape[0] - RMAX))):
        part = inv[side, :PART, :]
        for k in range(1, FREQS):
            part = jnp.where(group == k, inv[side, k * PART : (k + 1) * PART, :], part)
        sent[rest, :] = jnp.zeros((to_next.shape[0] - 4 * NZ, NY), jnp.float32)
        sent[pl.ds(4 * NZ, PART), :] = part
        for k in range(RMAX):
            sent[slot_at(k, width)] = cells[pl.ds(first + k, 1), :]
        sent[slot_at(RMAX, width)] = spread
    for run in range(2):
        copies[run].wait()
        planes = [rows_in[run, k] for k in range(6)]
        magn = magnetic_yz(planes[4:], planes[:3], None)
        for k in range(2):
            to_next[plane_at(2 * run + k), :] = magn[k]
    wait_all(copies[6:])


def second_planes(fwd, adj, inverse, *rest):
    given, (_, to_prior, to_next, own, head, tail, inv, sems, *scratch) = rest[:6], rest[6:]
    rows = inverse.shape[0]
    small = source_copies(given, scratch) + [
        pltpu.make_async_copy(inverse.at[0], inv.at[0], sems.at[4]),
        pltpu.make_async_copy(inverse.at[rows - 1], inv.at[1], sems.at[5]),
    ]

    def ends(fields, run):
        return [
            pltpu.make_async_copy(fields.at[0, :, pl.ds(0, 2)], head.at[run], sems.at[2 * run]),
            pltpu.make_async_copy(
                fields.at[0, :, pl.ds(rows - 2, 2)], tail.at[run], sems.at[2 * run + 1]
            ),
        ]

    start_all(ends(fwd, 0) + small + ends(adj, 1))
    wait_all(small)

    def one_run(run, carry):
        wait_all(ends(fwd, run))

        def row(ref, x):
            return tuple(
                tuple(ref[run, k, x] for k in range(first, first + 3)) for first in (0, 3)
            )

        source = source_of(run, 0, given, scratch)
        elec, magn = row(head, 0)
        magn = magnetic(magn, elec, (head[run, 1, 1], head[run, 2, 1]))
        elec = electric(elec, magn, None, courant * inv[0], source)
        for k in range(2):
            to_prior[plane_at(2 * run + k), :] = elec[1 + k]
        for k in range(3):
            own[run, k] = elec[k]
        (elec_6, magn_6), (elec, magn) = row(tail, 0), row(tail, 1)
        yz_6 = magnetic_yz(magn_6[1:], elec_6, elec[1:])
        magn = magnetic(magn, elec, None)
        elec = electric(elec, magn, yz_6, courant * inv[1], source)
        magn = magnetic(magn, elec, None)
        for k in range(2):
            to_next[plane_at(2 * run + k), :] = magn[1 + k]
        for k in range(3):
            own[run, 3 + k] = elec[k]
            own[run, 6 + k] = magn[k]
        return carry

    lax.fori_loop(0, 2, one_run, 0)


class State:
    def __init__(self, given, home, written):
        self.given, self.home = given, home
        self.written = None if given is None else set(written)

    def load(self, run, first, x, count=3):
        parts = []
        for k in range(first, first + count):
            at_home = self.written is None or (k, x) in self.written
            ref, at = (self.home if at_home else self.given)(k, x)
            parts.append(ref[run, k, at])
        return tuple(parts)

    def store(self, run, first, x, planes):
        for k, value in enumerate(planes):
            ref, at = self.home(first + k, x)
            ref[run, first + k, at] = value
            if self.written is not None:
                self.written.add((first + k, x))

    def magnetic(self, run, x, following):
        magn = magnetic(self.load(run, 3, x), self.load(run, 0, x), following)
        self.store(run, 3, x, magn)
        return magn

    def electric(self, run, x, prior, scaled, source):
        elec = electric(self.load(run, 0, x), self.load(run, 3, x), prior, scaled, source)
        self.store(run, 0, x, elec)

    def electric_yz(self, run, x):
        return self.load(run, 1, x, 2)

    def magnetic_yz(self, run, x):
        return self.load(run, 4, x, 2)


def in_place(ref):
    return State(None, lambda k, x: (ref, x), ())


def products(ref, x):
    total = ref[0, 0, x] * ref[1, 0, x]
    for k in (1, 2):
        total = total + ref[0, k, x] * ref[1, k, x]
    return jnp.sum(total.reshape(NZ // 8, 8, NY), axis=0)


def interior(fwd, adj, inverse, *rest):
    given, (_, state, share, inv, sems, *scratch) = rest[:6], rest[6:]
    rows = inverse.shape[0]
    last = rows - 1
    into = source_copies(given, scratch) + [pltpu.make_async_copy(inverse, inv, sems.at[4])]

    def load(fields, run):
        return pltpu.make_async_copy(fields.at[0], state.at[run], sems.at[run])

    start_all([load(fwd, 0)] + into + [load(adj, 1)])
    wait_all(into)
    rows_of = in_place(state)

    for turn in range(STEPS):

        def one_run(run, carry, turn=turn):
            if turn == 0:
                load(fwd, run).wait()
            source = source_of(run, turn, given, scratch)
            for x in range(turn, last - turn):
                rows_of.magnetic(run, x, rows_of.electric_yz(run, x + 1))
                if x > turn:
                    rows_of.electric(
                        run, x, rows_of.magnetic_yz(run, x - 1), courant * inv[x], source
                    )
            return carry

        lax.fori_loop(0, 2, one_run, 0)
        for x in range(turn + 1, last - turn):
            share[x] = products(state, x) + (share[x] if turn > 0 else 0.0)
    for x in (0, last):
        share[x] = jnp.zeros(share.shape[1:], jnp.float32)


def flags():
    slab = lax.axis_index("slab")
    has_prior = (slab > 0).astype(jnp.float32)
    has_next = (slab < lax.axis_size("slab") - 1).astype(jnp.float32)
    return has_prior, has_next


def write_copies(parts, fields, sems, runs=(0, 1)):
    return [
        pltpu.make_async_copy(
            ref.at[run, *(pl.ds(at, n) for at, n in zip(source, count))],
            fields[run].at[0, *(pl.ds(at, n) for at, n in zip(target, count))],
            sems.at[len(parts) * run + part],
        )
        for run in runs
        for part, (ref, source, count, target) in enumerate(parts)
    ]


def respond(before, early, parts, resp, scaled):
    for side, flag in enumerate(flags()):
        for k in range(FREQS):
            part = parts[k, pl.ds(side * PART, PART), :]
            scaled[side, pl.ds(k * PART, PART), :] = courant * flag * part
    flagged = courant * flags()[0]

    def one_run(run, carry):
        magn_y, magn_z = flagged * before[run, 2, 0], -flagged * before[run, 1, 0]
        resp[run, 0] = scaled[0] * (dy_b(magn_z) - dz_b(magn_y))
        resp[run, 1] = -scaled[0] * magn_z
        resp[run, 2] = scaled[0] * magn_y
        resp[run, 3] = jnp.zeros(PLANE, jnp.float32)
        resp[run, 4] = magn_y
        resp[run, 5] = magn_z
        resp[run, 6] = scaled[1] * early[run, 5, 1]
        resp[run, 7] = -scaled[1] * early[run, 4, 1]
        return carry

    lax.fori_loop(0, 2, one_run, 0)


def border_rows(run, turn, state, source, inv, here, resp_in=None, resp_out=None, scaled=None):
    has_prior, has_next = flags()
    flagged = courant * has_prior
    last = inv.shape[0] - 1
    whole = here is not None

    def received(ref):
        return tuple(ref[plane_at(2 * run + k), :] for k in range(2))

    own_y, own_z = state.electric_yz(run, 0)
    if turn == 0:
        magn_r = (None, flagged * own_z, -flagged * own_y)
    else:
        elec_r = tuple(resp_in[run, k] for k in range(3))
        old = tuple(resp_in[run, k] for k in range(3, 6))
        magn_r = (
            old[0] - courant * (dy_f(elec_r[2]) - dz_f(elec_r[1])),
            old[1] - courant * (dz_f(elec_r[0]) + elec_r[2]) + flagged * own_z,
            old[2] + courant * (elec_r[1] + dy_f(elec_r[0])) - flagged * own_y,
        )
        if whole:
            resp_out[run, 0] = elec_r[0] + scaled[0] * (dy_b(magn_r[2]) - dz_b(magn_r[1]))
            resp_out[run, 1] = elec_r[1] + scaled[0] * (
                dz_b(magn_r[0]) - (magn_r[2] + courant * elec_r[1])
            )
            resp_out[run, 2] = elec_r[2] + scaled[0] * (
                (magn_r[1] - courant * elec_r[2]) - dy_b(magn_r[0])
            )
            resp_out[run, 3] = magn_r[0]
        resp_out[run, 4] = magn_r[1]
        resp_out[run, 5] = magn_r[2]
    for x in range(turn):
        state.magnetic(run, x, state.electric_yz(run, x + 1))
    if whole:
        arrived = received(here[0])
        prior = tuple(has_prior * arrived[k] + magn_r[1 + k] for k in range(2))
        state.electric(run, 0, prior, courant * inv[0], source)
    else:
        elec_x = electric_x(state.load(run, 0, 0, 1)[0], state.load(run, 3, 0), courant * inv[0])
        state.store(run, 0, 0, (elec_x + source,))
    for x in range(1, turn + 1):
        state.electric(run, x, state.magnetic_yz(run, x - 1), courant * inv[x], source)
    for x in range(last - turn, last):
        state.magnetic(run, x, state.electric_yz(run, x + 1))
    if whole:
        arrived = received(here[1])
        following = tuple(has_next * plane for plane in arrived)
        if turn > 0:
            following = tuple(following[k] + resp_in[run, 6 + k] for k in range(2))
        magn = state.magnetic(run, last, following)
    else:
        magn_x = magnetic_x(state.load(run, 3, last, 1)[0], state.load(run, 0, last))
        state.store(run, 3, last, (magn_x,))
    for x in range(last - turn, last + (1 if whole else 0)):
        state.electric(run, x, state.magnetic_yz(run, x - 1), courant * inv[x], source)
    if turn > 0 and whole:
        elec_y, elec_z = resp_in[run, 6], resp_in[run, 7]
        magn_x = -courant * (dy_f(elec_z) - dz_f(elec_y))
        resp_out[run, 6] = elec_y + scaled[1] * (dz_b(magn_x) - (courant * elec_y - magn[2]))
        resp_out[run, 7] = elec_z + scaled[1] * ((-courant * elec_z - magn[1]) - dy_b(magn_x))
    elif turn > 0:
        resp_out[run, 6] = resp_in[run, 6]
        resp_out[run, 7] = resp_in[run, 7]


def third_planes(inv, *rest):
    given, (before, own, to_prior, to_next) = rest[:6], rest[6:]
    last = inv.shape[0] - 1

    def one_run(run, carry):
        state = State(lambda k, x: (before, x), None, ())
        elec = tuple(own[run, k] for k in range(3))
        magn = magnetic(state.load(run, 3, 0), elec, state.electric_yz(run, 1))
        sent = electric_yz(elec[1:], magn, None, courant * inv[0])
        for k in range(2):
            to_prior[plane_at(2 * run + k), :] = sent[k]
        elec = tuple(own[run, 3 + k] for k in range(3))
        magn = tuple(own[run, 6 + k] for k in range(3))
        yz = magnetic_yz(
            state.magnetic_yz(run, last - 1), state.load(run, 0, last - 1), elec[1:]
        )
        elec = electric(elec, magn, yz, courant * inv[last], source_of(run, 1, given, ()))
        sent = magnetic_yz(magn[1:], elec, None)
        for k in range(2):
            to_next[plane_at(2 * run + k), :] = sent[k]
        return carry

    lax.fori_loop(0, 2, one_run, 0)


def step_one(inv, *rest):
    given, (before, next_a, prior_a, early, parts, share) = rest[:6], rest[6:]
    parts[...] = jnp.zeros_like(parts)
    for side, ref in enumerate((prior_a, next_a)):
        parts[pl.ds(side * PART, PART), :] = ref[pl.ds(4 * NZ, PART), :]

    def one_run(run, carry):
        state = State(lambda k, x: (before, x), lambda k, x: (early, min(x, 1)), ())
        border_rows(run, 0, state, source_of(run, 0, given, ()), inv, (prior_a, next_a))
        return carry

    lax.fori_loop(0, 2, one_run, 0)
    for side in range(2):
        share[side] = products(early, side)


def borders(inv, *rest):
    given, (before, early, resp_in, scaled, share, ends, next_b, prior_b) = rest[:6], rest[6:14]
    kept, summed, waiting, fwd_out, adj_out, inner, resp, total, inside_sems, sems = rest[14:]
    rows = inv.shape[0]
    last = rows - 1
    inside = rows - 2 * STEPS
    out = write_copies(
        (
            (before, (0, STEPS), (3, inside), (0, STEPS)),
            (before, (3, STEPS - 1), (3, inside + 1), (3, STEPS - 1)),
        ),
        (fwd_out, adj_out),
        inside_sems,
    )
    start_all(out)
    rows_done = (
        (inner, (0, 0), (6, 1), (0, 1)),
        (inner, (0, 1), (3, 1), (0, 2)),
        (inner, (0, 2), (6, 1), (0, last - 2)),
        (kept, (0, 1), (6, 1), (0, last - 1)),
        (kept, (0, 0), (1, 1), (0, 0)),
        (kept, (3, 0), (3, 1), (3, 0)),
        (kept, (3, 2), (1, 1), (3, last)),
    )
    homes = {0: (kept, 0), last - 1: (kept, 1), last: (kept, 2)}
    homes |= {1: (inner, 0), 2: (inner, 1), last - 2: (inner, 2)}

    def handed_in(k, x):
        if x == last or (x == 0 and k < 3):
            return (early, min(x, 1))
        return (before, x)

    written = set()
    for turn in range(1, STEPS):
        whole = turn < STEPS - 1
        seen = []

        def one_run(run, carry, turn=turn, whole=whole, seen=seen):
            state = State(handed_in, lambda k, x: homes[x], written)
            border_rows(
                run, turn, state, source_of(run, turn, given, ()), inv,
                (prior_b, next_b) if whole else None,
                resp_in if turn == 1 else resp, resp if whole else waiting, scaled,
            )
            seen[:] = [state.written]
            return carry

        if whole:
            lax.fori_loop(0, 2, one_run, 0)
        else:
            for run in range(2):
                one_run(run, 0)
                mine = write_copies(rows_done, (fwd_out, adj_out), sems, (run,))
                start_all(mine)
                out = out + mine
        written = seen[0]
        reached = list(range(turn + 1)) + list(range(last - turn, last + 1))
        for x in reached if whole else reached[1:-1]:
            if turn > 1 and min(x, last - x) < turn:
                so_far = total[x]
            else:
                so_far = ends[min(x, 1)] if x in (0, last) else share[x]
            total[x] = so_far + products(*homes[x])
    for x in range(STEPS, rows - STEPS):
        total[x] = share[x]
    summed[...] = jnp.sum(total[...], axis=1)
    wait_all(out)


def last_planes(inv, *rest):
    given, (kept, summed, waiting, prior_c, next_c, blocks, ends) = rest[:6], rest[6:]
    last = inv.shape[0] - 1
    has_prior, has_next = flags()

    def one_run(run, carry):
        def row(first, slot, count):
            return tuple(kept[run, first + k, slot] for k in range(count))

        def arrived(ref, flag, first):
            return tuple(
                flag * ref[plane_at(2 * run + k), :] + waiting[run, first + k] for k in range(2)
            )

        elec = electric_yz(
            row(1, 0, 2), row(3, 0, 3), arrived(prior_c, has_prior, 4), courant * inv[0]
        )
        for k in range(2):
            ends[run, k, 0] = elec[k]
        elec = row(0, 2, 3)
        yz = magnetic_yz(row(4, 2, 2), elec, arrived(next_c, has_next, 6))
        source = source_of(run, STEPS - 1, given, ())
        elec = electric(elec, row(3, 2, 1) + yz, row(4, 1, 2), courant * inv[last], source)
        for k in range(3):
            ends[run, 2 + k, 0] = elec[k]
        for k in range(2):
            ends[run, 5 + k, 0] = yz[k]
        return carry

    lax.fori_loop(0, 2, one_run, 0)

    def row_sum(pairs):
        total = pairs[0][0] * pairs[0][1]
        for first, second in pairs[1:]:
            total = total + first * second
        return jnp.sum(total, axis=0, keepdims=True)

    head = row_sum(
        [(kept[0, 0, 0], kept[1, 0, 0])] + [(ends[0, k, 0], ends[1, k, 0]) for k in range(2)]
    )
    tail = row_sum([(ends[0, 2 + k, 0], ends[1, 2 + k, 0]) for k in range(3)])
    at = lax.broadcasted_iota(jnp.int32, summed.shape, 0)
    full = summed[...] + jnp.where(at == 0, head, 0.0) + jnp.where(at == last, tail, 0.0)
    slabs, width = blocks.shape[1], blocks.shape[3]
    for k in range(slabs):
        turned = pltpu.roll(full, (RMAX - k * (NY // slabs)) % NY, 1)
        for f in range(blocks.shape[0]):
            blocks[f, k] = turned[:, :width]


def write_ends(fwd, adj, ends, fwd_out, adj_out, sems):
    last = fwd.shape[2] - 1
    out = write_copies(
        (
            (ends, (0, 0), (2, 1), (1, 0)),
            (ends, (2, 0), (3, 1), (0, last)),
            (ends, (5, 0), (2, 1), (4, last)),
        ),
        (fwd_out, adj_out),
        sems,
    )
    start_all(out)
    wait_all(out)


def moved(rows, by):
    if by == 0:
        return rows
    count = rows.shape[0]
    at = lax.broadcasted_iota(jnp.int32, rows.shape, 0)
    keep = at < count - by if by > 0 else at >= -by
    return jnp.where(keep, pltpu.roll(rows, (-by) % count, 0), 0.0)


def rings(cells):
    tile = cells.shape[1] - 2 * RMAX
    columns = [cells[:, RMAX : RMAX + tile]]
    for a in range(1, RMAX + 1):
        columns.append(
            cells[:, RMAX - a : RMAX - a + tile] + cells[:, RMAX + a : RMAX + a + tile]
        )
    sums = {}
    for a in range(RMAX + 1):
        for b in range(RMAX + 1):
            part = columns[a]
            if b > 0:
                part = moved(part, b) + moved(part, -b)
            square = a * a + b * b
            sums[square] = sums[square] + part if square in sums else part
    return sums.items()


RINGS = len({a * a + b * b for a in range(RMAX + 1) for b in range(RMAX + 1)})


def by_tile(values, count):
    columns = count // values.shape[1]
    at = lax.broadcasted_iota(jnp.int32, (count, 1), 0) // columns
    spread = jnp.zeros((count, 1), jnp.float32)
    for k in range(values.shape[1]):
        spread = jnp.where(at == k, values[:, k : k + 1].astype(jnp.float32), spread)
    return spread


def filter_operands(
    prior_a, next_a, density, mask, radius_map, padded, chosen, weights, rows_of, marks_of
):
    tile_rows, width = density.shape
    reach = padded.shape[1]
    for side, (ref, first) in enumerate(((prior_a, 0), (next_a, RMAX + tile_rows))):
        for k in range(RMAX):
            rows_of[pl.ds(first + k, 1), :] = ref[slot_at(k, width)]
    rows_of[pl.ds(RMAX, tile_rows), :] = density[...]
    marks_of[...] = jnp.zeros_like(marks_of)
    for side, ref in enumerate((prior_a, next_a)):
        marks_of[pl.ds(side, 1), :] = ref[slot_at(RMAX, width)]
    sides = marks_of[...].T
    first = lax.axis_index("slab") * tile_rows - RMAX
    at = lax.broadcasted_iota(jnp.int32, (width, reach), 1)
    inside = (at + first >= 0) & (at + first < NY)
    padded[...] = jnp.where(inside, rows_of[...].T, 0.0)
    mark = jnp.where(
        at < RMAX,
        sides[:, 0:1],
        jnp.where(at < RMAX + tile_rows, by_tile(mask, width), sides[:, 1:2]),
    )
    scale = step_size / math.sqrt(3 * STEPS * NZ * FREQS)
    chosen[...] = jnp.where(inside, scale * mark, 0.0)
    radius = by_tile(radius_map, width)
    total = jnp.zeros((width, tile_rows), jnp.float32)
    for k, (square, part) in enumerate(rings(inside.astype(jnp.float32))):
        weight = jnp.maximum(radius - math.sqrt(square), 0.0)
        weights[k] = jnp.broadcast_to(weight, total.shape)
        total = total + weight * part
    total = 1.0 / total
    for k in range(RINGS):
        weights[k] = weights[k] * total


def project(blocks, padded, chosen, weights, projected):
    freqs, slabs, rows, width = blocks.shape
    gradient = jnp.sum(blocks[...], axis=0).reshape(slabs * rows, width)
    updated = padded[...] + chosen[...] * gradient
    filtered = jnp.zeros(weights.shape[1:], jnp.float32)
    for k, (_, part) in enumerate(rings(updated)):
        filtered = filtered + weights[k] * part
    base = math.tanh(sharpness * midpoint)
    value = (base + jnp.tanh(sharpness * (filtered - midpoint))) / (
        base + math.tanh(sharpness * (1.0 - midpoint))
    )
    projected[...] = value.T


def around(shard, axis, by):
    count = lax.axis_size(axis)
    return lax.ppermute(shard, axis, [(i, (i + by) % count) for i in range(count)])


def on_device(
    inverse_permittivity,
    forward_fields,
    adjoint_fields,
    source_wave,
    source_profile,
    adjoint_wave,
    adjoint_profile,
    source_plane,
    monitor_plane,
    radius_map,
    design_mask,
    design_density,
):
    rows = forward_fields.shape[2]
    freqs, slabs = lax.axis_size("freq"), lax.axis_size("slab")
    tile_rows, width = design_density.shape
    reach = tile_rows + 2 * RMAX
    waves = (source_wave, adjoint_wave, source_profile, adjoint_profile)
    planes = (source_plane, monitor_plane)

    def pinned(arrays):
        return tuple(pltpu.with_memory_space_constraint(array, pltpu.HBM) for array in arrays)

    fields = pinned((forward_fields, adjoint_fields, inverse_permittivity))
    sources = pinned(waves) + planes
    dma = pltpu.SemaphoreType.DMA
    field_shape = shaped(*forward_fields.shape)
    state_shape = shaped(2, 6, rows, *PLANE)
    four = shaped(4 * NZ, NY)

    def vmem(*shape, kind=jnp.float32):
        return pltpu.VMEM(shape, kind)

    to_prior, to_next = kernel_call(
        first_planes,
        (shaped(sent_rows(width), NY),) * 2,
        [HBM] * 5,
        (VMEM, VMEM),
        [
            vmem(2, 6, *PLANE),
            vmem(2, *PLANE),
            vmem(tile_rows, width),
            vmem(*design_mask.shape, kind=jnp.int32),
            dma((10,)),
        ],
        "first_planes",
    )(*fields, *pinned((design_density, design_mask)))
    prior_a = around(to_next, "slab", 1)
    next_a = around(to_prior, "slab", -1)
    to_prior, to_next, own = kernel_call(
        second_planes,
        (four, four, shaped(2, 9, *PLANE)),
        [HBM] * 3 + SOURCE_SPECS + [ANY],
        (VMEM,) * 3,
        [
            vmem(2, 6, 2, *PLANE),
            vmem(2, 6, 2, *PLANE),
            vmem(2, *PLANE),
            dma((6,)),
            *SOURCE_SCRATCH,
        ],
        "second_planes",
        micros=2,
    )(*fields, *sources, to_prior)
    prior_b = around(to_next, "slab", 1)
    next_b = around(to_prior, "slab", -1)
    state, share = kernel_call(
        interior,
        (state_shape, shaped(rows, 8, NY)),
        [HBM] * 3 + SOURCE_SPECS + [ANY],
        (VMEM, VMEM),
        [vmem(rows, *PLANE), dma((5,)), *SOURCE_SCRATCH],
        "interior",
        micros=8,
    )(*fields, *sources, own)
    to_prior, to_next = kernel_call(
        third_planes,
        (four, four),
        [VMEM] + SOURCE_VALUES + [VMEM] * 2,
        (VMEM,) * 2,
        [],
        "third_planes",
    )(inverse_permittivity, *waves, *planes, state, own)
    prior_c = around(to_next, "slab", 1)
    next_c = around(to_prior, "slab", -1)
    early, parts, ends = kernel_call(
        step_one,
        (shaped(2, 6, 2, *PLANE), shaped(-(-2 * PART // 8) * 8, NY), shaped(2, 8, NY)),
        [VMEM] + SOURCE_VALUES + [VMEM] * 3,
        (VMEM,) * 3,
        [],
        "step_one",
        micros=0,
    )(inverse_permittivity, *waves, *planes, state, next_a, prior_a)
    parts = lax.all_gather(parts, "freq")
    resp, scaled = kernel_call(
        respond,
        (shaped(2, 8, *PLANE), shaped(2, *PLANE)),
        [VMEM] * 3,
        (VMEM,) * 2,
        [],
        "respond",
        micros=0,
    )(state, early, parts)
    padded, chosen, weights = kernel_call(
        filter_operands,
        (shaped(width, reach), shaped(width, reach), shaped(RINGS, width, tile_rows)),
        [VMEM] * 5,
        (VMEM,) * 3,
        [vmem(reach, width), vmem(8, width)],
        "filter_operands",
        micros=0,
    )(prior_a, next_a, design_density, design_mask, radius_map)
    three = shaped(2, 6, 3, *PLANE)
    kept, summed, waiting, forward_part, adjoint_part = kernel_call(
        borders,
        (three, shaped(rows, NY), shaped(2, 8, *PLANE), field_shape, field_shape),
        [VMEM] + SOURCE_VALUES + [VMEM] * 8,
        (VMEM,) * 3 + (HBM,) * 2,
        [
            vmem(2, 6, 3, *PLANE),
            vmem(2, 8, *PLANE),
            vmem(rows, 8, NY),
            dma((4,)),
            dma((14,)),
        ],
        "borders",
        micros=0,
        grant=2 * GRANT,
    )(
        inverse_permittivity, *waves, *planes, state, early, resp, scaled, share, ends,
        next_b, prior_b,
    )
    blocks, ends = kernel_call(
        last_planes,
        (shaped(freqs, slabs, rows, reach), shaped(2, 7, 1, *PLANE)),
        [VMEM] + SOURCE_VALUES + [VMEM] * 5,
        (VMEM, VMEM),
        [],
        "last_planes",
    )(inverse_permittivity, *waves, *planes, kept, summed, waiting, prior_c, next_c)
    forward_out, adjoint_out = kernel_call(
        write_ends,
        (field_shape, field_shape),
        [HBM] * 2 + [VMEM],
        (HBM, HBM),
        [dma((6,))],
        "write_ends",
        input_output_aliases={0: 0, 1: 1},
    )(forward_part, adjoint_part, ends)

    blocks = blocks.reshape(freqs * slabs, rows, reach)
    blocks = lax.all_to_all(blocks, ("freq", "slab"), 0, 0, tiled=True)
    blocks = blocks.reshape(freqs, slabs, rows, reach)
    projected = kernel_call(
        project,
        shaped(tile_rows, width),
        [VMEM] * 4,
        VMEM,
        [],
        "project",
    )(blocks, padded, chosen, weights)
    return (forward_out, adjoint_out, projected)


def solution(mesh):
    return jax.shard_map(
        on_device,
        mesh=mesh,
        in_specs=(
            P("slab", None, None),
            P("freq", None, "slab", None, None),
            P("freq", None, "slab", None, None),
            P("freq", None),
            P("freq", None),
            P("freq", None),
            P("freq", None),
            P("freq"),
            P("freq"),
            P("slab", None),
            P("slab", None),
            P("slab", None),
        ),
        out_specs=(
            P("freq", None, "slab", None, None),
            P("freq", None, "slab", None, None),
            P("slab", None),
        ),
        check_vma=False,
    )
```

```python
import math

import jax
import jax.numpy as jnp
from jax import lax
from jax.experimental import pallas as pl
from jax.experimental.pallas import tpu as pltpu
from jax.sharding import PartitionSpec as P

NY = 512
NZ = 24
FREQS = 4
STEPS = 3
RMAX = 4


courant = 0.5
sharpness = 4.0
midpoint = 0.5
step_size = 0.3

PLANE = (NZ, NY)
VMEM = pl.BlockSpec(memory_space=pltpu.VMEM)
HBM = pl.BlockSpec(memory_space=pltpu.HBM)
ANY = pl.BlockSpec(memory_space=pl.ANY)
GRANT = 8 * 1024 * 1024
PART = NZ // FREQS
HALO = 4 * NZ + PART


def slot_at(index, width):
    beside = NY // width
    return (pl.ds(HALO + index // beside, 1), pl.ds(index % beside * width, width))


def sent_rows(width):
    return -(-(HALO + RMAX // (NY // width) + 1) // 8) * 8


def neighbour(plane, axis, by):
    size = (8, 128)[axis]
    count = plane.shape[axis] // size
    tiles = [lax.slice_in_dim(plane, k * size, (k + 1) * size, axis=axis) for k in range(count)]
    turned = [pltpu.roll(tile, (-by) % size, axis) for tile in tiles]
    at = lax.broadcasted_iota(jnp.int32, tiles[0].shape, axis)
    edge = at == (size - 1 if by > 0 else 0)
    out = []
    for k in range(count):
        other = turned[k + by] if 0 <= k + by < count else 0.0
        out.append(jnp.where(edge, other, turned[k]))
    return jnp.concatenate(out, axis=axis)


def ahead(plane, axis):
    return neighbour(plane, axis, 1)


def behind(plane, axis):
    return neighbour(plane, axis, -1)


def dy_f(plane):
    return ahead(plane, 1) - plane


def dz_f(plane):
    return ahead(plane, 0) - plane


def dy_b(plane):
    return plane - behind(plane, 1)


def dz_b(plane):
    return plane - behind(plane, 0)


def magnetic_x(magn_x, elec):
    return magn_x - courant * (dy_f(elec[2]) - dz_f(elec[1]))


def magnetic_yz(magn, elec, following):
    next_y, next_z = (0.0, 0.0) if following is None else following
    return (
        magn[0] - courant * (dz_f(elec[0]) - (next_z - elec[2])),
        magn[1] - courant * ((next_y - elec[1]) - dy_f(elec[0])),
    )


def magnetic(magn, elec, following):
    return (magnetic_x(magn[0], elec),) + magnetic_yz(magn[1:], elec, following)


def electric_x(elec_x, magn, scaled):
    return elec_x + scaled * (dy_b(magn[2]) - dz_b(magn[1]))


def electric_yz(elec, magn, prior, scaled):
    prior_y, prior_z = (0.0, 0.0) if prior is None else prior
    return (
        elec[0] + scaled * (dz_b(magn[0]) - (magn[2] - prior_z)),
        elec[1] + scaled * ((magn[1] - prior_y) - dy_b(magn[0])),
    )


def electric(elec, magn, prior, scaled, source):
    return (electric_x(elec[0], magn, scaled) + source,) + electric_yz(
        elec[1:], magn, prior, scaled
    )


SOURCE_SCRATCH = [
    pltpu.VMEM((2, 1, STEPS), jnp.float32),
    pltpu.VMEM((2, 1, NY), jnp.float32),
    pltpu.SemaphoreType.DMA((4,)),
]
SOURCE_SPECS = [HBM] * 4 + [VMEM] * 2
SOURCE_VALUES = [VMEM] * 6


def source_copies(given, scratch):
    wave, profile, sems = scratch
    return [
        pltpu.make_async_copy(given[2 * k + run], ref.at[run], sems.at[2 * k + run])
        for k, ref in enumerate((wave, profile))
        for run in range(2)
    ]


def source_of(run, turn, given, scratch):
    if scratch:
        wave, profile = scratch[0][run], scratch[1][run]
    else:
        wave, profile = (jnp.where(run == 0, given[k][...], given[k + 1][...]) for k in (0, 2))
    row = wave[:, turn : turn + 1] * profile
    plane = jnp.where(run == 0, *(given[k][...].reshape(1, 1) for k in (4, 5)))
    at = lax.broadcasted_iota(jnp.int32, PLANE, 0)
    return jnp.where(at == plane, row, 0.0)


def kernel_call(body, out_shape, in_specs, out_specs, scratch, name, micros=1, grant=GRANT, **more):
    return pl.pallas_call(
        body,
        out_shape=out_shape,
        in_specs=in_specs,
        out_specs=out_specs,
        scratch_shapes=scratch,
        compiler_params=pltpu.CompilerParams(vmem_limit_bytes=grant),
        cost_estimate=pl.CostEstimate(
            flops=micros * 10**9, bytes_accessed=0, transcendentals=0
        ),
        name=name,
        **more,
    )


def shaped(*shape):
    return jax.ShapeDtypeStruct(shape, jnp.float32)


def start_all(copies):
    for copy in copies:
        copy.start()


def wait_all(copies):
    for copy in copies:
        copy.wait()


def plane_at(index):
    return pl.ds(pl.multiple_of(index * NZ, 8), NZ)


def first_planes(
    fwd, adj, inverse, density, mask, to_prior, to_next, rows_in, inv, cells, chosen, sems
):
    rows = inverse.shape[0]
    width = density.shape[1]
    copies = [
        pltpu.make_async_copy(fwd.at[0, :, rows - 1], rows_in.at[0], sems.at[0]),
        pltpu.make_async_copy(adj.at[0, :, rows - 1], rows_in.at[1], sems.at[1]),
        pltpu.make_async_copy(density, cells, sems.at[2]),
        pltpu.make_async_copy(mask, chosen, sems.at[3]),
        pltpu.make_async_copy(inverse.at[0], inv.at[0], sems.at[4]),
        pltpu.make_async_copy(inverse.at[rows - 1], inv.at[1], sems.at[5]),
    ]
    for run, fields in enumerate((fwd, adj)):
        for k in range(2):
            at = 2 * run + k
            copies.append(
                pltpu.make_async_copy(
                    fields.at[0, 1 + k, 0], to_prior.at[plane_at(at)], sems.at[6 + at]
                )
            )
    start_all(copies)
    wait_all(copies[2:6])
    at = lax.broadcasted_iota(jnp.int32, (1, width), 1) // (width // mask.shape[1])
    spread = jnp.zeros((1, width), jnp.float32)
    for k in range(mask.shape[1]):
        spread = jnp.where(at == k, chosen[:, k : k + 1].astype(jnp.float32), spread)
    rest = pl.ds(4 * NZ, to_next.shape[0] - 4 * NZ)
    group = lax.axis_index("freq")
    for side, (sent, first) in enumerate(((to_prior, 0), (to_next, density.shape[0] - RMAX))):
        part = inv[side, :PART, :]
        for k in range(1, FREQS):
            part = jnp.where(group == k, inv[side, k * PART : (k + 1) * PART, :], part)
        sent[rest, :] = jnp.zeros((to_next.shape[0] - 4 * NZ, NY), jnp.float32)
        sent[pl.ds(4 * NZ, PART), :] = part
        for k in range(RMAX):
            sent[slot_at(k, width)] = cells[pl.ds(first + k, 1), :]
        sent[slot_at(RMAX, width)] = spread
    for run in range(2):
        copies[run].wait()
        planes = [rows_in[run, k] for k in range(6)]
        magn = magnetic_yz(planes[4:], planes[:3], None)
        for k in range(2):
            to_next[plane_at(2 * run + k), :] = magn[k]
    wait_all(copies[6:])


def second_planes(fwd, adj, inverse, *rest):
    given, (_, to_prior, to_next, own, head, tail, inv, sems, *scratch) = rest[:6], rest[6:]
    rows = inverse.shape[0]
    small = source_copies(given, scratch) + [
        pltpu.make_async_copy(inverse.at[0], inv.at[0], sems.at[4]),
        pltpu.make_async_copy(inverse.at[rows - 1], inv.at[1], sems.at[5]),
    ]

    def ends(fields, run):
        return [
            pltpu.make_async_copy(fields.at[0, :, pl.ds(0, 2)], head.at[run], sems.at[2 * run]),
            pltpu.make_async_copy(
                fields.at[0, :, pl.ds(rows - 2, 2)], tail.at[run], sems.at[2 * run + 1]
            ),
        ]

    start_all(ends(fwd, 0) + small + ends(adj, 1))
    wait_all(small)

    def one_run(run, carry):
        wait_all(ends(fwd, run))

        def row(ref, x):
            return tuple(
                tuple(ref[run, k, x] for k in range(first, first + 3)) for first in (0, 3)
            )

        source = source_of(run, 0, given, scratch)
        elec, magn = row(head, 0)
        magn = magnetic(magn, elec, (head[run, 1, 1], head[run, 2, 1]))
        elec = electric(elec, magn, None, courant * inv[0], source)
        for k in range(2):
            to_prior[plane_at(2 * run + k), :] = elec[1 + k]
        for k in range(3):
            own[run, k] = elec[k]
        (elec_6, magn_6), (elec, magn) = row(tail, 0), row(tail, 1)
        yz_6 = magnetic_yz(magn_6[1:], elec_6, elec[1:])
        magn = magnetic(magn, elec, None)
        elec = electric(elec, magn, yz_6, courant * inv[1], source)
        magn = magnetic(magn, elec, None)
        for k in range(2):
            to_next[plane_at(2 * run + k), :] = magn[1 + k]
        for k in range(3):
            own[run, 3 + k] = elec[k]
            own[run, 6 + k] = magn[k]
        return carry

    lax.fori_loop(0, 2, one_run, 0)


class State:
    def __init__(self, given, home, written):
        self.given, self.home = given, home
        self.written = None if given is None else set(written)

    def load(self, run, first, x, count=3):
        parts = []
        for k in range(first, first + count):
            at_home = self.written is None or (k, x) in self.written
            ref, at = (self.home if at_home else self.given)(k, x)
            parts.append(ref[run, k, at])
        return tuple(parts)

    def store(self, run, first, x, planes):
        for k, value in enumerate(planes):
            ref, at = self.home(first + k, x)
            ref[run, first + k, at] = value
            if self.written is not None:
                self.written.add((first + k, x))

    def magnetic(self, run, x, following):
        magn = magnetic(self.load(run, 3, x), self.load(run, 0, x), following)
        self.store(run, 3, x, magn)
        return magn

    def electric(self, run, x, prior, scaled, source):
        elec = electric(self.load(run, 0, x), self.load(run, 3, x), prior, scaled, source)
        self.store(run, 0, x, elec)

    def electric_yz(self, run, x):
        return self.load(run, 1, x, 2)

    def magnetic_yz(self, run, x):
        return self.load(run, 4, x, 2)


def in_place(ref):
    return State(None, lambda k, x: (ref, x), ())


def products(ref, x):
    total = ref[0, 0, x] * ref[1, 0, x]
    for k in (1, 2):
        total = total + ref[0, k, x] * ref[1, k, x]
    return jnp.sum(total.reshape(NZ // 8, 8, NY), axis=0)


def interior(fwd, adj, inverse, *rest):
    given, (_, state, share, inv, sems, *scratch) = rest[:6], rest[6:]
    rows = inverse.shape[0]
    last = rows - 1
    into = source_copies(given, scratch) + [pltpu.make_async_copy(inverse, inv, sems.at[4])]

    def load(fields, run):
        return pltpu.make_async_copy(fields.at[0], state.at[run], sems.at[run])

    start_all([load(fwd, 0)] + into + [load(adj, 1)])
    wait_all(into)
    rows_of = in_place(state)

    for turn in range(STEPS):

        def one_run(run, carry, turn=turn):
            if turn == 0:
                load(fwd, run).wait()
            source = source_of(run, turn, given, scratch)
            for x in range(turn, last - turn):
                rows_of.magnetic(run, x, rows_of.electric_yz(run, x + 1))
                if x > turn:
                    rows_of.electric(
                        run, x, rows_of.magnetic_yz(run, x - 1), courant * inv[x], source
                    )
            return carry

        lax.fori_loop(0, 2, one_run, 0)
        for x in range(turn + 1, last - turn):
            share[x] = products(state, x) + (share[x] if turn > 0 else 0.0)
    for x in (0, last):
        share[x] = jnp.zeros(share.shape[1:], jnp.float32)


def flags():
    slab = lax.axis_index("slab")
    has_prior = (slab > 0).astype(jnp.float32)
    has_next = (slab < lax.axis_size("slab") - 1).astype(jnp.float32)
    return has_prior, has_next


def write_copies(parts, fields, sems, runs=(0, 1)):
    return [
        pltpu.make_async_copy(
            ref.at[run, *(pl.ds(at, n) for at, n in zip(source, count))],
            fields[run].at[0, *(pl.ds(at, n) for at, n in zip(target, count))],
            sems.at[len(parts) * run + part],
        )
        for run in runs
        for part, (ref, source, count, target) in enumerate(parts)
    ]


def respond(before, early, parts, resp, scaled):
    for side, flag in enumerate(flags()):
        for k in range(FREQS):
            part = parts[k, pl.ds(side * PART, PART), :]
            scaled[side, pl.ds(k * PART, PART), :] = courant * flag * part
    flagged = courant * flags()[0]

    def one_run(run, carry):
        magn_y, magn_z = flagged * before[run, 2, 0], -flagged * before[run, 1, 0]
        resp[run, 0] = scaled[0] * (dy_b(magn_z) - dz_b(magn_y))
        resp[run, 1] = -scaled[0] * magn_z
        resp[run, 2] = scaled[0] * magn_y
        resp[run, 3] = jnp.zeros(PLANE, jnp.float32)
        resp[run, 4] = magn_y
        resp[run, 5] = magn_z
        resp[run, 6] = scaled[1] * early[run, 5, 1]
        resp[run, 7] = -scaled[1] * early[run, 4, 1]
        return carry

    lax.fori_loop(0, 2, one_run, 0)


def border_rows(run, turn, state, source, inv, here, resp_in=None, resp_out=None, scaled=None):
    has_prior, has_next = flags()
    flagged = courant * has_prior
    last = inv.shape[0] - 1
    whole = here is not None

    def received(ref):
        return tuple(ref[plane_at(2 * run + k), :] for k in range(2))

    own_y, own_z = state.electric_yz(run, 0)
    if turn == 0:
        magn_r = (None, flagged * own_z, -flagged * own_y)
    else:
        elec_r = tuple(resp_in[run, k] for k in range(3))
        old = tuple(resp_in[run, k] for k in range(3, 6))
        magn_r = (
            old[0] - courant * (dy_f(elec_r[2]) - dz_f(elec_r[1])),
            old[1] - courant * (dz_f(elec_r[0]) + elec_r[2]) + flagged * own_z,
            old[2] + courant * (elec_r[1] + dy_f(elec_r[0])) - flagged * own_y,
        )
        if whole:
            resp_out[run, 0] = elec_r[0] + scaled[0] * (dy_b(magn_r[2]) - dz_b(magn_r[1]))
            resp_out[run, 1] = elec_r[1] + scaled[0] * (
                dz_b(magn_r[0]) - (magn_r[2] + courant * elec_r[1])
            )
            resp_out[run, 2] = elec_r[2] + scaled[0] * (
                (magn_r[1] - courant * elec_r[2]) - dy_b(magn_r[0])
            )
            resp_out[run, 3] = magn_r[0]
        resp_out[run, 4] = magn_r[1]
        resp_out[run, 5] = magn_r[2]
    for x in range(turn):
        state.magnetic(run, x, state.electric_yz(run, x + 1))
    if whole:
        arrived = received(here[0])
        prior = tuple(has_prior * arrived[k] + magn_r[1 + k] for k in range(2))
        state.electric(run, 0, prior, courant * inv[0], source)
    else:
        elec_x = electric_x(state.load(run, 0, 0, 1)[0], state.load(run, 3, 0), courant * inv[0])
        state.store(run, 0, 0, (elec_x + source,))
    for x in range(1, turn + 1):
        state.electric(run, x, state.magnetic_yz(run, x - 1), courant * inv[x], source)
    for x in range(last - turn, last):
        state.magnetic(run, x, state.electric_yz(run, x + 1))
    if whole:
        arrived = received(here[1])
        following = tuple(has_next * plane for plane in arrived)
        if turn > 0:
            following = tuple(following[k] + resp_in[run, 6 + k] for k in range(2))
        magn = state.magnetic(run, last, following)
    else:
        magn_x = magnetic_x(state.load(run, 3, last, 1)[0], state.load(run, 0, last))
        state.store(run, 3, last, (magn_x,))
    for x in range(last - turn, last + (1 if whole else 0)):
        state.electric(run, x, state.magnetic_yz(run, x - 1), courant * inv[x], source)
    if turn > 0 and whole:
        elec_y, elec_z = resp_in[run, 6], resp_in[run, 7]
        magn_x = -courant * (dy_f(elec_z) - dz_f(elec_y))
        resp_out[run, 6] = elec_y + scaled[1] * (dz_b(magn_x) - (courant * elec_y - magn[2]))
        resp_out[run, 7] = elec_z + scaled[1] * ((-courant * elec_z - magn[1]) - dy_b(magn_x))
    elif turn > 0:
        resp_out[run, 6] = resp_in[run, 6]
        resp_out[run, 7] = resp_in[run, 7]


def third_planes(inv, *rest):
    given, (before, own, to_prior, to_next) = rest[:6], rest[6:]
    last = inv.shape[0] - 1

    def one_run(run, carry):
        state = State(lambda k, x: (before, x), None, ())
        elec = tuple(own[run, k] for k in range(3))
        magn = magnetic(state.load(run, 3, 0), elec, state.electric_yz(run, 1))
        sent = electric_yz(elec[1:], magn, None, courant * inv[0])
        for k in range(2):
            to_prior[plane_at(2 * run + k), :] = sent[k]
        elec = tuple(own[run, 3 + k] for k in range(3))
        magn = tuple(own[run, 6 + k] for k in range(3))
        yz = magnetic_yz(
            state.magnetic_yz(run, last - 1), state.load(run, 0, last - 1), elec[1:]
        )
        elec = electric(elec, magn, yz, courant * inv[last], source_of(run, 1, given, ()))
        sent = magnetic_yz(magn[1:], elec, None)
        for k in range(2):
            to_next[plane_at(2 * run + k), :] = sent[k]
        return carry

    lax.fori_loop(0, 2, one_run, 0)


def step_one(inv, *rest):
    given, (before, next_a, prior_a, early, parts, share) = rest[:6], rest[6:]
    parts[...] = jnp.zeros_like(parts)
    for side, ref in enumerate((prior_a, next_a)):
        parts[pl.ds(side * PART, PART), :] = ref[pl.ds(4 * NZ, PART), :]

    def one_run(run, carry):
        state = State(lambda k, x: (before, x), lambda k, x: (early, min(x, 1)), ())
        border_rows(run, 0, state, source_of(run, 0, given, ()), inv, (prior_a, next_a))
        return carry

    lax.fori_loop(0, 2, one_run, 0)
    for side in range(2):
        share[side] = products(early, side)


def borders(inv, *rest):
    given, (before, early, resp_in, scaled, share, ends, next_b, prior_b) = rest[:6], rest[6:14]
    kept, summed, waiting, fwd_out, adj_out, inner, resp, total, inside_sems, sems = rest[14:]
    rows = inv.shape[0]
    last = rows - 1
    inside = rows - 2 * STEPS
    out = write_copies(
        (
            (before, (0, STEPS), (3, inside), (0, STEPS)),
            (before, (3, STEPS - 1), (3, inside + 1), (3, STEPS - 1)),
        ),
        (fwd_out, adj_out),
        inside_sems,
    )
    start_all(out)
    rows_done = (
        (inner, (0, 0), (6, 1), (0, 1)),
        (inner, (0, 1), (3, 1), (0, 2)),
        (inner, (0, 2), (6, 1), (0, last - 2)),
        (kept, (0, 1), (6, 1), (0, last - 1)),
        (kept, (0, 0), (1, 1), (0, 0)),
        (kept, (3, 0), (3, 1), (3, 0)),
        (kept, (3, 2), (1, 1), (3, last)),
    )
    homes = {0: (kept, 0), last - 1: (kept, 1), last: (kept, 2)}
    homes |= {1: (inner, 0), 2: (inner, 1), last - 2: (inner, 2)}

    def handed_in(k, x):
        if x == last or (x == 0 and k < 3):
            return (early, min(x, 1))
        return (before, x)

    written = set()
    for turn in range(1, STEPS):
        whole = turn < STEPS - 1
        seen = []

        def one_run(run, carry, turn=turn, whole=whole, seen=seen):
            state = State(handed_in, lambda k, x: homes[x], written)
            border_rows(
                run, turn, state, source_of(run, turn, given, ()), inv,
                (prior_b, next_b) if whole else None,
                resp_in if turn == 1 else resp, resp if whole else waiting, scaled,
            )
            seen[:] = [state.written]
            return carry

        if whole:
            lax.fori_loop(0, 2, one_run, 0)
        else:
            for run in range(2):
                one_run(run, 0)
                mine = write_copies(rows_done, (fwd_out, adj_out), sems, (run,))
                start_all(mine)
                out = out + mine
        written = seen[0]
        reached = list(range(turn + 1)) + list(range(last - turn, last + 1))
        for x in reached if whole else reached[1:-1]:
            if turn > 1 and min(x, last - x) < turn:
                so_far = total[x]
            else:
                so_far = ends[min(x, 1)] if x in (0, last) else share[x]
            total[x] = so_far + products(*homes[x])
    for x in range(STEPS, rows - STEPS):
        total[x] = share[x]
    summed[...] = jnp.sum(total[...], axis=1)
    wait_all(out)


def last_planes(inv, *rest):
    given, (kept, summed, waiting, prior_c, next_c, blocks, ends, built, sems) = (
        rest[:6], rest[6:]
    )
    last = inv.shape[0] - 1
    has_prior, has_next = flags()

    def one_run(run, carry):
        def row(first, slot, count):
            return tuple(kept[run, first + k, slot] for k in range(count))

        def arrived(ref, flag, first):
            return tuple(
                flag * ref[plane_at(2 * run + k), :] + waiting[run, first + k] for k in range(2)
            )

        elec = electric_yz(
            row(1, 0, 2), row(3, 0, 3), arrived(prior_c, has_prior, 4), courant * inv[0]
        )
        for k in range(2):
            ends[run, k, 0] = elec[k]
        elec = row(0, 2, 3)
        yz = magnetic_yz(row(4, 2, 2), elec, arrived(next_c, has_next, 6))
        source = source_of(run, STEPS - 1, given, ())
        elec = electric(elec, row(3, 2, 1) + yz, row(4, 1, 2), courant * inv[last], source)
        for k in range(3):
            ends[run, 2 + k, 0] = elec[k]
        for k in range(2):
            ends[run, 5 + k, 0] = yz[k]
        return carry

    lax.fori_loop(0, 2, one_run, 0)

    def row_sum(pairs):
        total = pairs[0][0] * pairs[0][1]
        for first, second in pairs[1:]:
            total = total + first * second
        return jnp.sum(total, axis=0, keepdims=True)

    head = row_sum(
        [(kept[0, 0, 0], kept[1, 0, 0])] + [(ends[0, k, 0], ends[1, k, 0]) for k in range(2)]
    )
    tail = row_sum([(ends[0, 2 + k, 0], ends[1, 2 + k, 0]) for k in range(3)])
    at = lax.broadcasted_iota(jnp.int32, summed.shape, 0)
    full = summed[...] + jnp.where(at == 0, head, 0.0) + jnp.where(at == last, tail, 0.0)
    slabs, width = blocks.shape[1], blocks.shape[3]
    for k in range(slabs):
        turned = pltpu.roll(full, (RMAX - k * (NY // slabs)) % NY, 1)
        built[k] = turned[:, :width]
    out = [
        pltpu.make_async_copy(built, blocks.at[f], sems.at[f]) for f in range(blocks.shape[0])
    ]
    start_all(out)
    wait_all(out)


def write_ends(fwd, adj, ends, fwd_out, adj_out, sems):
    last = fwd.shape[2] - 1
    out = write_copies(
        (
            (ends, (0, 0), (2, 1), (1, 0)),
            (ends, (2, 0), (3, 1), (0, last)),
            (ends, (5, 0), (2, 1), (4, last)),
        ),
        (fwd_out, adj_out),
        sems,
    )
    start_all(out)
    wait_all(out)


def moved(rows, by):
    if by == 0:
        return rows
    count = rows.shape[0]
    at = lax.broadcasted_iota(jnp.int32, rows.shape, 0)
    keep = at < count - by if by > 0 else at >= -by
    return jnp.where(keep, pltpu.roll(rows, (-by) % count, 0), 0.0)


def rings(cells):
    tile = cells.shape[1] - 2 * RMAX
    columns = [cells[:, RMAX : RMAX + tile]]
    for a in range(1, RMAX + 1):
        columns.append(
            cells[:, RMAX - a : RMAX - a + tile] + cells[:, RMAX + a : RMAX + a + tile]
        )
    sums = {}
    for a in range(RMAX + 1):
        for b in range(RMAX + 1):
            part = columns[a]
            if b > 0:
                part = moved(part, b) + moved(part, -b)
            square = a * a + b * b
            sums[square] = sums[square] + part if square in sums else part
    return sums.items()


RINGS = len({a * a + b * b for a in range(RMAX + 1) for b in range(RMAX + 1)})


def by_tile(values, count):
    columns = count // values.shape[1]
    at = lax.broadcasted_iota(jnp.int32, (count, 1), 0) // columns
    spread = jnp.zeros((count, 1), jnp.float32)
    for k in range(values.shape[1]):
        spread = jnp.where(at == k, values[:, k : k + 1].astype(jnp.float32), spread)
    return spread


def filter_operands(
    prior_a, next_a, density, mask, radius_map, padded, chosen, weights, rows_of, marks_of
):
    tile_rows, width = density.shape
    reach = padded.shape[1]
    for side, (ref, first) in enumerate(((prior_a, 0), (next_a, RMAX + tile_rows))):
        for k in range(RMAX):
            rows_of[pl.ds(first + k, 1), :] = ref[slot_at(k, width)]
    rows_of[pl.ds(RMAX, tile_rows), :] = density[...]
    marks_of[...] = jnp.zeros_like(marks_of)
    for side, ref in enumerate((prior_a, next_a)):
        marks_of[pl.ds(side, 1), :] = ref[slot_at(RMAX, width)]
    sides = marks_of[...].T
    first = lax.axis_index("slab") * tile_rows - RMAX
    at = lax.broadcasted_iota(jnp.int32, (width, reach), 1)
    inside = (at + first >= 0) & (at + first < NY)
    padded[...] = jnp.where(inside, rows_of[...].T, 0.0)
    mark = jnp.where(
        at < RMAX,
        sides[:, 0:1],
        jnp.where(at < RMAX + tile_rows, by_tile(mask, width), sides[:, 1:2]),
    )
    scale = step_size / math.sqrt(3 * STEPS * NZ * FREQS)
    chosen[...] = jnp.where(inside, scale * mark, 0.0)
    radius = by_tile(radius_map, width)
    total = jnp.zeros((width, tile_rows), jnp.float32)
    for k, (square, part) in enumerate(rings(inside.astype(jnp.float32))):
        weight = jnp.maximum(radius - math.sqrt(square), 0.0)
        weights[k] = jnp.broadcast_to(weight, total.shape)
        total = total + weight * part
    total = 1.0 / total
    for k in range(RINGS):
        weights[k] = weights[k] * total


def project(blocks, padded, chosen, weights, projected):
    freqs, slabs, rows, width = blocks.shape
    gradient = jnp.sum(blocks[...], axis=0).reshape(slabs * rows, width)
    updated = padded[...] + chosen[...] * gradient
    filtered = jnp.zeros(weights.shape[1:], jnp.float32)
    for k, (_, part) in enumerate(rings(updated)):
        filtered = filtered + weights[k] * part
    base = math.tanh(sharpness * midpoint)
    value = (base + jnp.tanh(sharpness * (filtered - midpoint))) / (
        base + math.tanh(sharpness * (1.0 - midpoint))
    )
    projected[...] = value.T


def around(shard, axis, by):
    count = lax.axis_size(axis)
    return lax.ppermute(shard, axis, [(i, (i + by) % count) for i in range(count)])


def on_device(
    inverse_permittivity,
    forward_fields,
    adjoint_fields,
    source_wave,
    source_profile,
    adjoint_wave,
    adjoint_profile,
    source_plane,
    monitor_plane,
    radius_map,
    design_mask,
    design_density,
):
    rows = forward_fields.shape[2]
    freqs, slabs = lax.axis_size("freq"), lax.axis_size("slab")
    tile_rows, width = design_density.shape
    reach = tile_rows + 2 * RMAX
    waves = (source_wave, adjoint_wave, source_profile, adjoint_profile)
    planes = (source_plane, monitor_plane)

    def pinned(arrays):
        return tuple(pltpu.with_memory_space_constraint(array, pltpu.HBM) for array in arrays)

    fields = pinned((forward_fields, adjoint_fields, inverse_permittivity))
    sources = pinned(waves) + planes
    dma = pltpu.SemaphoreType.DMA
    field_shape = shaped(*forward_fields.shape)
    state_shape = shaped(2, 6, rows, *PLANE)
    four = shaped(4 * NZ, NY)

    def vmem(*shape, kind=jnp.float32):
        return pltpu.VMEM(shape, kind)

    to_prior, to_next = kernel_call(
        first_planes,
        (shaped(sent_rows(width), NY),) * 2,
        [HBM] * 5,
        (VMEM, VMEM),
        [
            vmem(2, 6, *PLANE),
            vmem(2, *PLANE),
            vmem(tile_rows, width),
            vmem(*design_mask.shape, kind=jnp.int32),
            dma((10,)),
        ],
        "first_planes",
    )(*fields, *pinned((design_density, design_mask)))
    prior_a = around(to_next, "slab", 1)
    next_a = around(to_prior, "slab", -1)
    to_prior, to_next, own = kernel_call(
        second_planes,
        (four, four, shaped(2, 9, *PLANE)),
        [HBM] * 3 + SOURCE_SPECS + [ANY],
        (VMEM,) * 3,
        [
            vmem(2, 6, 2, *PLANE),
            vmem(2, 6, 2, *PLANE),
            vmem(2, *PLANE),
            dma((6,)),
            *SOURCE_SCRATCH,
        ],
        "second_planes",
        micros=2,
    )(*fields, *sources, to_prior)
    prior_b = around(to_next, "slab", 1)
    next_b = around(to_prior, "slab", -1)
    state, share = kernel_call(
        interior,
        (state_shape, shaped(rows, 8, NY)),
        [HBM] * 3 + SOURCE_SPECS + [ANY],
        (VMEM, VMEM),
        [vmem(rows, *PLANE), dma((5,)), *SOURCE_SCRATCH],
        "interior",
        micros=8,
    )(*fields, *sources, own)
    to_prior, to_next = kernel_call(
        third_planes,
        (four, four),
        [VMEM] + SOURCE_VALUES + [VMEM] * 2,
        (VMEM,) * 2,
        [],
        "third_planes",
    )(inverse_permittivity, *waves, *planes, state, own)
    prior_c = around(to_next, "slab", 1)
    next_c = around(to_prior, "slab", -1)
    early, parts, ends = kernel_call(
        step_one,
        (shaped(2, 6, 2, *PLANE), shaped(-(-2 * PART // 8) * 8, NY), shaped(2, 8, NY)),
        [VMEM] + SOURCE_VALUES + [VMEM] * 3,
        (VMEM,) * 3,
        [],
        "step_one",
        micros=0,
    )(inverse_permittivity, *waves, *planes, state, next_a, prior_a)
    parts = lax.all_gather(parts, "freq")
    resp, scaled = kernel_call(
        respond,
        (shaped(2, 8, *PLANE), shaped(2, *PLANE)),
        [VMEM] * 3,
        (VMEM,) * 2,
        [],
        "respond",
        micros=0,
    )(state, early, parts)
    padded, chosen, weights = kernel_call(
        filter_operands,
        (shaped(width, reach), shaped(width, reach), shaped(RINGS, width, tile_rows)),
        [VMEM] * 5,
        (VMEM,) * 3,
        [vmem(reach, width), vmem(8, width)],
        "filter_operands",
        micros=0,
    )(prior_a, next_a, design_density, design_mask, radius_map)
    three = shaped(2, 6, 3, *PLANE)
    kept, summed, waiting, forward_part, adjoint_part = kernel_call(
        borders,
        (three, shaped(rows, NY), shaped(2, 8, *PLANE), field_shape, field_shape),
        [VMEM] + SOURCE_VALUES + [VMEM] * 8,
        (VMEM,) * 3 + (HBM,) * 2,
        [
            vmem(2, 6, 3, *PLANE),
            vmem(2, 8, *PLANE),
            vmem(rows, 8, NY),
            dma((4,)),
            dma((14,)),
        ],
        "borders",
        micros=0,
        grant=2 * GRANT,
    )(
        inverse_permittivity, *waves, *planes, state, early, resp, scaled, share, ends,
        next_b, prior_b,
    )
    blocks, ends = kernel_call(
        last_planes,
        (shaped(freqs, slabs, rows, reach), shaped(2, 7, 1, *PLANE)),
        [VMEM] + SOURCE_VALUES + [VMEM] * 5,
        (HBM, VMEM),
        [vmem(slabs, rows, reach), dma((freqs,))],
        "last_planes",
    )(inverse_permittivity, *waves, *planes, kept, summed, waiting, prior_c, next_c)
    forward_out, adjoint_out = kernel_call(
        write_ends,
        (field_shape, field_shape),
        [HBM] * 2 + [VMEM],
        (HBM, HBM),
        [dma((6,))],
        "write_ends",
        input_output_aliases={0: 0, 1: 1},
    )(forward_part, adjoint_part, ends)

    blocks = blocks.reshape(freqs * slabs, rows, reach)
    blocks = lax.all_to_all(blocks, ("freq", "slab"), 0, 0, tiled=True)
    blocks = blocks.reshape(freqs, slabs, rows, reach)
    projected = kernel_call(
        project,
        shaped(tile_rows, width),
        [VMEM] * 4,
        VMEM,
        [],
        "project",
    )(blocks, padded, chosen, weights)
    return (forward_out, adjoint_out, projected)


def solution(mesh):
    return jax.shard_map(
        on_device,
        mesh=mesh,
        in_specs=(
            P("slab", None, None),
            P("freq", None, "slab", None, None),
            P("freq", None, "slab", None, None),
            P("freq", None),
            P("freq", None),
            P("freq", None),
            P("freq", None),
            P("freq"),
            P("freq"),
            P("slab", None),
            P("slab", None),
            P("slab", None),
        ),
        out_specs=(
            P("freq", None, "slab", None, None),
            P("freq", None, "slab", None, None),
            P("slab", None),
        ),
        check_vma=False,
    )
```
